32 devices in a mesh: group: 2 (over x), lat: 16 (over z, y, core).
Axes of the slice: x: 2, y: 2, z: 4, core: 2. Of those that a mesh axis runs over, the one named last changes fastest.
Arguments:
- features: bfloat16 [96, 1440, 256], P(('group', 'lat')), parts along dimension 0, may hold values from -6 to 6
- disco_rows: int32 [48, 9], P('lat'), may hold values from 0 to 47, as said below
- disco_cols: int32 [48, 9], P('lat'), may hold values from -16 to 16
- disco_basis: bfloat16 [3, 48, 9], P(None, 'lat'), may hold values from -1 to 1
- disco_weight: bfloat16 [3, 256, 256], replicated, may hold values from -0.21875 to 0.21875
- spectral_gain: float32 [48, 256], replicated, may hold values from 0.5 to 2
- grad_output: bfloat16 [96, 1440, 256], P(('group', 'lat')), parts along dimension 0, may hold values from -6 to 6
Outputs:
- output: bfloat16 [96, 1440, 256], P(('group', 'lat')), parts along dimension 0
- grad_features: bfloat16 [96, 1440, 256], P(('group', 'lat')), parts along dimension 0
- grad_weight: float32 [6, 256, 256], P('group'), parts along dimension 0
- grad_gain: float32 [96, 256], P('group'), parts along dimension 0
The draws below stay inside these ranges and needn't reach their ends.
There are 2 independent parts, one for each index of `group`. The reference program is written for one: setup_inputs(seed, part) draws one part's arguments, and reference() takes and returns one part's arrays. A program takes and returns all parts, laid end to end along the dimension named above; an argument that names none is the same for every part. Nothing has to cross between parts.
Inputs may be any that keep to these rules, and one draw needn't show every extreme that they name: disco_rows[i, t] lies within 1 row of row i.
All inputs are finite; a program needn't handle non-finite values.
Results may differ from the reference program's by a relative error of at most 0.0083.
Values may be sent and summed in bfloat16 or wider, within the bound.
No kernel may reach another device: no remote copies, remote signals or barrier semaphores. Data moves between devices by JAX's collectives and lax.ppermute only.
A program may use at most 192 MiB of HBM per device.

```python
import math
import jax
import jax.numpy as jnp
import numpy as np
from jax import lax

C = 256
NLON = 1440
K = 3
TAPS = 9
HALO = 1
MAXSPAN = 16
NLAT = 48
M = 48
L = 48


def draw_disco_rows(key, part):
    key = jax.random.fold_in(key, 11)
    row_ids = lax.broadcasted_iota(jnp.int32, (NLAT, TAPS), 0)
    tap_ids = lax.broadcasted_iota(jnp.int32, (NLAT, TAPS), 1)
    offsets = jax.random.randint(key, (NLAT, TAPS), -HALO, HALO + 1, dtype=jnp.int32)
    offsets = jnp.where(tap_ids == 0, 0, jnp.where(tap_ids == 1, -HALO, jnp.where(tap_ids == 2, HALO, offsets)))
    return jnp.clip(row_ids + offsets, 0, NLAT - 1).astype(jnp.int32)


def draw_disco_cols(key, part):
    key = jax.random.fold_in(key, 12)
    row_ids = lax.broadcasted_iota(jnp.int32, (NLAT, TAPS), 0)
    tap_ids = lax.broadcasted_iota(jnp.int32, (NLAT, TAPS), 1)
    pole_gap = jnp.minimum(row_ids, NLAT - 1 - row_ids)
    spans = jnp.maximum(2, 2 * MAXSPAN // (pole_gap + 2))
    picked = jax.random.randint(key, (NLAT, TAPS), -spans, spans + 1, dtype=jnp.int32)
    picked = jnp.where(tap_ids == 0, 0, jnp.where(tap_ids == 1, -spans, jnp.where(tap_ids == 2, spans, picked)))
    return picked.astype(jnp.int32)


def level_of(rng, dims, split, smallest, largest):
    gain = 1.0
    for dim, blocks in split:
        draws = jax.random.uniform(jax.random.fold_in(jax.random.fold_in(rng, 6), dim), (blocks,), jnp.float32, smallest / len(split), largest / len(split))
        gain = gain * jnp.repeat(jnp.exp(draws), dims[dim] // blocks).reshape((-1,) + (1,) * (len(dims) - 1 - dim))
    return gain


def noise(key, shape, spread, most, pieces=(), kind=jnp.bfloat16):
    factor_of = level_of(key, shape, pieces, -0.22, 0.18) if pieces else 1.0
    array = jax.random.normal(key, shape, jnp.float32) * spread * factor_of
    return jnp.minimum(jnp.maximum(array, -most), most).astype(kind)


def setup_inputs(seed: int = 0, part: int = 0) -> dict:
    seeds = jax.random.split(jax.random.key(seed), 8)
    own_keys = jax.random.split(jax.random.fold_in(seeds[7], part), 8)
    features = noise(own_keys[0], (NLAT, NLON, C), 1.0, 6.0, ((0, 16),))
    disco_rows = draw_disco_rows(jax.random.fold_in(seeds[7], 71), part)
    disco_cols = draw_disco_cols(jax.random.fold_in(seeds[7], 71), part)
    disco_basis = noise(seeds[3], (K, NLAT, TAPS), 0.35, 1.0, ((1, 16),))
    disco_weight = noise(seeds[4], (K, C, C), (K * C) ** -0.5, 0.21875)
    spectral_gain = jnp.clip(jnp.exp(jax.random.uniform(seeds[5], (L, C), jnp.float32, math.log(0.5), math.log(2.0))), 0.5, 2.0)
    grad_output = noise(own_keys[6], (NLAT, NLON, C), 1.0, 6.0, ((0, 16),))
    return dict(features=features, disco_rows=disco_rows, disco_cols=disco_cols, disco_basis=disco_basis, disco_weight=disco_weight, spectral_gain=spectral_gain, grad_output=grad_output)


def legendre_pair(nodes, lat_count):
    before = nodes * 0.0 + 1.0
    current = nodes * 1.0
    for degree in range(2, lat_count + 1):
        following = ((2.0 * degree - 1.0) * nodes * current - (degree - 1.0) * before) / degree
        before = current
        current = following
    return (before, current)

def gauss_grid(lat_count):
    counter = np.arange(1, lat_count + 1) * 1.0
    nodes = np.cos(np.pi * (counter - 0.25) / (lat_count + 0.5))
    for sweep in range(12):
        before, current = legendre_pair(nodes, lat_count)
        slope = lat_count * (nodes * current - before) / (nodes * nodes - 1.0)
        nodes = nodes - current / slope
    before, current = legendre_pair(nodes, lat_count)
    slope = lat_count * (nodes * current - before) / (nodes * nodes - 1.0)
    weights = 2.0 / ((1.0 - nodes * nodes) * slope * slope)
    return (nodes, weights)

def diagonal_table(order_count, latitude_nodes):
    sine_values = np.sqrt(1.0 - latitude_nodes * latitude_nodes)
    orders = np.arange(order_count)
    positive = np.arange(1, order_count)
    log_steps = np.concatenate([np.zeros(1), 0.5 * np.cumsum(np.log((2.0 * positive + 1.0) / (2.0 * positive)))])
    log_values = 0.5 * np.log(0.5) + log_steps[:, None] + orders[:, None] * np.log(sine_values)[None, :]
    return np.exp(log_values)

def legendre_block(orders, order_count, degrees, lat_count):
    latitude_nodes, weights = gauss_grid(lat_count)
    diagonal_start = jnp.asarray(diagonal_table(order_count, latitude_nodes), jnp.float32)[orders]
    node_row = jnp.asarray(latitude_nodes, jnp.float32)[None, :]
    order_column = orders.astype(jnp.float32)[:, None]

    def block_step(carry, block_index):
        previous, earlier = carry
        produced = []
        for offset in range(16):
            degree = (block_index * 16 + offset).astype(jnp.float32)
            squared = degree * degree
            order_squared = order_column * order_column
            forward_factor = jnp.sqrt(jnp.maximum(4.0 * squared - 1.0, 1.0) / jnp.maximum(squared - order_squared, 1.0))
            lower = (degree - 1.0) * (degree - 1.0)
            back_factor = jnp.sqrt(jnp.maximum(lower - order_squared, 0.0) / jnp.maximum(4.0 * lower - 1.0, 1.0))
            recurred = forward_factor * (node_row * previous - back_factor * earlier)
            fresh = jnp.where(degree < order_column, 0.0, jnp.where(degree == order_column, diagonal_start, recurred))
            earlier = previous
            previous = fresh
            produced.append(fresh)
        return ((previous, earlier), jnp.stack(produced))
    zeros = jnp.zeros((orders.shape[0], lat_count), jnp.float32)
    _, blocks = lax.scan(block_step, (zeros, zeros), jnp.arange(degrees // 16, dtype=jnp.int32))
    legendre = blocks.reshape(degrees, orders.shape[0], lat_count)
    return jnp.transpose(legendre, (1, 0, 2))

def fourier_tables(lon_count, order_count):
    frequency = lax.broadcasted_iota(jnp.int32, (lon_count, order_count), 1)
    column = lax.broadcasted_iota(jnp.int32, (lon_count, order_count), 0)
    phases = 2.0 * math.pi / lon_count * (frequency * column % lon_count).astype(jnp.float32)
    cosine = jnp.cos(phases)
    sine_part = jnp.sin(phases)
    forward_table = (jnp.stack([cosine, -sine_part], axis=2) / lon_count).reshape(lon_count, 2 * order_count).astype(jnp.bfloat16)
    weight_m = jnp.where(frequency == 0, 1.0, 2.0).astype(jnp.float32)
    inverse_table = jnp.stack([weight_m * cosine, -weight_m * sine_part], axis=2).reshape(lon_count, 2 * order_count)
    return (forward_table, jnp.transpose(inverse_table).astype(jnp.bfloat16))

def reference(features, disco_rows, disco_cols, disco_basis, disco_weight, spectral_gain, grad_output):
    forward_table, inverse_table = fourier_tables(NLON, M)
    _, gauss_weights = gauss_grid(NLAT)
    weights = jnp.asarray(gauss_weights, jnp.float32)
    padded = jnp.pad(features, ((HALO, HALO), (0, 0), (0, 0)))
    basis_rows = jnp.transpose(disco_basis, (1, 0, 2))
    local_rows = disco_rows + HALO
    weight_wide = disco_weight.astype(jnp.float32)

    def longitudes(col_shift):
        return (lax.broadcasted_iota(jnp.int32, (col_shift.shape[0], NLON), 1) + col_shift[:, None]) % NLON

    def disco_row(packed):
        row_index, col_shift, basis = packed
        gathered = padded[row_index[:, None], longitudes(col_shift)]
        mixed = jnp.einsum('kt,tjc->kjc', basis.astype(jnp.float32), gathered.astype(jnp.float32)).astype(jnp.bfloat16)
        row_term = jnp.einsum('kjc,kcd->jd', mixed.astype(jnp.float32), weight_wide)
        return (mixed, row_term)
    mixed, disco_term = lax.map(disco_row, (local_rows, disco_cols, basis_rows))
    coefficients = jnp.einsum('ijc,jq->iqc', features.astype(jnp.float32), forward_table.astype(jnp.float32)).astype(jnp.bfloat16)
    block_count = M // 16
    by_block = jnp.transpose(coefficients.reshape(NLAT, block_count, 16, 2 * C), (1, 0, 2, 3))
    gain_pair = jnp.concatenate([spectral_gain, spectral_gain], axis=1)
    block_ids = jnp.arange(block_count, dtype=jnp.int32)

    def tables_for(block_index):
        orders = block_index * 16 + jnp.arange(16, dtype=jnp.int32)
        legendre = legendre_block(orders, M, M, NLAT)
        return (legendre.astype(jnp.bfloat16), (legendre * weights[None, None, :]).astype(jnp.bfloat16))

    def spectral_block(packed):
        block_index, block_coeffs = packed
        plain_half, weighted_half = tables_for(block_index)
        analysed = jnp.einsum('rln,nrq->rlq', weighted_half.astype(jnp.float32), block_coeffs.astype(jnp.float32))
        scaled = (analysed * gain_pair[None]).astype(jnp.bfloat16)
        synthesized = jnp.einsum('rln,rlq->nrq', plain_half.astype(jnp.float32), scaled.astype(jnp.float32)).astype(jnp.bfloat16)
        return (analysed, synthesized)
    analysed, synthesized = lax.map(spectral_block, (block_ids, by_block))
    synthesized = jnp.transpose(synthesized, (1, 0, 2, 3)).reshape(NLAT, 2 * M, C)
    spectral_term = jnp.einsum('iqc,qj->ijc', synthesized.astype(jnp.float32), inverse_table.astype(jnp.float32))
    total = disco_term + spectral_term
    output, gelu_pull = jax.vjp(jax.nn.gelu, total)
    grad_total = gelu_pull(grad_output.astype(jnp.float32))[0].astype(jnp.bfloat16)
    grad_synth = jnp.einsum('ijc,qj->iqc', grad_total.astype(jnp.float32), inverse_table.astype(jnp.float32)).astype(jnp.bfloat16)
    grad_blocks = jnp.transpose(grad_synth.reshape(NLAT, block_count, 16, 2 * C), (1, 0, 2, 3))

    def adjoint_block(packed):
        block_index, block_grads, block_analysed = packed
        plain_half, weighted_half = tables_for(block_index)
        grad_scaled = jnp.einsum('rln,nrq->rlq', plain_half.astype(jnp.float32), block_grads.astype(jnp.float32))
        gain_terms = lax.optimization_barrier(jnp.sum(block_analysed * grad_scaled, axis=0))
        grad_analysed = (gain_pair[None] * grad_scaled).astype(jnp.bfloat16)
        grad_coeff = jnp.einsum('rln,rlq->nrq', weighted_half.astype(jnp.float32), grad_analysed.astype(jnp.float32)).astype(jnp.bfloat16)
        return (gain_terms, grad_coeff)
    gain_terms, grad_coeff = lax.map(adjoint_block, (block_ids, grad_blocks, analysed))
    gain_total = lax.optimization_barrier(jnp.sum(gain_terms, axis=0))
    grad_gain = gain_total[:, :C] + gain_total[:, C:]
    grad_coeff = jnp.transpose(grad_coeff, (1, 0, 2, 3)).reshape(NLAT, 2 * M, C)
    grad_spectral = jnp.einsum('iqc,jq->ijc', grad_coeff.astype(jnp.float32), forward_table.astype(jnp.float32))

    def adjoint_row(carry, packed):
        weight_acc, ext_grad = carry
        row_index, col_shift, basis, mixed_row, grad_row = packed
        grad_wide = grad_row.astype(jnp.float32)
        grad_mixed = jnp.einsum('jd,kcd->kjc', grad_wide, weight_wide)
        weight_acc = weight_acc + jnp.einsum('kjc,jd->kcd', mixed_row.astype(jnp.float32), grad_wide)
        tap_grad = jnp.einsum('kt,kjc->tjc', basis.astype(jnp.float32), grad_mixed, precision=lax.Precision.HIGHEST)
        ext_grad = ext_grad.at[row_index[:, None], longitudes(col_shift)].add(tap_grad)
        return ((weight_acc, ext_grad), None)
    start_carry = (jnp.zeros((K, C, C), jnp.float32), jnp.zeros((NLAT + 2 * HALO, NLON, C), jnp.float32))
    (grad_weight, ext_grad), _ = lax.scan(adjoint_row, start_carry, (local_rows, disco_cols, basis_rows, mixed, grad_total))
    grad_features = (grad_spectral + ext_grad[HALO:HALO + NLAT]).astype(jnp.bfloat16)
    return (output.astype(jnp.bfloat16), grad_features, grad_weight, grad_gain)
```

```python
import math

import jax
import jax.numpy as jnp
import numpy as np
from jax import lax
from jax.experimental import pallas as pl
from jax.experimental.pallas import tpu as pltpu
from jax.sharding import PartitionSpec as P

HALO = 1
SPAN = 16
STEP = 48
WIN = STEP + 2 * SPAN
GROUP = 8
NONE = -4096
ROOT = math.sqrt(2.0 / math.pi)
CUBE = 0.044715
F32 = jnp.float32
BF16 = jnp.bfloat16
MIB = 1 << 20
TABLE_CAP = 1 << 22


def legendre_pair(nodes, lat_count):
    before = nodes * 0.0 + 1.0
    current = nodes * 1.0
    for degree in range(2, lat_count + 1):
        following = ((2.0 * degree - 1.0) * nodes * current - (degree - 1.0) * before) / degree
        before = current
        current = following
    return (before, current)


def gauss_grid(lat_count):
    counter = np.arange(1, lat_count + 1) * 1.0
    nodes = np.cos(np.pi * (counter - 0.25) / (lat_count + 0.5))
    for sweep in range(12):
        before, current = legendre_pair(nodes, lat_count)
        slope = lat_count * (nodes * current - before) / (nodes * nodes - 1.0)
        nodes = nodes - current / slope
    before, current = legendre_pair(nodes, lat_count)
    slope = lat_count * (nodes * current - before) / (nodes * nodes - 1.0)
    weights = 2.0 / ((1.0 - nodes * nodes) * slope * slope)
    return (nodes, weights)


def diagonal_table(order_count, latitude_nodes):
    sine_values = np.sqrt(1.0 - latitude_nodes * latitude_nodes)
    orders = np.arange(order_count)
    positive = np.arange(1, order_count)
    log_steps = np.concatenate(
        [np.zeros(1), 0.5 * np.cumsum(np.log((2.0 * positive + 1.0) / (2.0 * positive)))]
    )
    log_values = (
        0.5 * np.log(0.5) + log_steps[:, None] + orders[:, None] * np.log(sine_values)[None, :]
    )
    return np.exp(log_values)


def legendre_block(orders, order_count, degrees, lat_count):
    latitude_nodes, weights = gauss_grid(lat_count)
    diagonal_start = jnp.asarray(diagonal_table(order_count, latitude_nodes), jnp.float32)[orders]
    node_row = jnp.asarray(latitude_nodes, jnp.float32)[None, :]
    order_column = orders.astype(jnp.float32)[:, None]

    def block_step(carry, block_index):
        previous, earlier = carry
        produced = []
        for offset in range(16):
            degree = (block_index * 16 + offset).astype(jnp.float32)
            squared = degree * degree
            order_squared = order_column * order_column
            forward_factor = jnp.sqrt(
                jnp.maximum(4.0 * squared - 1.0, 1.0) / jnp.maximum(squared - order_squared, 1.0)
            )
            lower = (degree - 1.0) * (degree - 1.0)
            back_factor = jnp.sqrt(
                jnp.maximum(lower - order_squared, 0.0) / jnp.maximum(4.0 * lower - 1.0, 1.0)
            )
            recurred = forward_factor * (node_row * previous - back_factor * earlier)
            fresh = jnp.where(
                degree < order_column,
                0.0,
                jnp.where(degree == order_column, diagonal_start, recurred),
            )
            earlier = previous
            previous = fresh
            produced.append(fresh)
        return ((previous, earlier), jnp.stack(produced))

    zeros = jnp.zeros((orders.shape[0], lat_count), jnp.float32)
    _, blocks = lax.scan(block_step, (zeros, zeros), jnp.arange(degrees // 16, dtype=jnp.int32))
    legendre = blocks.reshape(degrees, orders.shape[0], lat_count)
    return jnp.transpose(legendre, (1, 0, 2))


def legendre_table(order_count, degrees, lat_count):
    nodes, weights = gauss_grid(lat_count)
    start = diagonal_table(order_count, nodes).astype(np.float32)
    node_row = nodes.astype(np.float32)[None, :]
    order = np.arange(order_count, dtype=np.float32)[:, None]
    one = np.float32(1.0)
    four = np.float32(4.0)
    previous = np.zeros((order_count, lat_count), np.float32)
    earlier = previous
    produced = []
    for step in range(degrees):
        degree = np.float32(step)
        squared = degree * degree
        lower = (degree - one) * (degree - one)
        ahead = np.sqrt(
            np.maximum(four * squared - one, one) / np.maximum(squared - order * order, one)
        )
        back = np.sqrt(
            np.maximum(lower - order * order, np.float32(0.0))
            / np.maximum(four * lower - one, one)
        )
        recurred = ahead * (node_row * previous - back * earlier)
        fresh = np.where(degree < order, np.float32(0.0), np.where(degree == order, start, recurred))
        earlier = previous
        previous = fresh.astype(np.float32)
        produced.append(previous)
    legendre = np.stack(produced, axis=1)
    weighted = legendre * weights.astype(np.float32)[None, None, :]
    return (legendre.astype(BF16), weighted.astype(BF16))


def fourier_tables(lon_count, order_count, devices):
    angle = 2.0 * np.pi / lon_count * (np.outer(np.arange(lon_count), np.arange(order_count)) % lon_count)
    cosine = np.cos(angle)
    sine = np.sin(angle)
    doubled = np.where(np.arange(order_count) == 0, 1.0, 2.0)[None, :]
    owned = order_count // devices
    group = -(-2 * owned // GROUP) * GROUP

    def grouped(real, imaginary):
        pairs = np.stack([real, imaginary], axis=2).reshape(lon_count, devices, 2 * owned)
        pairs = np.pad(pairs, ((0, 0), (0, 0), (0, group - 2 * owned)))
        return pairs.reshape(lon_count, devices * group).astype(np.float32).astype(BF16)

    forward = grouped(cosine / lon_count, -sine / lon_count)
    inverse = grouped(doubled * cosine, -doubled * sine)
    return (forward, inverse)


def spectral_table(table, devices, lat_dev, group):
    orders, degrees, lats = table.shape
    owned = orders // devices
    split = np.asarray(table, np.float32).reshape(devices, owned, degrees, devices, lat_dev)
    full = np.zeros((devices, owned, 2, degrees, lat_dev, devices, group), np.float32)
    for r in range(owned):
        for p in range(2):
            full[:, r, p, :, :, :, 2 * r + p] = np.transpose(split[:, r], (0, 1, 3, 2))
    return full.reshape(devices, owned * 2 * degrees, lat_dev * devices * group).astype(BF16)


def params(limit, **kwargs):
    return pltpu.CompilerParams(vmem_limit_bytes=limit * MIB, **kwargs)


def cost(flops, nbytes):
    return pl.CostEstimate(flops=int(flops), bytes_accessed=int(nbytes), transcendentals=0)


def dot(a, b):
    return jnp.dot(a, b, preferred_element_type=F32)


def dot_t(a, b):
    return lax.dot_general(a, b, (((0,), (0,)), ((), ())), preferred_element_type=F32)


def transform(features, table):
    lat_dev, lon, channels = features.shape
    rows = table.shape[0]

    def body(x_ref, t_ref, o_ref):
        o_ref[...] = dot(t_ref[...], x_ref[0]).astype(BF16)

    return pl.pallas_call(
        body,
        grid=(lat_dev,),
        in_specs=[
            pl.BlockSpec((1, lon, channels), lambda i: (i, 0, 0)),
            pl.BlockSpec((rows, lon), lambda i: (0, 0)),
        ],
        out_specs=pl.BlockSpec((rows, channels), lambda i: (0, i)),
        out_shape=jax.ShapeDtypeStruct((rows, lat_dev * channels), BF16),
        compiler_params=params(24),
        cost_estimate=cost(2 * rows * lon * channels * lat_dev, features.size * 2),
        name="transform",
    )(features, table)


def filtered(middle, north, south, shifts, taps, weights, keep):
    lat_dev, lon, channels = middle.shape
    kernels = taps.shape[0]
    count = taps.shape[2]
    wide = kernels * channels
    per = 5
    chunk = per * STEP
    rows = lat_dev + 2

    def body(shift_ref, tap_ref, mid_ref, north_ref, south_ref, w_ref, *rest):
        if keep:
            mixed_ref, out_ref, ext, sem = rest
        else:
            out_ref, mixed_ref, ext, sem = rest
        row = pl.program_id(0)

        def copies():
            made = []
            for e in range(rows):
                src = north_ref.at[0] if e == 0 else (south_ref.at[0] if e == rows - 1 else mid_ref.at[e - 1])
                for a, b, n in ((0, SPAN, lon), (lon - SPAN, 0, SPAN), (0, lon + SPAN, SPAN)):
                    made.append(
                        pltpu.make_async_copy(
                            src.at[pl.ds(a, n)], ext.at[e, pl.ds(b, n)], sem.at[len(made)]
                        )
                    )
            return made

        @pl.when(row == 0)
        def _():
            for copy in copies():
                copy.start()

        across = lax.broadcasted_iota(jnp.int32, (STEP, 3 * WIN), 1)
        down = lax.broadcasted_iota(jnp.int32, (STEP, 3 * WIN), 0)
        delta = across - down
        band = [jnp.zeros((STEP, 3 * WIN), F32) for _ in range(kernels)]
        for t in range(count):
            hit = delta == shift_ref[row, t]
            for k in range(kernels):
                band[k] = band[k] + jnp.where(hit, tap_ref[k, row, t], 0.0)
        band = jnp.concatenate(band, axis=0).astype(BF16)

        @pl.when(row == 0)
        def _():
            for copy in copies():
                copy.wait()

        def step(c, carry):
            for b in range(per):
                start = pl.multiple_of(c * chunk + b * STEP, STEP)
                window = jnp.concatenate(
                    [ext[row + e, pl.ds(start, WIN), :] for e in range(3)], axis=0
                )
                sums = dot(band, window).astype(BF16)
                for k in range(kernels):
                    place = (pl.ds(start, STEP), pl.ds(k * channels, channels))
                    if keep:
                        mixed_ref[(0,) + place] = sums[k * STEP : (k + 1) * STEP]
                    else:
                        mixed_ref[pl.ds(b * STEP, STEP), pl.ds(k * channels, channels)] = sums[
                            k * STEP : (k + 1) * STEP
                        ]
            start = pl.multiple_of(c * chunk, chunk)
            if keep:
                block = mixed_ref[0, pl.ds(start, chunk), :]
            else:
                block = mixed_ref[...]
            out_ref[0, pl.ds(start, chunk), :] = dot(block, w_ref[...])
            return carry

        lax.fori_loop(0, lon // chunk, step, 0)

    out_specs = [pl.BlockSpec((1, lon, channels), lambda i: (i, 0, 0))]
    out_shape = [jax.ShapeDtypeStruct((lat_dev, lon, channels), F32)]
    scratch = []
    if keep:
        out_specs.insert(0, pl.BlockSpec((1, lon, wide), lambda i: (i, 0, 0)))
        out_shape.insert(0, jax.ShapeDtypeStruct((lat_dev, lon, wide), BF16))
    else:
        scratch.append(pltpu.VMEM((chunk, wide), BF16))
    result = pl.pallas_call(
        body,
        grid=(lat_dev,),
        in_specs=[
            pl.BlockSpec(memory_space=pltpu.SMEM),
            pl.BlockSpec(memory_space=pltpu.SMEM),
            pl.BlockSpec(memory_space=pl.ANY),
            pl.BlockSpec(memory_space=pl.ANY),
            pl.BlockSpec(memory_space=pl.ANY),
            pl.BlockSpec((wide, channels), lambda i: (0, 0)),
        ],
        out_specs=out_specs,
        out_shape=out_shape,
        scratch_shapes=scratch
        + [pltpu.VMEM((rows, lon + 2 * SPAN, channels), BF16), pltpu.SemaphoreType.DMA((3 * rows,))],
        compiler_params=params(32),
        cost_estimate=cost(
            2 * lat_dev * lon * channels * (3 * wide + 3 * WIN * kernels), middle.size * 10
        ),
        name="filtered",
    )(shifts, taps, middle, north, south, weights)
    return result if keep else result[0]


def spectral_forward(position, owned, table_in, table_out, gain):
    group_rows, width = owned.shape
    _, rows, depth = table_in.shape
    degrees, channels = gain.shape
    lat_dev = width // channels

    def body(p_ref, x_ref, a_ref, b_ref, g_ref, analysed_ref, o_ref):
        analysed = jnp.zeros((rows, channels), F32)
        for i in range(lat_dev):
            analysed = analysed + dot(
                a_ref[0, :, i * group_rows : (i + 1) * group_rows],
                x_ref[:, i * channels : (i + 1) * channels],
            )
        analysed_ref[...] = analysed
        gain_rows = jnp.concatenate([g_ref[...]] * (rows // degrees), axis=0)
        scaled = (analysed * gain_rows).astype(BF16)
        for i in range(lat_dev):
            o_ref[:, i * channels : (i + 1) * channels] = dot_t(
                b_ref[0, :, i * group_rows : (i + 1) * group_rows], scaled
            ).astype(BF16)

    table_spec = pl.BlockSpec((1, rows, depth), lambda g, p: (p[0], 0, 0))
    return pl.pallas_call(
        body,
        grid_spec=pltpu.PrefetchScalarGridSpec(
            num_scalar_prefetch=1,
            grid=(1,),
            in_specs=[
                pl.BlockSpec((group_rows, width), lambda g, p: (0, 0)),
                table_spec,
                table_spec,
                pl.BlockSpec((degrees, channels), lambda g, p: (0, 0)),
            ],
            out_specs=[
                pl.BlockSpec((rows, channels), lambda g, p: (0, 0)),
                pl.BlockSpec((group_rows, width), lambda g, p: (0, 0)),
            ],
        ),
        out_shape=[
            jax.ShapeDtypeStruct((rows, channels), F32),
            jax.ShapeDtypeStruct((group_rows, width), BF16),
        ],
        compiler_params=params(16),
        name="spectral_forward",
    )(position, owned, table_in, table_out, gain)


def spectral_adjoint(position, owned, table_in, table_out, gain, analysed):
    group_rows, width = owned.shape
    _, rows, depth = table_in.shape
    degrees, channels = gain.shape
    lat_dev = width // channels

    def body(p_ref, x_ref, b_ref, a_ref, g_ref, analysed_ref, gain_ref, o_ref):
        scaled = jnp.zeros((rows, channels), F32)
        for i in range(lat_dev):
            scaled = scaled + dot(
                b_ref[0, :, i * group_rows : (i + 1) * group_rows],
                x_ref[:, i * channels : (i + 1) * channels],
            )
        terms = analysed_ref[...] * scaled
        total = jnp.zeros((degrees, channels), F32)
        for s in range(rows // degrees):
            total = total + terms[s * degrees : (s + 1) * degrees]
        gain_ref[...] = total
        gain_rows = jnp.concatenate([g_ref[...]] * (rows // degrees), axis=0)
        grad = (gain_rows * scaled).astype(BF16)
        for i in range(lat_dev):
            o_ref[:, i * channels : (i + 1) * channels] = dot_t(
                a_ref[0, :, i * group_rows : (i + 1) * group_rows], grad
            ).astype(BF16)

    table_spec = pl.BlockSpec((1, rows, depth), lambda g, p: (p[0], 0, 0))
    return pl.pallas_call(
        body,
        grid_spec=pltpu.PrefetchScalarGridSpec(
            num_scalar_prefetch=1,
            grid=(1,),
            in_specs=[
                pl.BlockSpec((group_rows, width), lambda g, p: (0, 0)),
                table_spec,
                table_spec,
                pl.BlockSpec((degrees, channels), lambda g, p: (0, 0)),
                pl.BlockSpec((rows, channels), lambda g, p: (0, 0)),
            ],
            out_specs=[
                pl.BlockSpec((degrees, channels), lambda g, p: (0, 0)),
                pl.BlockSpec((group_rows, width), lambda g, p: (0, 0)),
            ],
        ),
        out_shape=[
            jax.ShapeDtypeStruct((degrees, channels), F32),
            jax.ShapeDtypeStruct((group_rows, width), BF16),
        ],
        compiler_params=params(16),
        name="spectral_adjoint",
    )(position, owned, table_in, table_out, gain, analysed)


def activation(disco, returned, grad_output, inverse, inverse_t):
    lat_dev, lon, channels = disco.shape
    group_rows = returned.shape[0]
    chunk = 240

    def body(d_ref, y_ref, g_ref, inv_ref, invt_ref, o_ref, gt_ref, x_ref):
        def step(c, carry):
            place = pl.ds(pl.multiple_of(c * chunk, chunk), chunk)
            total = d_ref[0, place, :] + dot(inv_ref[place, :], y_ref[...])
            square = total * total
            half = 0.5 + 0.5 * jnp.tanh(total * (ROOT + ROOT * CUBE * square))
            value = total * half
            slope = half + value * (1.0 - half) * (2.0 * ROOT + 6.0 * ROOT * CUBE * square)
            o_ref[0, place, :] = value.astype(BF16)
            gt_ref[0, place, :] = (g_ref[0, place, :].astype(F32) * slope).astype(BF16)
            return carry

        lax.fori_loop(0, lon // chunk, step, 0)
        x_ref[...] = dot(invt_ref[...], gt_ref[0]).astype(BF16)

    row_spec = pl.BlockSpec((1, lon, channels), lambda i: (i, 0, 0))
    column_spec = pl.BlockSpec((group_rows, channels), lambda i: (0, i))
    return pl.pallas_call(
        body,
        grid=(lat_dev,),
        in_specs=[
            row_spec,
            column_spec,
            row_spec,
            pl.BlockSpec((lon, group_rows), lambda i: (0, 0)),
            pl.BlockSpec((group_rows, lon), lambda i: (0, 0)),
        ],
        out_specs=[row_spec, row_spec, column_spec],
        out_shape=[
            jax.ShapeDtypeStruct((lat_dev, lon, channels), BF16),
            jax.ShapeDtypeStruct((lat_dev, lon, channels), BF16),
            jax.ShapeDtypeStruct((group_rows, lat_dev * channels), BF16),
        ],
        compiler_params=params(32),
        cost_estimate=cost(4 * disco.size * group_rows, disco.size * 10),
        name="activation",
    )(disco, returned, grad_output, inverse, inverse_t)


def weight_terms(mixed, grad_total):
    lat_dev, lon, wide = mixed.shape
    channels = grad_total.shape[2]

    def body(m_ref, g_ref, o_ref, acc):
        row = pl.program_id(0)
        part = dot(jnp.transpose(g_ref[0]), m_ref[0])

        @pl.when(row == 0)
        def _():
            acc[...] = part

        @pl.when(row > 0)
        def _():
            acc[...] += part

        @pl.when(row == lat_dev - 1)
        def _():
            o_ref[...] = jnp.transpose(acc[...]).astype(BF16)

    return pl.pallas_call(
        body,
        grid=(lat_dev,),
        in_specs=[
            pl.BlockSpec((1, lon, wide), lambda i: (i, 0, 0)),
            pl.BlockSpec((1, lon, channels), lambda i: (i, 0, 0)),
        ],
        out_specs=pl.BlockSpec((wide, channels), lambda i: (0, 0)),
        out_shape=jax.ShapeDtypeStruct((wide, channels), BF16),
        scratch_shapes=[pltpu.VMEM((channels, wide), F32)],
        compiler_params=params(32),
        cost_estimate=cost(2 * mixed.size * channels, mixed.size * 2),
        name="weight_terms",
    )(mixed, grad_total)


def final(bands, forward, grad_disco):
    lat_dev, lon, channels = grad_disco.shape
    group_rows = bands.shape[0]

    def body(y_ref, f_ref, d_ref, o_ref):
        o_ref[0] = (d_ref[0] + dot(f_ref[...], y_ref[...])).astype(BF16)

    row_spec = pl.BlockSpec((1, lon, channels), lambda i: (i, 0, 0))
    return pl.pallas_call(
        body,
        grid=(lat_dev,),
        in_specs=[
            pl.BlockSpec((group_rows, channels), lambda i: (0, i)),
            pl.BlockSpec((lon, group_rows), lambda i: (0, 0)),
            row_spec,
        ],
        out_specs=row_spec,
        out_shape=jax.ShapeDtypeStruct((lat_dev, lon, channels), BF16),
        compiler_params=params(24),
        cost_estimate=cost(2 * grad_disco.size * group_rows, grad_disco.size * 6),
        name="final",
    )(bands, forward, grad_disco)


def stages(count):
    found = []
    stride = 1
    while stride < count:
        factor = 4 if (count // stride) % 4 == 0 else 2
        found.append((stride, factor))
        stride *= factor
    return found


def partner(array, count, stride, by):
    return lax.ppermute(array, "lat", [(i, i ^ (by * stride)) for i in range(count)])


def sum_scatter_gather(array):
    count = lax.axis_size("lat")
    position = lax.axis_index("lat")
    plan = stages(count)
    for stride, factor in plan:
        digit = (position // stride) % factor
        pieces = array.reshape(factor, array.shape[0] // factor, array.shape[1])
        total = lax.dynamic_index_in_dim(pieces, digit, 0, False).astype(F32)
        for by in range(1, factor):
            piece = lax.dynamic_index_in_dim(pieces, digit ^ by, 0, False)
            total = total + partner(piece, count, stride, by).astype(F32)
        array = total.astype(BF16)
    for stride, factor in reversed(plan):
        digit = (position // stride) % factor
        whole = jnp.zeros((factor,) + array.shape, BF16)
        for by in range(factor):
            part = partner(array, count, stride, by) if by else array
            whole = lax.dynamic_update_index_in_dim(whole, part, digit ^ by, 0)
        array = whole.reshape(-1, array.shape[1])
    return array


def sum_everywhere(array):
    count = lax.axis_size("lat")
    for stride, factor in stages(count):
        parts = [array] + [partner(array, count, stride, by) for by in range(1, factor)]
        while len(parts) > 1:
            parts = [parts[k] + parts[k + 1] for k in range(0, len(parts), 2)]
        array = parts[0]
    return array


def neighbours(north_edge, south_edge):
    count = lax.axis_size("lat")
    from_north = lax.ppermute(south_edge, "lat", [(i, i + 1) for i in range(count - 1)])
    from_south = lax.ppermute(north_edge, "lat", [(i + 1, i) for i in range(count - 1)])
    return (from_north, from_south)


def exchange(array):
    count = lax.axis_size("lat")
    rows, width = array.shape
    blocks = array.reshape(count, rows // count, width)
    blocks = lax.all_to_all(blocks, "lat", split_axis=0, concat_axis=0, tiled=True)
    return blocks.reshape(rows, width)


def local(features, disco_rows, disco_cols, disco_basis, disco_weight, spectral_gain, grad_output):
    lat_dev, lon, channels = features.shape
    devices = lax.axis_size("lat")
    position = lax.axis_index("lat")
    degrees = spectral_gain.shape[0]
    lat_count = lat_dev * devices
    order_count = lat_count
    owned_orders = order_count // devices
    kernels, _, taps = disco_basis.shape
    forward, inverse = fourier_tables(lon, order_count, devices)
    group = forward.shape[1] // devices
    forward_t = jnp.asarray(np.ascontiguousarray(forward.T))
    inverse_t = jnp.asarray(np.ascontiguousarray(inverse.T))
    forward = jnp.asarray(forward)
    inverse = jnp.asarray(inverse)
    place = position.astype(jnp.int32).reshape(1)
    small = order_count * owned_orders * 2 * degrees * lat_dev * devices * group <= TABLE_CAP * 4

    north, south = neighbours(features[:HALO], features[lat_dev - HALO :])
    coefficients = transform(features, forward_t)
    owned = exchange(coefficients)

    packed = jnp.concatenate(
        [
            disco_rows.astype(F32)[:, None, :],
            disco_cols.astype(F32)[:, None, :],
            jnp.transpose(disco_basis, (1, 0, 2)).astype(F32),
        ],
        axis=1,
    )
    packed_north, packed_south = neighbours(packed[:HALO], packed[lat_dev - HALO :])
    packed_all = jnp.concatenate([packed_north, packed, packed_south], axis=0)
    band_rows = position * lat_dev + jnp.arange(lat_dev, dtype=jnp.int32)[:, None]
    shifts = (disco_rows - band_rows + 1) * WIN + SPAN + disco_cols
    rows_all = packed_all[:, 0].astype(jnp.int32)
    cols_all = packed_all[:, 1].astype(jnp.int32)
    back_shifts = []
    back_taps = []
    for e in range(3):
        aimed = rows_all[e : e + lat_dev] == band_rows
        back_shifts.append(jnp.where(aimed, e * WIN + SPAN - cols_all[e : e + lat_dev], NONE))
        back_taps.append(jnp.transpose(packed_all[e : e + lat_dev, 2:], (1, 0, 2)))
    back_shifts = jnp.concatenate(back_shifts, axis=1)
    back_taps = jnp.concatenate(back_taps, axis=2)
    weight_rows = disco_weight.reshape(kernels * channels, channels)
    weight_back = jnp.transpose(disco_weight, (0, 2, 1)).reshape(kernels * channels, channels)

    mixed, disco = filtered(
        features, north, south, shifts, disco_basis.astype(F32), weight_rows, True
    )

    if small:
        plain, weighted = legendre_table(order_count, degrees, lat_count)
        plain = jnp.asarray(spectral_table(plain, devices, lat_dev, group))
        weighted = jnp.asarray(spectral_table(weighted, devices, lat_dev, group))
        analysed, synthesized = spectral_forward(place, owned, weighted, plain, spectral_gain)
    else:
        _, gauss_weights = gauss_grid(lat_count)
        orders = position * owned_orders + jnp.arange(owned_orders, dtype=jnp.int32)
        legendre = legendre_block(orders, order_count, degrees, lat_count)
        plain = legendre.astype(BF16).reshape(owned_orders, degrees, devices, lat_dev)
        weighted = (legendre * jnp.asarray(gauss_weights, F32)[None, None, :]).astype(BF16)
        weighted = weighted.reshape(owned_orders, degrees, devices, lat_dev)

        def opened(array):
            array = array.reshape(devices, group, lat_dev, channels)[:, : 2 * owned_orders]
            return array.reshape(devices, owned_orders, 2, lat_dev, channels)

        def closed(array):
            array = array.reshape(devices, 2 * owned_orders, lat_dev * channels)
            array = jnp.pad(array, ((0, 0), (0, group - 2 * owned_orders), (0, 0)))
            return array.reshape(devices * group, lat_dev * channels).astype(BF16)

        analysed = jnp.einsum(
            "rlsi,srpic->rplc", weighted, opened(owned), preferred_element_type=F32
        )
        scaled = (analysed * spectral_gain).astype(BF16)
        synthesized = closed(
            jnp.einsum("rlsi,rplc->srpic", plain, scaled, preferred_element_type=F32)
        )

    returned = exchange(synthesized)
    output, grad_total, grad_synth = activation(disco, returned, grad_output, inverse, inverse_t)
    grad_owned = exchange(grad_synth)
    grad_north, grad_south = neighbours(grad_total[:HALO], grad_total[lat_dev - HALO :])
    weight_part = weight_terms(mixed, grad_total)

    if small:
        gain_part, grad_coeff = spectral_adjoint(
            place, grad_owned, plain, weighted, spectral_gain, analysed
        )
    else:
        grad_scaled = jnp.einsum(
            "rlsi,srpic->rplc", plain, opened(grad_owned), preferred_element_type=F32
        )
        gain_part = jnp.sum(analysed * grad_scaled, axis=(0, 1))
        grad_analysed = (grad_scaled * spectral_gain).astype(BF16)
        grad_coeff = closed(
            jnp.einsum("rlsi,rplc->srpic", weighted, grad_analysed, preferred_element_type=F32)
        )

    grad_bands = exchange(grad_coeff)
    grad_disco = filtered(
        grad_total, grad_north, grad_south, back_shifts, back_taps, weight_back, False
    )
    grad_features = final(grad_bands, forward, grad_disco)
    grad_weight = sum_scatter_gather(weight_part).astype(F32)
    grad_gain = sum_everywhere(gain_part)
    return (
        output,
        grad_features,
        grad_weight.reshape(kernels, channels, channels),
        grad_gain,
    )


def solution(mesh):
    return jax.shard_map(
        local,
        mesh=mesh,
        in_specs=(
            P(("group", "lat"), None, None),
            P("lat", None),
            P("lat", None),
            P(None, "lat", None),
            P(),
            P(),
            P(("group", "lat"), None, None),
        ),
        out_specs=(
            P(("group", "lat"), None, None),
            P(("group", "lat"), None, None),
            P("group", None, None),
            P("group", None),
        ),
        check_vma=False,
    )
```

```python
import math

import jax
import jax.numpy as jnp
import numpy as np
from jax import lax
from jax.experimental import pallas as pl
from jax.experimental.pallas import tpu as pltpu
from jax.sharding import PartitionSpec as P

HALO = 1
SPAN = 16
STEP = 48
WIN = STEP + 2 * SPAN
GROUP = 8
NONE = -4096
META = 16
PER = 5
CHUNK = 240
ROOT = math.sqrt(2.0 / math.pi)
CUBE = 0.044715
F32 = jnp.float32
BF16 = jnp.bfloat16
MIB = 1 << 20
TABLE_CAP = 1 << 22


def legendre_pair(nodes, lat_count):
    before = nodes * 0.0 + 1.0
    current = nodes * 1.0
    for degree in range(2, lat_count + 1):
        following = ((2.0 * degree - 1.0) * nodes * current - (degree - 1.0) * before) / degree
        before = current
        current = following
    return (before, current)


def gauss_grid(lat_count):
    counter = np.arange(1, lat_count + 1) * 1.0
    nodes = np.cos(np.pi * (counter - 0.25) / (lat_count + 0.5))
    for sweep in range(12):
        before, current = legendre_pair(nodes, lat_count)
        slope = lat_count * (nodes * current - before) / (nodes * nodes - 1.0)
        nodes = nodes - current / slope
    before, current = legendre_pair(nodes, lat_count)
    slope = lat_count * (nodes * current - before) / (nodes * nodes - 1.0)
    weights = 2.0 / ((1.0 - nodes * nodes) * slope * slope)
    return (nodes, weights)


def diagonal_table(order_count, latitude_nodes):
    sine_values = np.sqrt(1.0 - latitude_nodes * latitude_nodes)
    orders = np.arange(order_count)
    positive = np.arange(1, order_count)
    log_steps = np.concatenate(
        [np.zeros(1), 0.5 * np.cumsum(np.log((2.0 * positive + 1.0) / (2.0 * positive)))]
    )
    log_values = (
        0.5 * np.log(0.5) + log_steps[:, None] + orders[:, None] * np.log(sine_values)[None, :]
    )
    return np.exp(log_values)


def legendre_block(orders, order_count, degrees, lat_count):
    latitude_nodes, weights = gauss_grid(lat_count)
    diagonal_start = jnp.asarray(diagonal_table(order_count, latitude_nodes), jnp.float32)[orders]
    node_row = jnp.asarray(latitude_nodes, jnp.float32)[None, :]
    order_column = orders.astype(jnp.float32)[:, None]

    def block_step(carry, block_index):
        previous, earlier = carry
        produced = []
        for offset in range(16):
            degree = (block_index * 16 + offset).astype(jnp.float32)
            squared = degree * degree
            order_squared = order_column * order_column
            forward_factor = jnp.sqrt(
                jnp.maximum(4.0 * squared - 1.0, 1.0) / jnp.maximum(squared - order_squared, 1.0)
            )
            lower = (degree - 1.0) * (degree - 1.0)
            back_factor = jnp.sqrt(
                jnp.maximum(lower - order_squared, 0.0) / jnp.maximum(4.0 * lower - 1.0, 1.0)
            )
            recurred = forward_factor * (node_row * previous - back_factor * earlier)
            fresh = jnp.where(
                degree < order_column,
                0.0,
                jnp.where(degree == order_column, diagonal_start, recurred),
            )
            earlier = previous
            previous = fresh
            produced.append(fresh)
        return ((previous, earlier), jnp.stack(produced))

    zeros = jnp.zeros((orders.shape[0], lat_count), jnp.float32)
    _, blocks = lax.scan(block_step, (zeros, zeros), jnp.arange(degrees // 16, dtype=jnp.int32))
    legendre = blocks.reshape(degrees, orders.shape[0], lat_count)
    return jnp.transpose(legendre, (1, 0, 2))


def legendre_table(order_count, degrees, lat_count):
    nodes, weights = gauss_grid(lat_count)
    start = diagonal_table(order_count, nodes).astype(np.float32)
    node_row = nodes.astype(np.float32)[None, :]
    order = np.arange(order_count, dtype=np.float32)[:, None]
    one = np.float32(1.0)
    four = np.float32(4.0)
    previous = np.zeros((order_count, lat_count), np.float32)
    earlier = previous
    produced = []
    for step in range(degrees):
        degree = np.float32(step)
        squared = degree * degree
        lower = (degree - one) * (degree - one)
        ahead = np.sqrt(
            np.maximum(four * squared - one, one) / np.maximum(squared - order * order, one)
        )
        back = np.sqrt(
            np.maximum(lower - order * order, np.float32(0.0))
            / np.maximum(four * lower - one, one)
        )
        recurred = ahead * (node_row * previous - back * earlier)
        fresh = np.where(degree < order, np.float32(0.0), np.where(degree == order, start, recurred))
        earlier = previous
        previous = fresh.astype(np.float32)
        produced.append(previous)
    legendre = np.stack(produced, axis=1)
    weighted = legendre * weights.astype(np.float32)[None, None, :]
    return (legendre.astype(BF16), weighted.astype(BF16))


def fourier_tables(lon_count, order_count, devices):
    angle = 2.0 * np.pi / lon_count * (np.outer(np.arange(lon_count), np.arange(order_count)) % lon_count)
    cosine = np.cos(angle)
    sine = np.sin(angle)
    doubled = np.where(np.arange(order_count) == 0, 1.0, 2.0)[None, :]
    owned = order_count // devices
    group = -(-2 * owned // GROUP) * GROUP

    def grouped(real, imaginary):
        pairs = np.stack([real, imaginary], axis=2).reshape(lon_count, devices, 2 * owned)
        pairs = np.pad(pairs, ((0, 0), (0, 0), (0, group - 2 * owned)))
        return pairs.reshape(lon_count, devices * group).astype(np.float32).astype(BF16)

    forward = grouped(cosine / lon_count, -sine / lon_count)
    inverse = grouped(doubled * cosine, -doubled * sine)
    return (forward, inverse)


def spectral_table(table, devices, lat_dev, group):
    orders, degrees, lats = table.shape
    owned = orders // devices
    split = np.asarray(table, np.float32).reshape(devices, owned, degrees, devices, lat_dev)
    full = np.zeros((devices, owned, 2, degrees, lat_dev, devices, group), np.float32)
    for r in range(owned):
        for p in range(2):
            full[:, r, p, :, :, :, 2 * r + p] = np.transpose(split[:, r], (0, 1, 3, 2))
    return full.reshape(devices, owned * 2 * degrees, lat_dev * devices * group).astype(BF16)


def params(limit, **kwargs):
    return pltpu.CompilerParams(vmem_limit_bytes=limit * MIB, **kwargs)


def cost(flops, nbytes):
    return pl.CostEstimate(flops=int(flops), bytes_accessed=int(nbytes), transcendentals=0)


def dot(a, b):
    return jnp.dot(a, b, preferred_element_type=F32)


def dot_t(a, b):
    return lax.dot_general(a, b, (((0,), (0,)), ((), ())), preferred_element_type=F32)


def in_hbm(array):
    return pltpu.with_memory_space_constraint(array, pltpu.HBM)


def every(*shape):
    return pl.BlockSpec(shape, lambda *g: (0,) * len(shape))


VMEM = pl.BlockSpec(memory_space=pltpu.VMEM)
SMEM = pl.BlockSpec(memory_space=pltpu.SMEM)
ANYWHERE = pl.BlockSpec(memory_space=pl.ANY)


def transform(position, features, table, rows, cols, basis):
    lat_dev, lon, channels = features.shape
    depth = table.shape[0]
    kernels, _, taps = basis.shape
    edges = (0, lat_dev - 1)

    def body(p_ref, x_ref, t_ref, row_ref, col_ref, basis_ref, o_ref, first_ref, last_ref, *rest):
        edge_refs = (first_ref, last_ref)
        held, table_held, wide, meta, sem, edge_sem, small_sem = rest[:7]
        small_held = rest[7:]
        table_copy = pltpu.make_async_copy(t_ref, table_held, small_sem.at[3])
        copies = [
            pltpu.make_async_copy(x_ref.at[i], held.at[i], sem.at[i]) for i in range(lat_dev)
        ]
        small_copies = [
            pltpu.make_async_copy(ref, to, small_sem.at[n])
            for n, (ref, to) in enumerate(zip((row_ref, col_ref, basis_ref), small_held, strict=True))
        ]
        for copy in [*small_copies, table_copy, *copies]:
            copy.start()
        for copy in small_copies:
            copy.wait()
        rows_held, cols_held, basis_held = small_held
        sent = []
        for n, edge in enumerate(edges):
            wide[...] = jnp.zeros_like(wide)
            own = rows_held[edge : edge + 1, :] - (p_ref[0] * lat_dev + edge)
            wide[0:1, 0:taps] = own.astype(F32)
            wide[1:2, 0:taps] = cols_held[edge : edge + 1, :].astype(F32)
            for k in range(kernels):
                wide[2 + k : 3 + k, 0:taps] = basis_held[k, edge : edge + 1, :].astype(F32)
            meta[n] = wide[...].astype(BF16)
            sent.append(
                pltpu.make_async_copy(
                    meta.at[n], edge_refs[n].at[pl.ds(lon, META)], edge_sem.at[n, 1]
                )
            )
            sent[-1].start()
        table_copy.wait()
        for i, copy in enumerate(copies):
            copy.wait()
            for n, edge in enumerate(edges):
                if i == edge:
                    sent.append(
                        pltpu.make_async_copy(
                            held.at[i], edge_refs[n].at[pl.ds(0, lon)], edge_sem.at[n, 0]
                        )
                    )
                    sent[-1].start()
            o_ref[:, i * channels : (i + 1) * channels] = dot(table_held[...], held[i]).astype(BF16)
        for copy in sent:
            copy.wait()

    return pl.pallas_call(
        body,
        in_specs=[SMEM] + [ANYWHERE] * 5,
        out_specs=[VMEM, ANYWHERE, ANYWHERE],
        out_shape=[
            pltpu.HBM((depth, lat_dev * channels), BF16),
            pltpu.HBM((lon + META, channels), BF16),
            pltpu.HBM((lon + META, channels), BF16),
        ],
        scratch_shapes=[
            pltpu.VMEM((lat_dev, lon, channels), BF16),
            pltpu.VMEM(table.shape, BF16),
            pltpu.VMEM((META, channels), F32),
            pltpu.VMEM((2, META, channels), BF16),
            pltpu.SemaphoreType.DMA((lat_dev,)),
            pltpu.SemaphoreType.DMA((2, 2)),
            pltpu.SemaphoreType.DMA((4,)),
            pltpu.VMEM(rows.shape, rows.dtype),
            pltpu.VMEM(cols.shape, cols.dtype),
            pltpu.VMEM(basis.shape, basis.dtype),
        ],
        compiler_params=params(16),
        cost_estimate=cost(2 * depth * lon * channels * lat_dev, features.size * 2),
        name="transform",
    )(
        position,
        in_hbm(features),
        in_hbm(table),
        in_hbm(rows),
        in_hbm(cols),
        in_hbm(basis),
    )


def filtered(middle, north, south, shifts, taps, weights, rows, before=None):
    first, stride, total = rows
    lat_dev = shifts.shape[0]
    lon, channels = middle[0].shape[-2:]
    kernels = taps.shape[0]
    count = taps.shape[2]
    wide = kernels * channels
    per = PER
    chunk = per * STEP
    edges = north is not None
    keep = weights is None

    def body(shift_ref, tap_ref, *rest):
        rest = list(rest)
        mid_refs = [rest.pop(0) for _ in middle]
        if len(middle) == 1:
            mid_refs = [mid_refs[0].at[i] for i in range(lat_dev)]
        north_ref, south_ref = (rest.pop(0), rest.pop(0)) if edges else (None, None)
        w_ref = None if keep else rest.pop(0)
        if before is not None:
            rest.pop(0)
        out_ref, ext, sem = rest[:3]
        mixed_ref = None if keep else rest[3]
        step_id = pl.program_id(0)
        row = first + stride * step_id

        def copies(which):
            made = []
            for e in which:
                src = (
                    north_ref if e == 0 else south_ref if e == lat_dev + 1 else mid_refs[e - 1]
                )
                for n, (a, b, size) in enumerate(
                    ((0, SPAN, lon), (lon - SPAN, 0, SPAN), (0, lon + SPAN, SPAN))
                ):
                    made.append(
                        pltpu.make_async_copy(
                            src.at[pl.ds(a, size)], ext.at[e, pl.ds(b, size)], sem.at[e, n]
                        )
                    )
            return made

        needed = []
        seen = set()
        for g in range(total):
            now = [e for e in range(first + stride * g, first + stride * g + 3) if e not in seen]
            seen.update(now)
            needed.append(now)

        @pl.when(step_id == 0)
        def _():
            for now in needed:
                for copy in copies(now):
                    copy.start()

        across = lax.broadcasted_iota(jnp.int32, (STEP, 3 * WIN), 1)
        down = lax.broadcasted_iota(jnp.int32, (STEP, 3 * WIN), 0)
        delta = across - down
        band = [jnp.zeros((STEP, 3 * WIN), F32) for _ in range(kernels)]
        for t in range(count):
            hit = delta == shift_ref[row, t]
            for k in range(kernels):
                band[k] = band[k] + jnp.where(hit, tap_ref[k, row, t], 0.0)
        band = jnp.concatenate(band, axis=0).astype(BF16)

        for g, now in enumerate(needed):

            @pl.when(step_id == g)
            def _(now=now):
                for copy in copies(now):
                    copy.wait()

        for c in range(lon // chunk):
            for b in range(per):
                start = c * chunk + b * STEP
                window = jnp.concatenate(
                    [ext[row + e, start : start + WIN, :] for e in range(3)], axis=0
                )
                sums = dot(band, window).astype(BF16)
                for k in range(kernels):
                    part = sums[k * STEP : (k + 1) * STEP]
                    lanes = slice(k * channels, (k + 1) * channels)
                    if keep:
                        out_ref[0, start : start + STEP, lanes] = part
                    else:
                        mixed_ref[c % 2, b * STEP : (b + 1) * STEP, lanes] = part
            if not keep:
                out_ref[0, c * chunk : (c + 1) * chunk, :] = sum(
                    lax.dot_general(
                        mixed_ref[c % 2, :, k * channels : (k + 1) * channels],
                        w_ref[k * channels : (k + 1) * channels, :],
                        (((1,), (1,)), ((), ())),
                        preferred_element_type=F32,
                    )
                    for k in range(kernels)
                ).astype(BF16)

    depth = wide if keep else channels
    operands = [shifts, taps, *(in_hbm(array) for array in middle)]
    in_specs = [SMEM, SMEM] + [ANYWHERE] * len(middle)
    scratch = [
        pltpu.VMEM((lat_dev + 2, lon + 2 * SPAN, channels), BF16),
        pltpu.SemaphoreType.DMA((lat_dev + 2, 3)),
    ]
    if edges:
        operands += [in_hbm(north), in_hbm(south)]
        in_specs += [ANYWHERE, ANYWHERE]
    if not keep:
        operands.append(in_hbm(weights))
        in_specs.append(every(wide, channels))
        scratch.append(pltpu.VMEM((2, chunk, wide), BF16))
    aliases = {}
    if before is not None:
        aliases[len(operands)] = 0
        operands.append(before)
        in_specs.append(ANYWHERE)
    return pl.pallas_call(
        body,
        grid=(total,),
        in_specs=in_specs,
        out_specs=pl.BlockSpec((1, lon, depth), lambda g: (first + stride * g, 0, 0)),
        out_shape=pltpu.HBM((lat_dev, lon, depth), BF16),
        input_output_aliases=aliases,
        scratch_shapes=scratch,
        compiler_params=params(24),
        cost_estimate=cost(
            2 * total * lon * channels * (wide * (0 if keep else 1) + 3 * WIN * kernels),
            total * lon * channels * 8,
        ),
        name="filtered" if keep else "filtered_back",
    )(*operands)


def blocks_of(ref, start, rows, lanes):
    block = ref[:, start : start + rows, lanes].astype(F32)
    return block.reshape(block.shape[0] * rows, block.shape[2]).astype(BF16)


def spectral_forward(position, owned, table_in, table_out, gain):
    group_rows, width = owned.shape
    _, rows, depth = table_in.shape
    degrees, channels = gain.shape
    lat_dev = width // channels

    def body(p_ref, x_ref, a_ref, b_ref, g_ref, analysed_ref, o_ref):
        analysed = jnp.zeros((rows, channels), F32)
        for i in range(lat_dev):
            analysed = analysed + dot(
                a_ref[0, :, i * group_rows : (i + 1) * group_rows],
                x_ref[:, i * channels : (i + 1) * channels],
            )
        analysed_ref[...] = analysed
        gain_rows = jnp.concatenate([g_ref[...]] * (rows // degrees), axis=0)
        scaled = (analysed * gain_rows).astype(BF16)
        for i in range(lat_dev):
            o_ref[:, i * channels : (i + 1) * channels] = dot_t(
                b_ref[0, :, i * group_rows : (i + 1) * group_rows], scaled
            ).astype(BF16)

    table_spec = pl.BlockSpec((1, rows, depth), lambda g, p: (p[0], 0, 0))
    return pl.pallas_call(
        body,
        grid_spec=pltpu.PrefetchScalarGridSpec(
            num_scalar_prefetch=1,
            grid=(1,),
            in_specs=[
                pl.BlockSpec((group_rows, width), lambda g, p: (0, 0)),
                table_spec,
                table_spec,
                pl.BlockSpec((degrees, channels), lambda g, p: (0, 0)),
            ],
            out_specs=[
                pl.BlockSpec((rows, channels), lambda g, p: (0, 0)),
                pl.BlockSpec((group_rows, width), lambda g, p: (0, 0)),
            ],
        ),
        out_shape=[
            pltpu.HBM((rows, channels), F32),
            pltpu.HBM((group_rows, width), BF16),
        ],
        compiler_params=params(16),
        name="spectral_forward",
    )(position, owned, in_hbm(table_in), in_hbm(table_out), in_hbm(gain))


def spectral_adjoint(position, received, table_in, table_out, gain, analysed, terms):
    devices, block_rows, width = received.shape
    group = block_rows - terms
    group_rows = devices * group
    _, rows, depth = table_in.shape
    degrees, channels = gain.shape
    lat_dev = width // channels

    def body(p_ref, x_ref, b_ref, a_ref, g_ref, analysed_ref, gain_ref, o_ref):
        summed = jnp.sum(x_ref[:, 0:terms, :].astype(F32), axis=0).astype(BF16)
        for d in range(devices):
            o_ref[d, 0:terms, :] = summed
        scaled = jnp.zeros((rows, channels), F32)
        for i in range(lat_dev):
            scaled = scaled + dot(
                b_ref[0, :, i * group_rows : (i + 1) * group_rows],
                blocks_of(x_ref, terms, group, slice(i * channels, (i + 1) * channels)),
            )
        products = analysed_ref[...] * scaled
        total = jnp.zeros((degrees, channels), F32)
        for s in range(rows // degrees):
            total = total + products[s * degrees : (s + 1) * degrees]
        gain_ref[...] = total
        gain_rows = jnp.concatenate([g_ref[...]] * (rows // degrees), axis=0)
        grad = (gain_rows * scaled).astype(BF16)
        for i in range(lat_dev):
            part = dot_t(a_ref[0, :, i * group_rows : (i + 1) * group_rows], grad)
            o_ref[:, terms:block_rows, i * channels : (i + 1) * channels] = part.reshape(
                devices, group, channels
            ).astype(BF16)

    table_spec = pl.BlockSpec((1, rows, depth), lambda g, p: (p[0], 0, 0))
    return pl.pallas_call(
        body,
        grid_spec=pltpu.PrefetchScalarGridSpec(
            num_scalar_prefetch=1,
            grid=(1,),
            in_specs=[
                pl.BlockSpec((devices, block_rows, width), lambda g, p: (0, 0, 0)),
                table_spec,
                table_spec,
                pl.BlockSpec((degrees, channels), lambda g, p: (0, 0)),
                pl.BlockSpec((rows, channels), lambda g, p: (0, 0)),
            ],
            out_specs=[
                pl.BlockSpec((degrees, channels), lambda g, p: (0, 0)),
                pl.BlockSpec((devices, block_rows, width), lambda g, p: (0, 0, 0)),
            ],
        ),
        out_shape=[
            jax.ShapeDtypeStruct((degrees, channels), F32),
            pltpu.HBM((devices, block_rows, width), BF16),
        ],
        compiler_params=params(16),
        name="spectral_adjoint",
    )(
        position,
        received,
        in_hbm(table_in),
        in_hbm(table_out),
        in_hbm(gain),
        in_hbm(analysed),
    )


def activation(mixed, weights, returned, grad_output, inverse, inverse_t, devices, terms):
    lat_dev, lon, wide = mixed.shape
    channels = grad_output.shape[2]
    group_rows = returned.shape[0]
    group = group_rows // devices
    chunk = CHUNK
    piece = wide // devices // lat_dev

    def body(m_ref, w_ref, y_ref, g_ref, inv_ref, invt_ref, *rest):
        o_ref, row_refs = rest[0], rest[1 : 1 + lat_dev]
        rest = rest[1 + lat_dev :]
        acc, held, sem = rest[-3:]
        row = pl.program_id(0)
        gt_ref = held.at[row]
        for c in range(lon // chunk):
            place = slice(c * chunk, (c + 1) * chunk)
            total = dot(m_ref[0, place, :], w_ref[...]) + dot(inv_ref[place, :], y_ref[...])
            square = total * total
            half = 0.5 + 0.5 * jnp.tanh(total * (ROOT + ROOT * CUBE * square))
            value = total * half
            slope = half + value * (1.0 - half) * (2.0 * ROOT + 6.0 * ROOT * CUBE * square)
            o_ref[0, place, :] = value.astype(BF16)
            gt_ref[place, :] = (g_ref[0, place, :].astype(F32) * slope).astype(BF16)
        for i in range(lat_dev):

            @pl.when(row == i)
            def _(i=i):
                pltpu.make_async_copy(held.at[i], row_refs[i], sem.at[i]).start()

        spectrum = dot(invt_ref[...], gt_ref[...])
        part = dot(jnp.transpose(gt_ref[...]), m_ref[0])

        @pl.when(row == lat_dev - 1)
        def _():
            for i in range(lat_dev - 1):
                pltpu.make_async_copy(held.at[i], row_refs[i], sem.at[i]).wait()

        @pl.when(row == 0)
        def _():
            acc[...] = part

        @pl.when(row > 0)
        def _():
            acc[...] += part

        if not terms:
            x_ref, weight_ref = rest[0:2]
            x_ref[...] = spectrum.astype(BF16)

            @pl.when(row == lat_dev - 1)
            def _():
                weight_ref[...] = jnp.transpose(acc[...]).astype(BF16)
                pltpu.make_async_copy(held.at[row], row_refs[-1], sem.at[row]).wait()

            return
        x_ref = rest[0]
        spectrum = spectrum.reshape(devices, group, channels).astype(BF16)
        for i in range(lat_dev):

            @pl.when(row == i)
            def _(i=i):
                x_ref[:, terms : terms + group, i * channels : (i + 1) * channels] = spectrum

        @pl.when(row == lat_dev - 1)
        def _():
            weight = jnp.transpose(acc[...]).astype(BF16)
            for d in range(devices):
                for i in range(lat_dev):
                    at = (d * lat_dev + i) * piece
                    x_ref[d, 0:piece, i * channels : (i + 1) * channels] = weight[at : at + piece]
            pltpu.make_async_copy(held.at[row], row_refs[-1], sem.at[row]).wait()

    row_spec = pl.BlockSpec((1, lon, channels), lambda i: (i, 0, 0))
    column_spec = pl.BlockSpec((group_rows, channels), lambda i: (0, i))
    if terms:
        last_specs = [pl.BlockSpec((devices, terms + group, lat_dev * channels), lambda i: (0, 0, 0))]
        last_shapes = [pltpu.HBM((devices, terms + group, lat_dev * channels), BF16)]
    else:
        last_specs = [column_spec, pl.BlockSpec((wide, channels), lambda i: (0, 0))]
        last_shapes = [
            jax.ShapeDtypeStruct((group_rows, lat_dev * channels), BF16),
            jax.ShapeDtypeStruct((wide, channels), BF16),
        ]
    return pl.pallas_call(
        body,
        grid=(lat_dev,),
        in_specs=[
            pl.BlockSpec((1, lon, wide), lambda i: (i, 0, 0)),
            every(wide, channels),
            column_spec,
            row_spec,
            every(lon, group_rows),
            every(group_rows, lon),
        ],
        out_specs=[row_spec] + [ANYWHERE] * lat_dev + last_specs,
        out_shape=[
            pltpu.HBM((lat_dev, lon, channels), BF16),
        ]
        + [pltpu.HBM((lon, channels), BF16)] * lat_dev
        + last_shapes,
        scratch_shapes=[
            pltpu.VMEM((channels, wide), F32),
            pltpu.VMEM((lat_dev, lon, channels), BF16),
            pltpu.SemaphoreType.DMA((lat_dev,)),
        ],
        compiler_params=params(40),
        cost_estimate=cost(
            4 * grad_output.size * (group_rows + wide), grad_output.size * 14
        ),
        name="activation",
    )(
        in_hbm(mixed),
        in_hbm(weights),
        returned,
        in_hbm(grad_output),
        in_hbm(inverse),
        in_hbm(inverse_t),
    )


def final(received, forward, grad_disco, terms):
    lat_dev, lon, channels = grad_disco.shape
    row_spec = pl.BlockSpec((1, lon, channels), lambda i: (i, 0, 0))
    out_specs = [row_spec]
    out_shape = [pltpu.HBM((lat_dev, lon, channels), BF16)]
    if terms:
        devices, block_rows, _ = received.shape
        first_spec = pl.BlockSpec((devices, block_rows, channels), lambda i: (0, 0, i))
        out_specs.append(pl.BlockSpec((devices, 1, terms, channels), lambda i: (0, i, 0, 0)))
        out_shape.append(pltpu.HBM((devices, lat_dev, terms, channels), F32))
    else:
        first_spec = pl.BlockSpec((received.shape[0], channels), lambda i: (0, i))
    depth = forward.shape[1]

    def body(y_ref, f_ref, d_ref, o_ref, *rest):
        if terms:
            rest[0][:, 0] = y_ref[:, 0:terms, :].astype(F32)
            bands = blocks_of(y_ref, terms, block_rows - terms, slice(0, channels))
        else:
            bands = y_ref[...]
        o_ref[0] = (d_ref[0].astype(F32) + dot(f_ref[...], bands)).astype(BF16)

    return pl.pallas_call(
        body,
        grid=(lat_dev,),
        in_specs=[first_spec, pl.BlockSpec((lon, depth), lambda i: (0, 0)), row_spec],
        out_specs=out_specs,
        out_shape=out_shape,
        compiler_params=params(24),
        cost_estimate=cost(2 * grad_disco.size * depth, grad_disco.size * 6),
        name="final",
    )(received, in_hbm(forward), in_hbm(grad_disco))


def stages(count):
    found = []
    stride = 1
    while stride < count:
        factor = 4 if (count // stride) % 4 == 0 else 2
        found.append((stride, factor))
        stride *= factor
    return found


def partner(array, count, stride, by):
    return lax.ppermute(array, "lat", [(i, i ^ (by * stride)) for i in range(count)])


def sum_scatter_gather(array):
    count = lax.axis_size("lat")
    position = lax.axis_index("lat")
    plan = stages(count)
    for stride, factor in plan:
        digit = (position // stride) % factor
        pieces = array.reshape(factor, array.shape[0] // factor, array.shape[1])
        total = lax.dynamic_index_in_dim(pieces, digit, 0, False).astype(F32)
        for by in range(1, factor):
            piece = lax.dynamic_index_in_dim(pieces, digit ^ by, 0, False)
            total = total + partner(piece, count, stride, by).astype(F32)
        array = total.astype(BF16)
    for stride, factor in reversed(plan):
        digit = (position // stride) % factor
        whole = jnp.zeros((factor,) + array.shape, BF16)
        for by in range(factor):
            part = partner(array, count, stride, by) if by else array
            whole = lax.dynamic_update_index_in_dim(whole, part, digit ^ by, 0)
        array = whole.reshape(-1, array.shape[1])
    return array


def sum_everywhere(array, between):
    count = lax.axis_size("lat")
    plan = stages(count)
    for n, (stride, factor) in enumerate(plan):
        if n == len(plan) - 1:
            array, between = lax.optimization_barrier((array, between))
        parts = [array] + [partner(array, count, stride, by) for by in range(1, factor)]
        while len(parts) > 1:
            parts = [parts[k] + parts[k + 1] for k in range(0, len(parts), 2)]
        array = parts[0]
    return (array, between)


def neighbours(north_edge, south_edge):
    count = lax.axis_size("lat")
    from_north = lax.ppermute(south_edge, "lat", [(i, i + 1) for i in range(count - 1)])
    from_south = lax.ppermute(north_edge, "lat", [(i + 1, i) for i in range(count - 1)])
    return (from_north, from_south)


def exchange(blocks):
    return lax.all_to_all(blocks, "lat", split_axis=0, concat_axis=0, tiled=True)


def exchange_rows(array):
    count = lax.axis_size("lat")
    rows, width = array.shape
    return exchange(array.reshape(count, rows // count, width)).reshape(rows, width)


def local(features, disco_rows, disco_cols, disco_basis, disco_weight, spectral_gain, grad_output):
    lat_dev, lon, channels = features.shape
    devices = lax.axis_size("lat")
    position = lax.axis_index("lat")
    degrees = spectral_gain.shape[0]
    lat_count = lat_dev * devices
    order_count = lat_count
    owned_orders = order_count // devices
    kernels, _, taps = disco_basis.shape
    wide = kernels * channels
    forward, inverse = fourier_tables(lon, order_count, devices)
    group = forward.shape[1] // devices
    forward_t = jnp.asarray(np.ascontiguousarray(forward.T))
    inverse_t = jnp.asarray(np.ascontiguousarray(inverse.T))
    forward = jnp.asarray(forward)
    inverse = jnp.asarray(inverse)
    place = position.astype(jnp.int32).reshape(1)
    piece = wide // devices // lat_dev
    small = (
        order_count * owned_orders * 2 * degrees * lat_dev * devices * group <= TABLE_CAP * 4
        and piece * devices * lat_dev == wide
        and piece % 16 == 0
    )
    terms = piece if small else 0
    inner = (1, 1, lat_dev - 2)
    outer = (0, lat_dev - 1, 2)

    coefficients, first_row, last_row = transform(
        place, features, forward_t, disco_rows, disco_cols, disco_basis
    )
    north, south = neighbours(first_row, last_row)
    owned = exchange_rows(coefficients)

    band_rows = position * lat_dev + jnp.arange(lat_dev, dtype=jnp.int32)[:, None]
    basis = disco_basis.astype(F32)
    offsets = disco_rows - band_rows
    shifts = (offsets + 1) * WIN + SPAN + disco_cols
    weight_rows = disco_weight.reshape(wide, channels)
    mixed = filtered([features], None, None, shifts, basis, None, inner)
    owned, mixed = lax.optimization_barrier((owned, mixed))
    mixed = filtered([features], north, south, shifts, basis, None, outer, mixed)

    packed = jnp.concatenate(
        [
            offsets.astype(F32)[:, None, :],
            disco_cols.astype(F32)[:, None, :],
            jnp.transpose(basis, (1, 0, 2)),
        ],
        axis=1,
    )
    packed_all = jnp.concatenate(
        [
            north[None, lon : lon + 2 + kernels, :taps].astype(F32),
            packed,
            south[None, lon : lon + 2 + kernels, :taps].astype(F32),
        ],
        axis=0,
    )
    back_shifts = []
    back_taps = []
    for e in range(3):
        aimed = packed_all[e : e + lat_dev, 0] == 1.0 - e
        columns = packed_all[e : e + lat_dev, 1].astype(jnp.int32)
        back_shifts.append(jnp.where(aimed, e * WIN + SPAN - columns, NONE))
        back_taps.append(jnp.transpose(packed_all[e : e + lat_dev, 2:], (1, 0, 2)))
    back_shifts = jnp.concatenate(back_shifts, axis=1)
    back_taps = jnp.concatenate(back_taps, axis=2)

    if small:
        plain, weighted = legendre_table(order_count, degrees, lat_count)
        plain = jnp.asarray(spectral_table(plain, devices, lat_dev, group))
        weighted = jnp.asarray(spectral_table(weighted, devices, lat_dev, group))
        analysed, synthesized = spectral_forward(place, owned, weighted, plain, spectral_gain)
    else:
        _, gauss_weights = gauss_grid(lat_count)
        orders = position * owned_orders + jnp.arange(owned_orders, dtype=jnp.int32)
        legendre = legendre_block(orders, order_count, degrees, lat_count)
        plain = legendre.astype(BF16).reshape(owned_orders, degrees, devices, lat_dev)
        weighted = (legendre * jnp.asarray(gauss_weights, F32)[None, None, :]).astype(BF16)
        weighted = weighted.reshape(owned_orders, degrees, devices, lat_dev)

        def opened(array):
            array = array.reshape(devices, group, lat_dev, channels)[:, : 2 * owned_orders]
            return array.reshape(devices, owned_orders, 2, lat_dev, channels)

        def closed(array):
            array = array.reshape(devices, 2 * owned_orders, lat_dev * channels)
            array = jnp.pad(array, ((0, 0), (0, group - 2 * owned_orders), (0, 0)))
            return array.reshape(devices * group, lat_dev * channels).astype(BF16)

        analysed = jnp.einsum(
            "rlsi,srpic->rplc", weighted, opened(owned), preferred_element_type=F32
        )
        scaled = (analysed * spectral_gain).astype(BF16)
        synthesized = closed(
            jnp.einsum("rlsi,rplc->srpic", plain, scaled, preferred_element_type=F32)
        )

    returned = exchange_rows(synthesized)
    output, *blocks = activation(
        mixed, weight_rows, returned, grad_output, inverse, inverse_t, devices, terms
    )
    grad_rows, blocks = blocks[:lat_dev], blocks[lat_dev:]
    grad_north, grad_south = neighbours(grad_rows[0], grad_rows[-1])
    part = filtered(grad_rows, None, None, back_shifts, back_taps, weight_rows, inner)
    if small:
        grad_owned, part = lax.optimization_barrier((exchange(blocks[0]), part))
        gain_part, grad_blocks = spectral_adjoint(
            place, grad_owned, plain, weighted, spectral_gain, analysed, terms
        )
        grad_bands = exchange(grad_blocks)
    else:
        grad_owned = exchange_rows(blocks[0])
        grad_scaled = jnp.einsum(
            "rlsi,srpic->rplc", plain, opened(grad_owned), preferred_element_type=F32
        )
        gain_part = jnp.sum(analysed * grad_scaled, axis=(0, 1))
        grad_analysed = (grad_scaled * spectral_gain).astype(BF16)
        grad_coeff = closed(
            jnp.einsum("rlsi,rplc->srpic", weighted, grad_analysed, preferred_element_type=F32)
        )
        grad_bands = exchange_rows(grad_coeff)

    grad_disco = filtered(
        grad_rows, grad_north, grad_south, back_shifts, back_taps, weight_rows, outer, part
    )
    grad_gain, grad_disco = sum_everywhere(gain_part, grad_disco)
    grad_features, *grad_weight = final(grad_bands, forward, grad_disco, terms)
    if not small:
        grad_weight = [sum_scatter_gather(blocks[1]).astype(F32)]
    return (
        output,
        grad_features,
        grad_weight[0].reshape(kernels, channels, channels),
        grad_gain,
    )


def solution(mesh):
    return jax.shard_map(
        local,
        mesh=mesh,
        in_specs=(
            P(("group", "lat"), None, None),
            P("lat", None),
            P("lat", None),
            P(None, "lat", None),
            P(),
            P(),
            P(("group", "lat"), None, None),
        ),
        out_specs=(
            P(("group", "lat"), None, None),
            P(("group", "lat"), None, None),
            P("group", None, None),
            P("group", None),
        ),
        check_vma=False,
    )
```

```python
import math

import jax
import jax.numpy as jnp
import numpy as np
from jax import lax
from jax.experimental import pallas as pl
from jax.experimental.pallas import tpu as pltpu
from jax.sharding import PartitionSpec as P

HALO = 1
SPAN = 16
STEP = 48
WIN = STEP + 2 * SPAN
GROUP = 8
NONE = -4096
META = 16
PER = 5
CHUNK = 240
ROOT = math.sqrt(2.0 / math.pi)
CUBE = 0.044715
F32 = jnp.float32
BF16 = jnp.bfloat16
MIB = 1 << 20
TABLE_CAP = 1 << 22


def legendre_pair(nodes, lat_count):
    before = nodes * 0.0 + 1.0
    current = nodes * 1.0
    for degree in range(2, lat_count + 1):
        following = ((2.0 * degree - 1.0) * nodes * current - (degree - 1.0) * before) / degree
        before = current
        current = following
    return (before, current)


def gauss_grid(lat_count):
    counter = np.arange(1, lat_count + 1) * 1.0
    nodes = np.cos(np.pi * (counter - 0.25) / (lat_count + 0.5))
    for sweep in range(12):
        before, current = legendre_pair(nodes, lat_count)
        slope = lat_count * (nodes * current - before) / (nodes * nodes - 1.0)
        nodes = nodes - current / slope
    before, current = legendre_pair(nodes, lat_count)
    slope = lat_count * (nodes * current - before) / (nodes * nodes - 1.0)
    weights = 2.0 / ((1.0 - nodes * nodes) * slope * slope)
    return (nodes, weights)


def diagonal_table(order_count, latitude_nodes):
    sine_values = np.sqrt(1.0 - latitude_nodes * latitude_nodes)
    orders = np.arange(order_count)
    positive = np.arange(1, order_count)
    log_steps = np.concatenate(
        [np.zeros(1), 0.5 * np.cumsum(np.log((2.0 * positive + 1.0) / (2.0 * positive)))]
    )
    log_values = (
        0.5 * np.log(0.5) + log_steps[:, None] + orders[:, None] * np.log(sine_values)[None, :]
    )
    return np.exp(log_values)


def legendre_block(orders, order_count, degrees, lat_count):
    latitude_nodes, weights = gauss_grid(lat_count)
    diagonal_start = jnp.asarray(diagonal_table(order_count, latitude_nodes), jnp.float32)[orders]
    node_row = jnp.asarray(latitude_nodes, jnp.float32)[None, :]
    order_column = orders.astype(jnp.float32)[:, None]

    def block_step(carry, block_index):
        previous, earlier = carry
        produced = []
        for offset in range(16):
            degree = (block_index * 16 + offset).astype(jnp.float32)
            squared = degree * degree
            order_squared = order_column * order_column
            forward_factor = jnp.sqrt(
                jnp.maximum(4.0 * squared - 1.0, 1.0) / jnp.maximum(squared - order_squared, 1.0)
            )
            lower = (degree - 1.0) * (degree - 1.0)
            back_factor = jnp.sqrt(
                jnp.maximum(lower - order_squared, 0.0) / jnp.maximum(4.0 * lower - 1.0, 1.0)
            )
            recurred = forward_factor * (node_row * previous - back_factor * earlier)
            fresh = jnp.where(
                degree < order_column,
                0.0,
                jnp.where(degree == order_column, diagonal_start, recurred),
            )
            earlier = previous
            previous = fresh
            produced.append(fresh)
        return ((previous, earlier), jnp.stack(produced))

    zeros = jnp.zeros((orders.shape[0], lat_count), jnp.float32)
    _, blocks = lax.scan(block_step, (zeros, zeros), jnp.arange(degrees // 16, dtype=jnp.int32))
    legendre = blocks.reshape(degrees, orders.shape[0], lat_count)
    return jnp.transpose(legendre, (1, 0, 2))


def legendre_table(order_count, degrees, lat_count):
    nodes, weights = gauss_grid(lat_count)
    start = diagonal_table(order_count, nodes).astype(np.float32)
    node_row = nodes.astype(np.float32)[None, :]
    order = np.arange(order_count, dtype=np.float32)[:, None]
    one = np.float32(1.0)
    four = np.float32(4.0)
    previous = np.zeros((order_count, lat_count), np.float32)
    earlier = previous
    produced = []
    for step in range(degrees):
        degree = np.float32(step)
        squared = degree * degree
        lower = (degree - one) * (degree - one)
        ahead = np.sqrt(
            np.maximum(four * squared - one, one) / np.maximum(squared - order * order, one)
        )
        back = np.sqrt(
            np.maximum(lower - order * order, np.float32(0.0))
            / np.maximum(four * lower - one, one)
        )
        recurred = ahead * (node_row * previous - back * earlier)
        fresh = np.where(degree < order, np.float32(0.0), np.where(degree == order, start, recurred))
        earlier = previous
        previous = fresh.astype(np.float32)
        produced.append(previous)
    legendre = np.stack(produced, axis=1)
    weighted = legendre * weights.astype(np.float32)[None, None, :]
    return (legendre.astype(BF16), weighted.astype(BF16))


def fourier_tables(lon_count, order_count, devices):
    angle = 2.0 * np.pi / lon_count * (np.outer(np.arange(lon_count), np.arange(order_count)) % lon_count)
    cosine = np.cos(angle)
    sine = np.sin(angle)
    doubled = np.where(np.arange(order_count) == 0, 1.0, 2.0)[None, :]
    owned = order_count // devices
    group = -(-2 * owned // GROUP) * GROUP

    def grouped(real, imaginary):
        pairs = np.stack([real, imaginary], axis=2).reshape(lon_count, devices, 2 * owned)
        pairs = np.pad(pairs, ((0, 0), (0, 0), (0, group - 2 * owned)))
        return pairs.reshape(lon_count, devices * group).astype(np.float32).astype(BF16)

    forward = grouped(cosine / lon_count, -sine / lon_count)
    inverse = grouped(doubled * cosine, -doubled * sine)
    return (forward, inverse)


def spectral_table(table, devices, lat_dev, group):
    orders, degrees, lats = table.shape
    owned = orders // devices
    split = np.asarray(table, np.float32).reshape(devices, owned, degrees, devices, lat_dev)
    full = np.zeros((devices, owned, 2, degrees, lat_dev, devices, group), np.float32)
    for r in range(owned):
        for p in range(2):
            full[:, r, p, :, :, :, 2 * r + p] = np.transpose(split[:, r], (0, 1, 3, 2))
    return full.reshape(devices, owned * 2 * degrees, lat_dev * devices * group).astype(BF16)


def params(limit, **kwargs):
    return pltpu.CompilerParams(vmem_limit_bytes=limit * MIB, **kwargs)


def cost(flops, nbytes):
    return pl.CostEstimate(flops=int(flops), bytes_accessed=int(nbytes), transcendentals=0)


def dot(a, b):
    return jnp.dot(a, b, preferred_element_type=F32)


def dot_t(a, b):
    return lax.dot_general(a, b, (((0,), (0,)), ((), ())), preferred_element_type=F32)


def in_hbm(array):
    return pltpu.with_memory_space_constraint(array, pltpu.HBM)


def every(*shape):
    return pl.BlockSpec(shape, lambda *g: (0,) * len(shape))


VMEM = pl.BlockSpec(memory_space=pltpu.VMEM)
SMEM = pl.BlockSpec(memory_space=pltpu.SMEM)
ANYWHERE = pl.BlockSpec(memory_space=pl.ANY)


def transform(position, features, table, rows, cols, basis):
    lat_dev, lon, channels = features.shape
    depth = table.shape[0]
    kernels, _, taps = basis.shape
    edges = (0, lat_dev - 1)

    def body(p_ref, x_ref, t_ref, row_ref, col_ref, basis_ref, o_ref, first_ref, last_ref, *rest):
        edge_refs = (first_ref, last_ref)
        held, table_held, wide, meta, sem, edge_sem, small_sem = rest[:7]
        small_held = rest[7:]
        table_copy = pltpu.make_async_copy(t_ref, table_held, small_sem.at[3])
        copies = [
            pltpu.make_async_copy(x_ref.at[i], held.at[i], sem.at[i]) for i in range(lat_dev)
        ]
        small_copies = [
            pltpu.make_async_copy(ref, to, small_sem.at[n])
            for n, (ref, to) in enumerate(zip((row_ref, col_ref, basis_ref), small_held, strict=True))
        ]
        order = edges + tuple(i for i in range(lat_dev) if i not in edges)
        for copy in [*small_copies, table_copy, *(copies[i] for i in order)]:
            copy.start()
        for copy in small_copies:
            copy.wait()
        rows_held, cols_held, basis_held = small_held
        sent = []
        for n, edge in enumerate(edges):
            wide[...] = jnp.zeros_like(wide)
            own = rows_held[edge : edge + 1, :] - (p_ref[0] * lat_dev + edge)
            wide[0:1, 0:taps] = own.astype(F32)
            wide[1:2, 0:taps] = cols_held[edge : edge + 1, :].astype(F32)
            for k in range(kernels):
                wide[2 + k : 3 + k, 0:taps] = basis_held[k, edge : edge + 1, :].astype(F32)
            meta[n] = wide[...].astype(BF16)
            sent.append(
                pltpu.make_async_copy(
                    meta.at[n], edge_refs[n].at[pl.ds(lon, META)], edge_sem.at[n, 1]
                )
            )
            sent[-1].start()
        table_copy.wait()
        for i in order:
            copies[i].wait()
            for n, edge in enumerate(edges):
                if i == edge:
                    sent.append(
                        pltpu.make_async_copy(
                            held.at[i], edge_refs[n].at[pl.ds(0, lon)], edge_sem.at[n, 0]
                        )
                    )
                    sent[-1].start()
            o_ref[:, i * channels : (i + 1) * channels] = dot(table_held[...], held[i]).astype(BF16)
        for copy in sent:
            copy.wait()

    return pl.pallas_call(
        body,
        in_specs=[SMEM] + [ANYWHERE] * 5,
        out_specs=[VMEM, ANYWHERE, ANYWHERE],
        out_shape=[
            pltpu.HBM((depth, lat_dev * channels), BF16),
            pltpu.HBM((lon + META, channels), BF16),
            pltpu.HBM((lon + META, channels), BF16),
        ],
        scratch_shapes=[
            pltpu.VMEM((lat_dev, lon, channels), BF16),
            pltpu.VMEM(table.shape, BF16),
            pltpu.VMEM((META, channels), F32),
            pltpu.VMEM((2, META, channels), BF16),
            pltpu.SemaphoreType.DMA((lat_dev,)),
            pltpu.SemaphoreType.DMA((2, 2)),
            pltpu.SemaphoreType.DMA((4,)),
            pltpu.VMEM(rows.shape, rows.dtype),
            pltpu.VMEM(cols.shape, cols.dtype),
            pltpu.VMEM(basis.shape, basis.dtype),
        ],
        compiler_params=params(16),
        cost_estimate=cost(2 * depth * lon * channels * lat_dev, features.size * 2),
        name="transform",
    )(
        position,
        in_hbm(features),
        in_hbm(table),
        in_hbm(rows),
        in_hbm(cols),
        in_hbm(basis),
    )


def filtered(middle, north, south, shifts, taps, weights, rows, before=None):
    first, stride, total = rows
    lat_dev = shifts.shape[0]
    lon, channels = middle[0].shape[-2:]
    kernels = taps.shape[0]
    count = taps.shape[2]
    wide = kernels * channels
    per = PER
    chunk = per * STEP
    edges = north is not None
    keep = weights is None

    def body(shift_ref, tap_ref, *rest):
        rest = list(rest)
        mid_refs = [rest.pop(0) for _ in middle]
        if len(middle) == 1:
            mid_refs = [mid_refs[0].at[i] for i in range(lat_dev)]
        north_ref, south_ref = (rest.pop(0), rest.pop(0)) if edges else (None, None)
        w_ref = None if keep else rest.pop(0)
        if before is not None:
            rest.pop(0)
        out_ref, ext, sem = rest[:3]
        mixed_ref = None if keep else rest[3]
        step_id = pl.program_id(0)
        row = first + stride * step_id

        def copies(which):
            made = []
            for e in which:
                src = (
                    north_ref if e == 0 else south_ref if e == lat_dev + 1 else mid_refs[e - 1]
                )
                for n, (a, b, size) in enumerate(
                    ((0, SPAN, lon), (lon - SPAN, 0, SPAN), (0, lon + SPAN, SPAN))
                ):
                    made.append(
                        pltpu.make_async_copy(
                            src.at[pl.ds(a, size)], ext.at[e, pl.ds(b, size)], sem.at[e, n]
                        )
                    )
            return made

        needed = []
        seen = set()
        for g in range(total):
            now = [e for e in range(first + stride * g, first + stride * g + 3) if e not in seen]
            seen.update(now)
            needed.append(now)

        @pl.when(step_id == 0)
        def _():
            for now in needed:
                for copy in copies(now):
                    copy.start()

        across = lax.broadcasted_iota(jnp.int32, (STEP, 3 * WIN), 1)
        down = lax.broadcasted_iota(jnp.int32, (STEP, 3 * WIN), 0)
        delta = across - down
        band = [jnp.zeros((STEP, 3 * WIN), F32) for _ in range(kernels)]
        for t in range(count):
            hit = delta == shift_ref[row, t]
            for k in range(kernels):
                band[k] = band[k] + jnp.where(hit, tap_ref[k, row, t], 0.0)
        band = jnp.concatenate(band, axis=0).astype(BF16)

        for g, now in enumerate(needed):

            @pl.when(step_id == g)
            def _(now=now):
                for copy in copies(now):
                    copy.wait()

        for c in range(lon // chunk):
            for b in range(per):
                start = c * chunk + b * STEP
                window = jnp.concatenate(
                    [ext[row + e, start : start + WIN, :] for e in range(3)], axis=0
                )
                sums = dot(band, window).astype(BF16)
                for k in range(kernels):
                    part = sums[k * STEP : (k + 1) * STEP]
                    lanes = slice(k * channels, (k + 1) * channels)
                    if keep:
                        out_ref[0, start : start + STEP, lanes] = part
                    else:
                        mixed_ref[c % 2, b * STEP : (b + 1) * STEP, lanes] = part
            if not keep:
                out_ref[0, c * chunk : (c + 1) * chunk, :] = sum(
                    lax.dot_general(
                        mixed_ref[c % 2, :, k * channels : (k + 1) * channels],
                        w_ref[k * channels : (k + 1) * channels, :],
                        (((1,), (1,)), ((), ())),
                        preferred_element_type=F32,
                    )
                    for k in range(kernels)
                ).astype(BF16)

    depth = wide if keep else channels
    operands = [shifts, taps, *(in_hbm(array) for array in middle)]
    in_specs = [SMEM, SMEM] + [ANYWHERE] * len(middle)
    scratch = [
        pltpu.VMEM((lat_dev + 2, lon + 2 * SPAN, channels), BF16),
        pltpu.SemaphoreType.DMA((lat_dev + 2, 3)),
    ]
    if edges:
        operands += [north, south]
        in_specs += [ANYWHERE, ANYWHERE]
    if not keep:
        operands.append(in_hbm(weights))
        in_specs.append(every(wide, channels))
        scratch.append(pltpu.VMEM((2, chunk, wide), BF16))
    aliases = {}
    if before is not None:
        aliases[len(operands)] = 0
        operands.append(before)
        in_specs.append(ANYWHERE)
    return pl.pallas_call(
        body,
        grid=(total,),
        in_specs=in_specs,
        out_specs=pl.BlockSpec((1, lon, depth), lambda g: (first + stride * g, 0, 0)),
        out_shape=pltpu.HBM((lat_dev, lon, depth), BF16),
        input_output_aliases=aliases,
        scratch_shapes=scratch,
        compiler_params=params(24),
        cost_estimate=cost(
            2 * total * lon * channels * (wide * (0 if keep else 1) + 3 * WIN * kernels),
            total * lon * channels * 8,
        ),
        name="filtered" if keep else "filtered_back",
    )(*operands)


def blocks_of(ref, start, rows, lanes):
    block = ref[:, start : start + rows, lanes].astype(F32)
    return block.reshape(block.shape[0] * rows, block.shape[2]).astype(BF16)


def spectral_forward(position, owned, table_in, table_out, gain):
    group_rows, width = owned.shape
    _, rows, depth = table_in.shape
    degrees, channels = gain.shape
    lat_dev = width // channels

    def body(p_ref, x_ref, a_ref, b_ref, g_ref, analysed_ref, o_ref):
        analysed = jnp.zeros((rows, channels), F32)
        for i in range(lat_dev):
            analysed = analysed + dot(
                a_ref[0, :, i * group_rows : (i + 1) * group_rows],
                x_ref[:, i * channels : (i + 1) * channels],
            )
        analysed_ref[...] = analysed
        gain_rows = jnp.concatenate([g_ref[...]] * (rows // degrees), axis=0)
        scaled = (analysed * gain_rows).astype(BF16)
        for i in range(lat_dev):
            o_ref[:, i * channels : (i + 1) * channels] = dot_t(
                b_ref[0, :, i * group_rows : (i + 1) * group_rows], scaled
            ).astype(BF16)

    table_spec = pl.BlockSpec((1, rows, depth), lambda g, p: (p[0], 0, 0))
    return pl.pallas_call(
        body,
        grid_spec=pltpu.PrefetchScalarGridSpec(
            num_scalar_prefetch=1,
            grid=(1,),
            in_specs=[
                pl.BlockSpec((group_rows, width), lambda g, p: (0, 0)),
                table_spec,
                table_spec,
                pl.BlockSpec((degrees, channels), lambda g, p: (0, 0)),
            ],
            out_specs=[
                pl.BlockSpec((rows, channels), lambda g, p: (0, 0)),
                pl.BlockSpec((group_rows, width), lambda g, p: (0, 0)),
            ],
        ),
        out_shape=[
            pltpu.HBM((rows, channels), F32),
            pltpu.HBM((group_rows, width), BF16),
        ],
        compiler_params=params(16),
        name="spectral_forward",
    )(position, owned, in_hbm(table_in), in_hbm(table_out), in_hbm(gain))


def spectral_adjoint(position, received, table_in, table_out, gain, analysed, terms):
    devices, block_rows, width = received.shape
    group = block_rows - terms
    group_rows = devices * group
    _, rows, depth = table_in.shape
    degrees, channels = gain.shape
    lat_dev = width // channels

    def body(p_ref, x_ref, b_ref, a_ref, g_ref, analysed_ref, gain_ref, o_ref):
        summed = jnp.sum(x_ref[:, 0:terms, :].astype(F32), axis=0).astype(BF16)
        for d in range(devices):
            o_ref[d, 0:terms, :] = summed
        scaled = jnp.zeros((rows, channels), F32)
        for i in range(lat_dev):
            scaled = scaled + dot(
                b_ref[0, :, i * group_rows : (i + 1) * group_rows],
                blocks_of(x_ref, terms, group, slice(i * channels, (i + 1) * channels)),
            )
        products = analysed_ref[...] * scaled
        total = jnp.zeros((degrees, channels), F32)
        for s in range(rows // degrees):
            total = total + products[s * degrees : (s + 1) * degrees]
        gain_ref[...] = total
        gain_rows = jnp.concatenate([g_ref[...]] * (rows // degrees), axis=0)
        grad = (gain_rows * scaled).astype(BF16)
        for i in range(lat_dev):
            part = dot_t(a_ref[0, :, i * group_rows : (i + 1) * group_rows], grad)
            o_ref[:, terms:block_rows, i * channels : (i + 1) * channels] = part.reshape(
                devices, group, channels
            ).astype(BF16)

    table_spec = pl.BlockSpec((1, rows, depth), lambda g, p: (p[0], 0, 0))
    return pl.pallas_call(
        body,
        grid_spec=pltpu.PrefetchScalarGridSpec(
            num_scalar_prefetch=1,
            grid=(1,),
            in_specs=[
                pl.BlockSpec((devices, block_rows, width), lambda g, p: (0, 0, 0)),
                table_spec,
                table_spec,
                pl.BlockSpec((degrees, channels), lambda g, p: (0, 0)),
                pl.BlockSpec((rows, channels), lambda g, p: (0, 0)),
            ],
            out_specs=[
                pl.BlockSpec((degrees, channels), lambda g, p: (0, 0)),
                pl.BlockSpec((devices, block_rows, width), lambda g, p: (0, 0, 0)),
            ],
        ),
        out_shape=[
            jax.ShapeDtypeStruct((degrees, channels), F32),
            pltpu.HBM((devices, block_rows, width), BF16),
        ],
        compiler_params=params(16),
        name="spectral_adjoint",
    )(
        position,
        received,
        in_hbm(table_in),
        in_hbm(table_out),
        in_hbm(gain),
        in_hbm(analysed),
    )


def activation(mixed, weights, returned, grad_output, inverse, inverse_t, devices, terms):
    lat_dev, lon, wide = mixed.shape
    channels = grad_output.shape[2]
    group_rows = returned.shape[0]
    group = group_rows // devices
    chunk = CHUNK
    piece = wide // devices // lat_dev

    def body(m_ref, w_ref, y_ref, g_ref, inv_ref, invt_ref, *rest):
        o_ref, row_refs = rest[0], rest[1 : 1 + lat_dev]
        rest = rest[1 + lat_dev :]
        acc, held, sem = rest[-3:]
        row = pl.program_id(0)
        gt_ref = held.at[row]
        for c in range(lon // chunk):
            place = slice(c * chunk, (c + 1) * chunk)
            total = dot(m_ref[0, place, :], w_ref[...]) + dot(inv_ref[place, :], y_ref[...])
            square = total * total
            half = 0.5 + 0.5 * jnp.tanh(total * (ROOT + ROOT * CUBE * square))
            value = total * half
            slope = half + value * (1.0 - half) * (2.0 * ROOT + 6.0 * ROOT * CUBE * square)
            o_ref[0, place, :] = value.astype(BF16)
            gt_ref[place, :] = (g_ref[0, place, :].astype(F32) * slope).astype(BF16)
        for i in range(lat_dev):

            @pl.when(row == i)
            def _(i=i):
                pltpu.make_async_copy(held.at[i], row_refs[i], sem.at[i]).start()

        spectrum = dot(invt_ref[...], gt_ref[...])
        part = dot(jnp.transpose(gt_ref[...]), m_ref[0])

        @pl.when(row == lat_dev - 1)
        def _():
            for i in range(lat_dev - 1):
                pltpu.make_async_copy(held.at[i], row_refs[i], sem.at[i]).wait()

        @pl.when(row == 0)
        def _():
            acc[...] = part

        @pl.when(row > 0)
        def _():
            acc[...] += part

        if not terms:
            x_ref, weight_ref = rest[0:2]
            x_ref[...] = spectrum.astype(BF16)

            @pl.when(row == lat_dev - 1)
            def _():
                weight_ref[...] = jnp.transpose(acc[...]).astype(BF16)
                pltpu.make_async_copy(held.at[row], row_refs[-1], sem.at[row]).wait()

            return
        x_ref = rest[0]
        spectrum = spectrum.reshape(devices, group, channels).astype(BF16)
        for i in range(lat_dev):

            @pl.when(row == i)
            def _(i=i):
                x_ref[:, terms : terms + group, i * channels : (i + 1) * channels] = spectrum

        @pl.when(row == lat_dev - 1)
        def _():
            weight = jnp.transpose(acc[...]).astype(BF16)
            for d in range(devices):
                for i in range(lat_dev):
                    at = (d * lat_dev + i) * piece
                    x_ref[d, 0:piece, i * channels : (i + 1) * channels] = weight[at : at + piece]
            pltpu.make_async_copy(held.at[row], row_refs[-1], sem.at[row]).wait()

    row_spec = pl.BlockSpec((1, lon, channels), lambda i: (i, 0, 0))
    column_spec = pl.BlockSpec((group_rows, channels), lambda i: (0, i))
    if terms:
        last_specs = [pl.BlockSpec((devices, terms + group, lat_dev * channels), lambda i: (0, 0, 0))]
        last_shapes = [pltpu.HBM((devices, terms + group, lat_dev * channels), BF16)]
    else:
        last_specs = [column_spec, pl.BlockSpec((wide, channels), lambda i: (0, 0))]
        last_shapes = [
            jax.ShapeDtypeStruct((group_rows, lat_dev * channels), BF16),
            jax.ShapeDtypeStruct((wide, channels), BF16),
        ]
    return pl.pallas_call(
        body,
        grid=(lat_dev,),
        in_specs=[
            pl.BlockSpec((1, lon, wide), lambda i: (i, 0, 0)),
            every(wide, channels),
            column_spec,
            row_spec,
            every(lon, group_rows),
            every(group_rows, lon),
        ],
        out_specs=[row_spec] + [ANYWHERE] * lat_dev + last_specs,
        out_shape=[
            pltpu.HBM((lat_dev, lon, channels), BF16),
        ]
        + [pltpu.HBM((lon, channels), BF16)] * lat_dev
        + last_shapes,
        scratch_shapes=[
            pltpu.VMEM((channels, wide), F32),
            pltpu.VMEM((lat_dev, lon, channels), BF16),
            pltpu.SemaphoreType.DMA((lat_dev,)),
        ],
        compiler_params=params(40),
        cost_estimate=cost(
            4 * grad_output.size * (group_rows + wide), grad_output.size * 14
        ),
        name="activation",
    )(
        in_hbm(mixed),
        in_hbm(weights),
        returned,
        in_hbm(grad_output),
        in_hbm(inverse),
        in_hbm(inverse_t),
    )


def final(received, forward, grad_disco, terms):
    lat_dev, lon, channels = grad_disco.shape
    depth = forward.shape[1]

    def body(y_ref, f_ref, d_ref, o_ref, *rest):
        w_ref = rest[0] if terms else None
        f_held, d_held, o_held, f_sem, d_sem, o_sem = rest[-7:-1]
        w_held = rest[-1]
        table = pltpu.make_async_copy(f_ref, f_held, f_sem)
        incoming = [
            pltpu.make_async_copy(d_ref.at[i], d_held.at[i], d_sem.at[i]) for i in range(lat_dev)
        ]
        outgoing = [
            pltpu.make_async_copy(o_held.at[i], o_ref.at[i], o_sem.at[i]) for i in range(lat_dev)
        ]
        table.start()
        for copy in incoming:
            copy.start()
        if terms:
            for i in range(lat_dev):
                w_held[:, i] = y_ref[:, 0:terms, i * channels : (i + 1) * channels].astype(F32)
            outgoing.append(pltpu.make_async_copy(w_held, w_ref, o_sem.at[lat_dev]))
            outgoing[-1].start()
        table.wait()
        for i in range(lat_dev):
            lanes = slice(i * channels, (i + 1) * channels)
            if terms:
                bands = blocks_of(y_ref, terms, y_ref.shape[1] - terms, lanes)
            else:
                bands = y_ref[:, lanes]
            incoming[i].wait()
            for c in range(lon // CHUNK):
                place = slice(c * CHUNK, (c + 1) * CHUNK)
                o_held[i, place, :] = (
                    d_held[i, place, :].astype(F32) + dot(f_held[place, :], bands)
                ).astype(BF16)
            outgoing[i].start()
        for copy in outgoing:
            copy.wait()

    out_shape = [pltpu.HBM((lat_dev, lon, channels), BF16)]
    gathered = (16, 128)
    if terms:
        gathered = (received.shape[0], lat_dev, terms, channels)
        out_shape.append(pltpu.HBM(gathered, F32))
    return pl.pallas_call(
        body,
        in_specs=[VMEM, ANYWHERE, ANYWHERE],
        out_specs=[ANYWHERE] * len(out_shape),
        out_shape=out_shape,
        scratch_shapes=[
            pltpu.VMEM((lon, depth), BF16),
            pltpu.VMEM((lat_dev, lon, channels), BF16),
            pltpu.VMEM((lat_dev, lon, channels), BF16),
            pltpu.SemaphoreType.DMA,
            pltpu.SemaphoreType.DMA((lat_dev,)),
            pltpu.SemaphoreType.DMA((lat_dev + 1,)),
            pltpu.VMEM(gathered, F32),
        ],
        compiler_params=params(24),
        cost_estimate=cost(2 * grad_disco.size * depth, grad_disco.size * 6),
        name="final",
    )(received, in_hbm(forward), in_hbm(grad_disco))


def stages(count):
    found = []
    stride = 1
    while stride < count:
        factor = 4 if (count // stride) % 4 == 0 else 2
        found.append((stride, factor))
        stride *= factor
    return found


def partner(array, count, stride, by):
    return lax.ppermute(array, "lat", [(i, i ^ (by * stride)) for i in range(count)])


def sum_scatter_gather(array):
    count = lax.axis_size("lat")
    position = lax.axis_index("lat")
    plan = stages(count)
    for stride, factor in plan:
        digit = (position // stride) % factor
        pieces = array.reshape(factor, array.shape[0] // factor, array.shape[1])
        total = lax.dynamic_index_in_dim(pieces, digit, 0, False).astype(F32)
        for by in range(1, factor):
            piece = lax.dynamic_index_in_dim(pieces, digit ^ by, 0, False)
            total = total + partner(piece, count, stride, by).astype(F32)
        array = total.astype(BF16)
    for stride, factor in reversed(plan):
        digit = (position // stride) % factor
        whole = jnp.zeros((factor,) + array.shape, BF16)
        for by in range(factor):
            part = partner(array, count, stride, by) if by else array
            whole = lax.dynamic_update_index_in_dim(whole, part, digit ^ by, 0)
        array = whole.reshape(-1, array.shape[1])
    return array


def sum_everywhere(array, between, then):
    count = lax.axis_size("lat")
    plan = stages(count)
    for n, (stride, factor) in enumerate(plan):
        last = n == len(plan) - 1
        if last:
            array, between = lax.optimization_barrier((array, between))
        parts = [array] + [partner(array, count, stride, by) for by in range(1, factor)]
        if last:
            parts, result = lax.optimization_barrier((parts, then(between)))
        while len(parts) > 1:
            parts = [parts[k] + parts[k + 1] for k in range(0, len(parts), 2)]
        array = parts[0]
    return (array, result)


def neighbours(north_edge, south_edge):
    count = lax.axis_size("lat")
    from_north = lax.ppermute(south_edge, "lat", [(i, i + 1) for i in range(count - 1)])
    from_south = lax.ppermute(north_edge, "lat", [(i + 1, i) for i in range(count - 1)])
    return (from_north, from_south)


def exchange(blocks):
    return lax.all_to_all(blocks, "lat", split_axis=0, concat_axis=0, tiled=True)


def exchange_rows(array):
    count = lax.axis_size("lat")
    rows, width = array.shape
    return exchange(array.reshape(count, rows // count, width)).reshape(rows, width)


def local(features, disco_rows, disco_cols, disco_basis, disco_weight, spectral_gain, grad_output):
    lat_dev, lon, channels = features.shape
    devices = lax.axis_size("lat")
    position = lax.axis_index("lat")
    degrees = spectral_gain.shape[0]
    lat_count = lat_dev * devices
    order_count = lat_count
    owned_orders = order_count // devices
    kernels, _, taps = disco_basis.shape
    wide = kernels * channels
    forward, inverse = fourier_tables(lon, order_count, devices)
    group = forward.shape[1] // devices
    forward_t = jnp.asarray(np.ascontiguousarray(forward.T))
    inverse_t = jnp.asarray(np.ascontiguousarray(inverse.T))
    forward = jnp.asarray(forward)
    inverse = jnp.asarray(inverse)
    place = position.astype(jnp.int32).reshape(1)
    piece = wide // devices // lat_dev
    small = (
        order_count * owned_orders * 2 * degrees * lat_dev * devices * group <= TABLE_CAP * 4
        and piece * devices * lat_dev == wide
        and piece % 16 == 0
    )
    terms = piece if small else 0
    inner = (1, 1, lat_dev - 2)
    outer = (0, lat_dev - 1, 2)

    coefficients, first_row, last_row = transform(
        place, features, forward_t, disco_rows, disco_cols, disco_basis
    )
    north, south = neighbours(first_row, last_row)
    owned = exchange_rows(coefficients)

    band_rows = position * lat_dev + jnp.arange(lat_dev, dtype=jnp.int32)[:, None]
    basis = disco_basis.astype(F32)
    offsets = disco_rows - band_rows
    shifts = (offsets + 1) * WIN + SPAN + disco_cols
    weight_rows = disco_weight.reshape(wide, channels)
    mixed = filtered([features], None, None, shifts, basis, None, inner)
    owned, mixed = lax.optimization_barrier((owned, mixed))
    mixed = filtered([features], north, south, shifts, basis, None, outer, mixed)

    packed = jnp.concatenate(
        [
            offsets.astype(F32)[:, None, :],
            disco_cols.astype(F32)[:, None, :],
            jnp.transpose(basis, (1, 0, 2)),
        ],
        axis=1,
    )
    packed_all = jnp.concatenate(
        [
            north[None, lon : lon + 2 + kernels, :taps].astype(F32),
            packed,
            south[None, lon : lon + 2 + kernels, :taps].astype(F32),
        ],
        axis=0,
    )
    back_shifts = []
    back_taps = []
    for e in range(3):
        aimed = packed_all[e : e + lat_dev, 0] == 1.0 - e
        columns = packed_all[e : e + lat_dev, 1].astype(jnp.int32)
        back_shifts.append(jnp.where(aimed, e * WIN + SPAN - columns, NONE))
        back_taps.append(jnp.transpose(packed_all[e : e + lat_dev, 2:], (1, 0, 2)))
    back_shifts = jnp.concatenate(back_shifts, axis=1)
    back_taps = jnp.concatenate(back_taps, axis=2)

    if small:
        plain, weighted = legendre_table(order_count, degrees, lat_count)
        plain = jnp.asarray(spectral_table(plain, devices, lat_dev, group))
        weighted = jnp.asarray(spectral_table(weighted, devices, lat_dev, group))
        analysed, synthesized = spectral_forward(place, owned, weighted, plain, spectral_gain)
    else:
        _, gauss_weights = gauss_grid(lat_count)
        orders = position * owned_orders + jnp.arange(owned_orders, dtype=jnp.int32)
        legendre = legendre_block(orders, order_count, degrees, lat_count)
        plain = legendre.astype(BF16).reshape(owned_orders, degrees, devices, lat_dev)
        weighted = (legendre * jnp.asarray(gauss_weights, F32)[None, None, :]).astype(BF16)
        weighted = weighted.reshape(owned_orders, degrees, devices, lat_dev)

        def opened(array):
            array = array.reshape(devices, group, lat_dev, channels)[:, : 2 * owned_orders]
            return array.reshape(devices, owned_orders, 2, lat_dev, channels)

        def closed(array):
            array = array.reshape(devices, 2 * owned_orders, lat_dev * channels)
            array = jnp.pad(array, ((0, 0), (0, group - 2 * owned_orders), (0, 0)))
            return array.reshape(devices * group, lat_dev * channels).astype(BF16)

        analysed = jnp.einsum(
            "rlsi,srpic->rplc", weighted, opened(owned), preferred_element_type=F32
        )
        scaled = (analysed * spectral_gain).astype(BF16)
        synthesized = closed(
            jnp.einsum("rlsi,rplc->srpic", plain, scaled, preferred_element_type=F32)
        )

    returned = exchange_rows(synthesized)
    output, *blocks = activation(
        mixed, weight_rows, returned, grad_output, inverse, inverse_t, devices, terms
    )
    grad_rows, blocks = blocks[:lat_dev], blocks[lat_dev:]
    grad_north, grad_south = neighbours(grad_rows[0], grad_rows[-1])
    part = filtered(grad_rows, None, None, back_shifts, back_taps, weight_rows, inner)
    if small:
        grad_owned, part = lax.optimization_barrier((exchange(blocks[0]), part))
        gain_part, grad_blocks = spectral_adjoint(
            place, grad_owned, plain, weighted, spectral_gain, analysed, terms
        )
        grad_bands = exchange(grad_blocks)
    else:
        grad_owned = exchange_rows(blocks[0])
        grad_scaled = jnp.einsum(
            "rlsi,srpic->rplc", plain, opened(grad_owned), preferred_element_type=F32
        )
        gain_part = jnp.sum(analysed * grad_scaled, axis=(0, 1))
        grad_analysed = (grad_scaled * spectral_gain).astype(BF16)
        grad_coeff = closed(
            jnp.einsum("rlsi,rplc->srpic", weighted, grad_analysed, preferred_element_type=F32)
        )
        grad_bands = exchange_rows(grad_coeff)

    grad_disco = filtered(
        grad_rows, grad_north, grad_south, back_shifts, back_taps, weight_rows, outer, part
    )
    grad_gain, (grad_features, *grad_weight) = sum_everywhere(
        gain_part, grad_disco, lambda held: final(grad_bands, forward, held, terms)
    )
    if not small:
        grad_weight = [sum_scatter_gather(blocks[1]).astype(F32)]
    return (
        output,
        grad_features,
        grad_weight[0].reshape(kernels, channels, channels),
        grad_gain,
    )


def solution(mesh):
    return jax.shard_map(
        local,
        mesh=mesh,
        in_specs=(
            P(("group", "lat"), None, None),
            P("lat", None),
            P("lat", None),
            P(None, "lat", None),
            P(),
            P(),
            P(("group", "lat"), None, None),
        ),
        out_specs=(
            P(("group", "lat"), None, None),
            P(("group", "lat"), None, None),
            P("group", None, None),
            P("group", None),
        ),
        check_vma=False,
    )
```

```python
import math

import jax
import jax.numpy as jnp
import numpy as np
from jax import lax
from jax.experimental import pallas as pl
from jax.experimental.pallas import tpu as pltpu
from jax.sharding import PartitionSpec as P

HALO = 1
SPAN = 16
STEP = 48
WIN = STEP + 2 * SPAN
GROUP = 8
NONE = -4096
META = 16
PER = 5
CHUNK = 240
ROOT = math.sqrt(2.0 / math.pi)
CUBE = 0.044715
F32 = jnp.float32
BF16 = jnp.bfloat16
MIB = 1 << 20
TABLE_CAP = 1 << 22


def legendre_pair(nodes, lat_count):
    before = nodes * 0.0 + 1.0
    current = nodes * 1.0
    for degree in range(2, lat_count + 1):
        following = ((2.0 * degree - 1.0) * nodes * current - (degree - 1.0) * before) / degree
        before = current
        current = following
    return (before, current)


def gauss_grid(lat_count):
    counter = np.arange(1, lat_count + 1) * 1.0
    nodes = np.cos(np.pi * (counter - 0.25) / (lat_count + 0.5))
    for sweep in range(12):
        before, current = legendre_pair(nodes, lat_count)
        slope = lat_count * (nodes * current - before) / (nodes * nodes - 1.0)
        nodes = nodes - current / slope
    before, current = legendre_pair(nodes, lat_count)
    slope = lat_count * (nodes * current - before) / (nodes * nodes - 1.0)
    weights = 2.0 / ((1.0 - nodes * nodes) * slope * slope)
    return (nodes, weights)


def diagonal_table(order_count, latitude_nodes):
    sine_values = np.sqrt(1.0 - latitude_nodes * latitude_nodes)
    orders = np.arange(order_count)
    positive = np.arange(1, order_count)
    log_steps = np.concatenate(
        [np.zeros(1), 0.5 * np.cumsum(np.log((2.0 * positive + 1.0) / (2.0 * positive)))]
    )
    log_values = (
        0.5 * np.log(0.5) + log_steps[:, None] + orders[:, None] * np.log(sine_values)[None, :]
    )
    return np.exp(log_values)


def legendre_block(orders, order_count, degrees, lat_count):
    latitude_nodes, weights = gauss_grid(lat_count)
    diagonal_start = jnp.asarray(diagonal_table(order_count, latitude_nodes), jnp.float32)[orders]
    node_row = jnp.asarray(latitude_nodes, jnp.float32)[None, :]
    order_column = orders.astype(jnp.float32)[:, None]

    def block_step(carry, block_index):
        previous, earlier = carry
        produced = []
        for offset in range(16):
            degree = (block_index * 16 + offset).astype(jnp.float32)
            squared = degree * degree
            order_squared = order_column * order_column
            forward_factor = jnp.sqrt(
                jnp.maximum(4.0 * squared - 1.0, 1.0) / jnp.maximum(squared - order_squared, 1.0)
            )
            lower = (degree - 1.0) * (degree - 1.0)
            back_factor = jnp.sqrt(
                jnp.maximum(lower - order_squared, 0.0) / jnp.maximum(4.0 * lower - 1.0, 1.0)
            )
            recurred = forward_factor * (node_row * previous - back_factor * earlier)
            fresh = jnp.where(
                degree < order_column,
                0.0,
                jnp.where(degree == order_column, diagonal_start, recurred),
            )
            earlier = previous
            previous = fresh
            produced.append(fresh)
        return ((previous, earlier), jnp.stack(produced))

    zeros = jnp.zeros((orders.shape[0], lat_count), jnp.float32)
    _, blocks = lax.scan(block_step, (zeros, zeros), jnp.arange(degrees // 16, dtype=jnp.int32))
    legendre = blocks.reshape(degrees, orders.shape[0], lat_count)
    return jnp.transpose(legendre, (1, 0, 2))


def legendre_table(order_count, degrees, lat_count):
    nodes, weights = gauss_grid(lat_count)
    start = diagonal_table(order_count, nodes).astype(np.float32)
    node_row = nodes.astype(np.float32)[None, :]
    order = np.arange(order_count, dtype=np.float32)[:, None]
    one = np.float32(1.0)
    four = np.float32(4.0)
    previous = np.zeros((order_count, lat_count), np.float32)
    earlier = previous
    produced = []
    for step in range(degrees):
        degree = np.float32(step)
        squared = degree * degree
        lower = (degree - one) * (degree - one)
        ahead = np.sqrt(
            np.maximum(four * squared - one, one) / np.maximum(squared - order * order, one)
        )
        back = np.sqrt(
            np.maximum(lower - order * order, np.float32(0.0))
            / np.maximum(four * lower - one, one)
        )
        recurred = ahead * (node_row * previous - back * earlier)
        fresh = np.where(degree < order, np.float32(0.0), np.where(degree == order, start, recurred))
        earlier = previous
        previous = fresh.astype(np.float32)
        produced.append(previous)
    legendre = np.stack(produced, axis=1)
    weighted = legendre * weights.astype(np.float32)[None, None, :]
    return (legendre.astype(BF16), weighted.astype(BF16))


def fourier_tables(lon_count, order_count, devices):
    angle = 2.0 * np.pi / lon_count * (np.outer(np.arange(lon_count), np.arange(order_count)) % lon_count)
    cosine = np.cos(angle)
    sine = np.sin(angle)
    doubled = np.where(np.arange(order_count) == 0, 1.0, 2.0)[None, :]
    owned = order_count // devices
    group = -(-2 * owned // GROUP) * GROUP

    def grouped(real, imaginary):
        pairs = np.stack([real, imaginary], axis=2).reshape(lon_count, devices, 2 * owned)
        pairs = np.pad(pairs, ((0, 0), (0, 0), (0, group - 2 * owned)))
        return pairs.reshape(lon_count, devices * group).astype(np.float32).astype(BF16)

    forward = grouped(cosine / lon_count, -sine / lon_count)
    inverse = grouped(doubled * cosine, -doubled * sine)
    return (forward, inverse)


def spectral_table(table, devices, lat_dev, group):
    orders, degrees, lats = table.shape
    owned = orders // devices
    split = np.asarray(table, np.float32).reshape(devices, owned, degrees, devices, lat_dev)
    full = np.zeros((devices, owned, 2, degrees, lat_dev, devices, group), np.float32)
    for r in range(owned):
        for p in range(2):
            full[:, r, p, :, :, :, 2 * r + p] = np.transpose(split[:, r], (0, 1, 3, 2))
    return full.reshape(devices, owned * 2 * degrees, lat_dev * devices * group).astype(BF16)


def params(limit, **kwargs):
    return pltpu.CompilerParams(vmem_limit_bytes=limit * MIB, **kwargs)


def cost(flops, nbytes):
    return pl.CostEstimate(flops=int(flops), bytes_accessed=int(nbytes), transcendentals=0)


def dot(a, b):
    return jnp.dot(a, b, preferred_element_type=F32)


def dot_t(a, b):
    return lax.dot_general(a, b, (((0,), (0,)), ((), ())), preferred_element_type=F32)


def in_hbm(array):
    return pltpu.with_memory_space_constraint(array, pltpu.HBM)


def every(*shape):
    return pl.BlockSpec(shape, lambda *g: (0,) * len(shape))


VMEM = pl.BlockSpec(memory_space=pltpu.VMEM)
SMEM = pl.BlockSpec(memory_space=pltpu.SMEM)
ANYWHERE = pl.BlockSpec(memory_space=pl.ANY)


def transform(position, features, table, rows, cols, basis):
    lat_dev, lon, channels = features.shape
    depth = table.shape[0]
    kernels, _, taps = basis.shape
    edges = (0, lat_dev - 1)

    def body(p_ref, x_ref, t_ref, row_ref, col_ref, basis_ref, o_ref, first_ref, last_ref, *rest):
        edge_refs = (first_ref, last_ref)
        held, table_held, wide, meta, sem, edge_sem, small_sem = rest[:7]
        small_held = rest[7:]
        table_copy = pltpu.make_async_copy(t_ref, table_held, small_sem.at[3])
        copies = [
            pltpu.make_async_copy(x_ref.at[i], held.at[i], sem.at[i]) for i in range(lat_dev)
        ]
        small_copies = [
            pltpu.make_async_copy(ref, to, small_sem.at[n])
            for n, (ref, to) in enumerate(zip((row_ref, col_ref, basis_ref), small_held, strict=True))
        ]
        order = edges + tuple(i for i in range(lat_dev) if i not in edges)
        for copy in [*small_copies, table_copy, *(copies[i] for i in order)]:
            copy.start()
        for copy in small_copies:
            copy.wait()
        rows_held, cols_held, basis_held = small_held
        sent = []
        for n, edge in enumerate(edges):
            wide[...] = jnp.zeros_like(wide)
            own = rows_held[edge : edge + 1, :] - (p_ref[0] * lat_dev + edge)
            wide[0:1, 0:taps] = own.astype(F32)
            wide[1:2, 0:taps] = cols_held[edge : edge + 1, :].astype(F32)
            for k in range(kernels):
                wide[2 + k : 3 + k, 0:taps] = basis_held[k, edge : edge + 1, :].astype(F32)
            meta[n] = wide[...].astype(BF16)
        far = lax.rem(p_ref[0], 2)
        near = 1 - far
        for e, away in enumerate((near, far)):
            sent.append(
                pltpu.make_async_copy(
                    meta.at[away], edge_refs[e].at[pl.ds(lon, META)], edge_sem.at[e, 1]
                )
            )
            sent[-1].start()
        table_copy.wait()
        for n, i in enumerate(order):
            copies[i].wait()
            if n == 1:
                for e, away in enumerate((near, far)):
                    sent.append(
                        pltpu.make_async_copy(
                            held.at[away * (lat_dev - 1)],
                            edge_refs[e].at[pl.ds(0, lon)],
                            edge_sem.at[e, 0],
                        )
                    )
                    sent[-1].start()
            o_ref[:, i * channels : (i + 1) * channels] = dot(table_held[...], held[i]).astype(BF16)
        for copy in sent:
            copy.wait()

    return pl.pallas_call(
        body,
        in_specs=[SMEM] + [ANYWHERE] * 5,
        out_specs=[VMEM, ANYWHERE, ANYWHERE],
        out_shape=[
            pltpu.HBM((depth, lat_dev * channels), BF16),
            pltpu.HBM((lon + META, channels), BF16),
            pltpu.HBM((lon + META, channels), BF16),
        ],
        scratch_shapes=[
            pltpu.VMEM((lat_dev, lon, channels), BF16),
            pltpu.VMEM(table.shape, BF16),
            pltpu.VMEM((META, channels), F32),
            pltpu.VMEM((2, META, channels), BF16),
            pltpu.SemaphoreType.DMA((lat_dev,)),
            pltpu.SemaphoreType.DMA((2, 2)),
            pltpu.SemaphoreType.DMA((4,)),
            pltpu.VMEM(rows.shape, rows.dtype),
            pltpu.VMEM(cols.shape, cols.dtype),
            pltpu.VMEM(basis.shape, basis.dtype),
        ],
        compiler_params=params(16),
        cost_estimate=cost(2 * depth * lon * channels * lat_dev, features.size * 2),
        name="transform",
    )(
        position,
        in_hbm(features),
        in_hbm(table),
        in_hbm(rows),
        in_hbm(cols),
        in_hbm(basis),
    )


def filtered(order, middle, near, far, shifts, taps, weights, before=None):
    total = order.shape[0] - 1
    lat_dev = shifts.shape[0]
    lon, channels = middle[0].shape[-2:]
    kernels = taps.shape[0]
    count = taps.shape[2]
    wide = kernels * channels
    per = PER
    chunk = per * STEP
    keep = weights is None
    beyond = [array for array in (near, far) if array is not None]

    def body(order_ref, shift_ref, tap_ref, *rest):
        rest = list(rest)
        mid_refs = [rest.pop(0) for _ in middle]
        beyond_refs = [rest.pop(0) for _ in beyond]
        w_ref = None if keep else rest.pop(0)
        if before is not None:
            rest.pop(0)
        out_ref, ext, sem, held, out_sem = rest[:5]
        mixed_ref = None if keep else rest[5]
        step_id = pl.program_id(0)
        odd = order_ref[0]
        row = order_ref[1 + step_id]

        sources = []
        if len(middle) == 1:
            sources += [(mid_refs[0].at[i], i + 1) for i in range(1, lat_dev - 1)]
            if far is None:
                i = (1 - odd) * (lat_dev - 1)
                sources.append((mid_refs[0].at[i], i + 1))
            if near is None:
                i = odd * (lat_dev - 1)
                sources.append((mid_refs[0].at[i], i + 1))
        else:
            sources += [(mid_refs[i], i + 1) for i in range(1, lat_dev - 1)]
            sources.append((mid_refs[0], 1 + (1 - odd) * (lat_dev - 1)))
            sources.append((mid_refs[-1], 1 + odd * (lat_dev - 1)))
        if near is not None:
            sources.append((beyond_refs[0], (1 - odd) * (lat_dev + 1)))
        if far is not None:
            sources.append((beyond_refs[-1], odd * (lat_dev + 1)))

        def copies(which):
            return [
                pltpu.make_async_copy(
                    src.at[pl.ds(a, size)], ext.at[to, pl.ds(b, size)], sem.at[s, n]
                )
                for s, (src, to) in list(enumerate(sources))[which]
                for n, (a, b, size) in enumerate(
                    ((0, SPAN, lon), (lon - SPAN, 0, SPAN), (0, lon + SPAN, SPAN))
                )
            ]

        late = -1 if far is not None and total > 1 else len(sources)

        def outgoing(g, place):
            size = lon // 2
            return pltpu.make_async_copy(
                held.at[g, pl.ds(place * size, size)],
                out_ref.at[order_ref[1 + g], pl.ds(place * size, size)],
                out_sem.at[g, place],
            )

        @pl.when(step_id == 0)
        def _():
            for copy in copies(slice(None)):
                copy.start()

        across = lax.broadcasted_iota(jnp.int32, (STEP, 3 * WIN), 1)
        down = lax.broadcasted_iota(jnp.int32, (STEP, 3 * WIN), 0)
        delta = across - down
        band = [jnp.zeros((STEP, 3 * WIN), F32) for _ in range(kernels)]
        for t in range(count):
            hit = delta == shift_ref[row, t]
            for k in range(kernels):
                band[k] = band[k] + jnp.where(hit, tap_ref[k, row, t], 0.0)
        band = jnp.concatenate(band, axis=0).astype(BF16)

        @pl.when(step_id == 0)
        def _():
            for copy in copies(slice(None, late)):
                copy.wait()

        if late == -1:

            @pl.when(step_id == total - 1)
            def _():
                for copy in copies(slice(late, None)):
                    copy.wait()

        for c in range(lon // chunk):
            for b in range(per):
                start = c * chunk + b * STEP
                window = jnp.concatenate(
                    [ext[row + e, start : start + WIN, :] for e in range(3)], axis=0
                )
                sums = dot(band, window).astype(BF16)
                for k in range(kernels):
                    part = sums[k * STEP : (k + 1) * STEP]
                    lanes = slice(k * channels, (k + 1) * channels)
                    if keep:
                        held[step_id, start : start + STEP, lanes] = part
                    else:
                        mixed_ref[c % 2, b * STEP : (b + 1) * STEP, lanes] = part
            if not keep:
                held[step_id, c * chunk : (c + 1) * chunk, :] = sum(
                    lax.dot_general(
                        mixed_ref[c % 2, :, k * channels : (k + 1) * channels],
                        w_ref[k * channels : (k + 1) * channels, :],
                        (((1,), (1,)), ((), ())),
                        preferred_element_type=F32,
                    )
                    for k in range(kernels)
                ).astype(BF16)
            if (c + 1) * chunk * 2 % lon == 0:
                outgoing(step_id, (c + 1) * chunk * 2 // lon - 1).start()

        @pl.when(step_id == total - 1)
        def _():
            for g in range(total):
                for place in range(2):
                    outgoing(g, place).wait()

    depth = wide if keep else channels
    operands = [order, shifts, taps, *(in_hbm(array) for array in middle), *beyond]
    in_specs = [SMEM, SMEM] + [ANYWHERE] * (len(middle) + len(beyond))
    scratch = [
        pltpu.VMEM((lat_dev + 2, lon + 2 * SPAN, channels), BF16),
        pltpu.SemaphoreType.DMA((lat_dev + 2, 3)),
        pltpu.VMEM((total, lon, depth), BF16),
        pltpu.SemaphoreType.DMA((total, 2)),
    ]
    if not keep:
        operands.append(in_hbm(weights))
        in_specs.append(every(wide, channels))
        scratch.append(pltpu.VMEM((2, chunk, wide), BF16))
    aliases = {}
    if before is not None:
        aliases[len(operands)] = 0
        operands.append(before)
        in_specs.append(ANYWHERE)
    return pl.pallas_call(
        body,
        grid=(total,),
        in_specs=[SMEM] + in_specs,
        out_specs=ANYWHERE,
        scratch_shapes=scratch,
        out_shape=pltpu.HBM((lat_dev, lon, depth), BF16),
        input_output_aliases=aliases,
        compiler_params=params(24),
        cost_estimate=cost(
            2 * total * lon * channels * (wide * (0 if keep else 1) + 3 * WIN * kernels),
            total * lon * channels * 8,
        ),
        name="filtered" if keep else "filtered_back",
    )(*operands)


def blocks_of(ref, start, rows, lanes):
    block = ref[:, start : start + rows, lanes].astype(F32)
    return block.reshape(block.shape[0] * rows, block.shape[2]).astype(BF16)


def spectral_forward(position, owned, table_in, table_out, gain):
    group_rows, width = owned.shape
    _, rows, depth = table_in.shape
    degrees, channels = gain.shape
    lat_dev = width // channels

    def body(p_ref, x_ref, a_ref, b_ref, g_ref, analysed_ref, o_ref):
        analysed = jnp.zeros((rows, channels), F32)
        for i in range(lat_dev):
            analysed = analysed + dot(
                a_ref[0, :, i * group_rows : (i + 1) * group_rows],
                x_ref[:, i * channels : (i + 1) * channels],
            )
        analysed_ref[...] = analysed
        gain_rows = jnp.concatenate([g_ref[...]] * (rows // degrees), axis=0)
        scaled = (analysed * gain_rows).astype(BF16)
        for i in range(lat_dev):
            o_ref[:, i * channels : (i + 1) * channels] = dot_t(
                b_ref[0, :, i * group_rows : (i + 1) * group_rows], scaled
            ).astype(BF16)

    table_spec = pl.BlockSpec((1, rows, depth), lambda g, p: (p[0], 0, 0))
    return pl.pallas_call(
        body,
        grid_spec=pltpu.PrefetchScalarGridSpec(
            num_scalar_prefetch=1,
            grid=(1,),
            in_specs=[
                pl.BlockSpec((group_rows, width), lambda g, p: (0, 0)),
                table_spec,
                table_spec,
                pl.BlockSpec((degrees, channels), lambda g, p: (0, 0)),
            ],
            out_specs=[
                pl.BlockSpec((rows, channels), lambda g, p: (0, 0)),
                pl.BlockSpec((group_rows, width), lambda g, p: (0, 0)),
            ],
        ),
        out_shape=[
            pltpu.HBM((rows, channels), F32),
            pltpu.HBM((group_rows, width), BF16),
        ],
        compiler_params=params(16),
        name="spectral_forward",
    )(position, owned, in_hbm(table_in), in_hbm(table_out), in_hbm(gain))


def spectral_adjoint(position, received, table_in, table_out, gain, analysed, terms):
    devices, block_rows, width = received.shape
    group = block_rows - terms
    group_rows = devices * group
    _, rows, depth = table_in.shape
    degrees, channels = gain.shape
    lat_dev = width // channels

    def body(p_ref, x_ref, b_ref, a_ref, g_ref, analysed_ref, gain_ref, o_ref):
        summed = jnp.sum(x_ref[:, 0:terms, :].astype(F32), axis=0).astype(BF16)
        for d in range(devices):
            o_ref[d, 0:terms, :] = summed
        scaled = jnp.zeros((rows, channels), F32)
        for i in range(lat_dev):
            scaled = scaled + dot(
                b_ref[0, :, i * group_rows : (i + 1) * group_rows],
                blocks_of(x_ref, terms, group, slice(i * channels, (i + 1) * channels)),
            )
        products = analysed_ref[...] * scaled
        total = jnp.zeros((degrees, channels), F32)
        for s in range(rows // degrees):
            total = total + products[s * degrees : (s + 1) * degrees]
        gain_ref[...] = total
        gain_rows = jnp.concatenate([g_ref[...]] * (rows // degrees), axis=0)
        grad = (gain_rows * scaled).astype(BF16)
        for i in range(lat_dev):
            part = dot_t(a_ref[0, :, i * group_rows : (i + 1) * group_rows], grad)
            o_ref[:, terms:block_rows, i * channels : (i + 1) * channels] = part.reshape(
                devices, group, channels
            ).astype(BF16)

    table_spec = pl.BlockSpec((1, rows, depth), lambda g, p: (p[0], 0, 0))
    return pl.pallas_call(
        body,
        grid_spec=pltpu.PrefetchScalarGridSpec(
            num_scalar_prefetch=1,
            grid=(1,),
            in_specs=[
                pl.BlockSpec((devices, block_rows, width), lambda g, p: (0, 0, 0)),
                table_spec,
                table_spec,
                pl.BlockSpec((degrees, channels), lambda g, p: (0, 0)),
                pl.BlockSpec((rows, channels), lambda g, p: (0, 0)),
            ],
            out_specs=[
                pl.BlockSpec((degrees, channels), lambda g, p: (0, 0)),
                pl.BlockSpec((devices, block_rows, width), lambda g, p: (0, 0, 0)),
            ],
        ),
        out_shape=[
            jax.ShapeDtypeStruct((degrees, channels), F32),
            pltpu.HBM((devices, block_rows, width), BF16),
        ],
        compiler_params=params(16),
        name="spectral_adjoint",
    )(
        position,
        received,
        in_hbm(table_in),
        in_hbm(table_out),
        in_hbm(gain),
        in_hbm(analysed),
    )


def activation(position, mixed, weights, returned, grad_output, inverse, inverse_t, devices, terms):
    lat_dev, lon, wide = mixed.shape
    channels = grad_output.shape[2]
    group_rows = returned.shape[0]
    group = group_rows // devices
    chunk = CHUNK
    piece = wide // devices // lat_dev

    def body(p_ref, m_ref, w_ref, y_ref, g_ref, inv_ref, invt_ref, *rest):
        o_ref, row_refs = rest[0], rest[1 : 1 + lat_dev]
        rest = rest[1 + lat_dev :]
        acc, held, sem = rest[-3:]
        row = pl.program_id(0)
        gt_ref = held.at[row]
        for c in range(lon // chunk):
            place = slice(c * chunk, (c + 1) * chunk)
            total = dot(m_ref[0, place, :], w_ref[...]) + dot(inv_ref[place, :], y_ref[...])
            square = total * total
            half = 0.5 + 0.5 * jnp.tanh(total * (ROOT + ROOT * CUBE * square))
            value = total * half
            slope = half + value * (1.0 - half) * (2.0 * ROOT + 6.0 * ROOT * CUBE * square)
            o_ref[0, place, :] = value.astype(BF16)
            gt_ref[place, :] = (g_ref[0, place, :].astype(F32) * slope).astype(BF16)
        odd = lax.rem(p_ref[0], 2)
        for i in range(lat_dev):
            for side in range(2):
                to = i if side == 1 else lat_dev - 1 - i

                @pl.when((row == i) & (odd == side))
                def _(i=i, to=to):
                    pltpu.make_async_copy(held.at[i], row_refs[to], sem.at[i]).start()

        spectrum = dot(invt_ref[...], gt_ref[...])
        part = dot(jnp.transpose(gt_ref[...]), m_ref[0])

        @pl.when(row == lat_dev - 1)
        def _():
            for i in range(lat_dev - 1):
                pltpu.make_async_copy(held.at[i], row_refs[i], sem.at[i]).wait()

        @pl.when(row == 0)
        def _():
            acc[...] = part

        @pl.when(row > 0)
        def _():
            acc[...] += part

        if not terms:
            x_ref, weight_ref = rest[0:2]
            x_ref[...] = spectrum.astype(BF16)

            @pl.when(row == lat_dev - 1)
            def _():
                weight_ref[...] = jnp.transpose(acc[...]).astype(BF16)
                pltpu.make_async_copy(held.at[row], row_refs[-1], sem.at[row]).wait()

            return
        x_ref = rest[0]
        spectrum = spectrum.reshape(devices, group, channels).astype(BF16)
        for i in range(lat_dev):

            @pl.when(row == i)
            def _(i=i):
                x_ref[:, terms : terms + group, i * channels : (i + 1) * channels] = spectrum

        @pl.when(row == lat_dev - 1)
        def _():
            weight = jnp.transpose(acc[...]).astype(BF16)
            for d in range(devices):
                for i in range(lat_dev):
                    at = (d * lat_dev + i) * piece
                    x_ref[d, 0:piece, i * channels : (i + 1) * channels] = weight[at : at + piece]
            pltpu.make_async_copy(held.at[row], row_refs[-1], sem.at[row]).wait()

    row_spec = pl.BlockSpec((1, lon, channels), lambda i: (i, 0, 0))
    column_spec = pl.BlockSpec((group_rows, channels), lambda i: (0, i))
    if terms:
        last_specs = [pl.BlockSpec((devices, terms + group, lat_dev * channels), lambda i: (0, 0, 0))]
        last_shapes = [pltpu.HBM((devices, terms + group, lat_dev * channels), BF16)]
    else:
        last_specs = [column_spec, pl.BlockSpec((wide, channels), lambda i: (0, 0))]
        last_shapes = [
            jax.ShapeDtypeStruct((group_rows, lat_dev * channels), BF16),
            jax.ShapeDtypeStruct((wide, channels), BF16),
        ]
    return pl.pallas_call(
        body,
        grid=(lat_dev,),
        in_specs=[
            SMEM,
            pl.BlockSpec((1, lon, wide), lambda i: (i, 0, 0)),
            every(wide, channels),
            column_spec,
            row_spec,
            every(lon, group_rows),
            every(group_rows, lon),
        ],
        out_specs=[row_spec] + [ANYWHERE] * lat_dev + last_specs,
        out_shape=[
            pltpu.HBM((lat_dev, lon, channels), BF16),
        ]
        + [pltpu.HBM((lon, channels), BF16)] * lat_dev
        + last_shapes,
        scratch_shapes=[
            pltpu.VMEM((channels, wide), F32),
            pltpu.VMEM((lat_dev, lon, channels), BF16),
            pltpu.SemaphoreType.DMA((lat_dev,)),
        ],
        compiler_params=params(40),
        cost_estimate=cost(
            4 * grad_output.size * (group_rows + wide), grad_output.size * 14
        ),
        name="activation",
    )(
        position,
        in_hbm(mixed),
        in_hbm(weights),
        returned,
        in_hbm(grad_output),
        in_hbm(inverse),
        in_hbm(inverse_t),
    )


def final(received, forward, grad_disco, terms):
    lat_dev, lon, channels = grad_disco.shape
    depth = forward.shape[1]

    def body(y_ref, f_ref, d_ref, o_ref, *rest):
        w_ref = rest[0] if terms else None
        f_held, d_held, o_held, f_sem, d_sem, o_sem = rest[-7:-1]
        w_held = rest[-1]
        table = pltpu.make_async_copy(f_ref, f_held, f_sem)
        incoming = [
            pltpu.make_async_copy(d_ref.at[i], d_held.at[i], d_sem.at[i]) for i in range(lat_dev)
        ]
        outgoing = [
            pltpu.make_async_copy(o_held.at[i], o_ref.at[i], o_sem.at[i]) for i in range(lat_dev)
        ]
        table.start()
        for copy in incoming:
            copy.start()
        if terms:
            for i in range(lat_dev):
                w_held[:, i] = y_ref[:, 0:terms, i * channels : (i + 1) * channels].astype(F32)
            outgoing.append(pltpu.make_async_copy(w_held, w_ref, o_sem.at[lat_dev]))
            outgoing[-1].start()
        table.wait()
        for i in range(lat_dev):
            lanes = slice(i * channels, (i + 1) * channels)
            if terms:
                bands = blocks_of(y_ref, terms, y_ref.shape[1] - terms, lanes)
            else:
                bands = y_ref[:, lanes]
            incoming[i].wait()
            for c in range(lon // CHUNK):
                place = slice(c * CHUNK, (c + 1) * CHUNK)
                o_held[i, place, :] = (
                    d_held[i, place, :].astype(F32) + dot(f_held[place, :], bands)
                ).astype(BF16)
            outgoing[i].start()
        for copy in outgoing:
            copy.wait()

    out_shape = [pltpu.HBM((lat_dev, lon, channels), BF16)]
    gathered = (16, 128)
    if terms:
        gathered = (received.shape[0], lat_dev, terms, channels)
        out_shape.append(pltpu.HBM(gathered, F32))
    return pl.pallas_call(
        body,
        in_specs=[VMEM, ANYWHERE, ANYWHERE],
        out_specs=[ANYWHERE] * len(out_shape),
        out_shape=out_shape,
        scratch_shapes=[
            pltpu.VMEM((lon, depth), BF16),
            pltpu.VMEM((lat_dev, lon, channels), BF16),
            pltpu.VMEM((lat_dev, lon, channels), BF16),
            pltpu.SemaphoreType.DMA,
            pltpu.SemaphoreType.DMA((lat_dev,)),
            pltpu.SemaphoreType.DMA((lat_dev + 1,)),
            pltpu.VMEM(gathered, F32),
        ],
        compiler_params=params(24),
        cost_estimate=cost(2 * grad_disco.size * depth, grad_disco.size * 6),
        name="final",
    )(received, in_hbm(forward), in_hbm(grad_disco))


def stages(count):
    found = []
    stride = 1
    while stride < count:
        factor = 4 if (count // stride) % 4 == 0 else 2
        found.append((stride, factor))
        stride *= factor
    return found


def partner(array, count, stride, by):
    return lax.ppermute(array, "lat", [(i, i ^ (by * stride)) for i in range(count)])


def sum_scatter_gather(array):
    count = lax.axis_size("lat")
    position = lax.axis_index("lat")
    plan = stages(count)
    for stride, factor in plan:
        digit = (position // stride) % factor
        pieces = array.reshape(factor, array.shape[0] // factor, array.shape[1])
        total = lax.dynamic_index_in_dim(pieces, digit, 0, False).astype(F32)
        for by in range(1, factor):
            piece = lax.dynamic_index_in_dim(pieces, digit ^ by, 0, False)
            total = total + partner(piece, count, stride, by).astype(F32)
        array = total.astype(BF16)
    for stride, factor in reversed(plan):
        digit = (position // stride) % factor
        whole = jnp.zeros((factor,) + array.shape, BF16)
        for by in range(factor):
            part = partner(array, count, stride, by) if by else array
            whole = lax.dynamic_update_index_in_dim(whole, part, digit ^ by, 0)
        array = whole.reshape(-1, array.shape[1])
    return array


def sum_everywhere(array, between, then):
    count = lax.axis_size("lat")
    plan = stages(count)
    for n, (stride, factor) in enumerate(plan):
        last = n == len(plan) - 1
        if last:
            array, between = lax.optimization_barrier((array, between))
        parts = [array] + [partner(array, count, stride, by) for by in range(1, factor)]
        if last:
            parts, result = lax.optimization_barrier((parts, then(between)))
        while len(parts) > 1:
            parts = [parts[k] + parts[k + 1] for k in range(0, len(parts), 2)]
        array = parts[0]
    return (array, result)


def paired(near_row, far_row):
    count = lax.axis_size("lat")
    near = lax.ppermute(near_row, "lat", [(i, i ^ 1) for i in range(count)])
    across = [(i, i + 1) for i in range(1, count - 1, 2)]
    far = lax.ppermute(far_row, "lat", across + [(b, a) for a, b in across])
    return (near, far)


def exchange(blocks):
    return lax.all_to_all(blocks, "lat", split_axis=0, concat_axis=0, tiled=True)


def exchange_rows(array):
    count = lax.axis_size("lat")
    rows, width = array.shape
    return exchange(array.reshape(count, rows // count, width)).reshape(rows, width)


def local(features, disco_rows, disco_cols, disco_basis, disco_weight, spectral_gain, grad_output):
    lat_dev, lon, channels = features.shape
    devices = lax.axis_size("lat")
    position = lax.axis_index("lat")
    degrees = spectral_gain.shape[0]
    lat_count = lat_dev * devices
    order_count = lat_count
    owned_orders = order_count // devices
    kernels, _, taps = disco_basis.shape
    wide = kernels * channels
    forward, inverse = fourier_tables(lon, order_count, devices)
    group = forward.shape[1] // devices
    forward_t = jnp.asarray(np.ascontiguousarray(forward.T))
    inverse_t = jnp.asarray(np.ascontiguousarray(inverse.T))
    forward = jnp.asarray(forward)
    inverse = jnp.asarray(inverse)
    place = position.astype(jnp.int32).reshape(1)
    piece = wide // devices // lat_dev
    small = (
        order_count * owned_orders * 2 * degrees * lat_dev * devices * group <= TABLE_CAP * 4
        and piece * devices * lat_dev == wide
        and piece % 16 == 0
    )
    terms = piece if small else 0
    inner = tuple(range(1, lat_dev - 1))

    coefficients, near_row, far_row = transform(
        place, features, forward_t, disco_rows, disco_cols, disco_basis
    )
    near, far = paired(near_row, far_row)
    owned = exchange_rows(coefficients)

    band_rows = position * lat_dev + jnp.arange(lat_dev, dtype=jnp.int32)[:, None]
    basis = disco_basis.astype(F32)
    offsets = disco_rows - band_rows
    shifts = (offsets + 1) * WIN + SPAN + disco_cols
    weight_rows = disco_weight.reshape(wide, channels)
    odd = position % 2
    near_id = (1 - odd) * (lat_dev - 1)
    far_id = odd * (lat_dev - 1)

    def order_of(*rows):
        return jnp.stack([odd, *rows]).astype(jnp.int32)

    mixed = filtered(order_of(*inner), [features], None, None, shifts, basis, None)
    owned, mixed = lax.optimization_barrier((owned, mixed))
    mixed = filtered(order_of(near_id), [features], near, None, shifts, basis, None, mixed)
    mixed = filtered(order_of(far_id), [features], None, far, shifts, basis, None, mixed)

    packed = jnp.concatenate(
        [
            offsets.astype(F32)[:, None, :],
            disco_cols.astype(F32)[:, None, :],
            jnp.transpose(basis, (1, 0, 2)),
        ],
        axis=1,
    )
    near_taps = near[None, lon : lon + 2 + kernels, :taps].astype(F32)
    far_taps = far[None, lon : lon + 2 + kernels, :taps].astype(F32)
    packed_all = jnp.concatenate(
        [jnp.where(odd == 1, near_taps, far_taps), packed, jnp.where(odd == 1, far_taps, near_taps)],
        axis=0,
    )
    back_shifts = []
    back_taps = []
    for e in range(3):
        aimed = packed_all[e : e + lat_dev, 0] == 1.0 - e
        columns = packed_all[e : e + lat_dev, 1].astype(jnp.int32)
        back_shifts.append(jnp.where(aimed, e * WIN + SPAN - columns, NONE))
        back_taps.append(jnp.transpose(packed_all[e : e + lat_dev, 2:], (1, 0, 2)))
    back_shifts = jnp.concatenate(back_shifts, axis=1)
    back_taps = jnp.concatenate(back_taps, axis=2)

    if small:
        plain, weighted = legendre_table(order_count, degrees, lat_count)
        plain = jnp.asarray(spectral_table(plain, devices, lat_dev, group))
        weighted = jnp.asarray(spectral_table(weighted, devices, lat_dev, group))
        analysed, synthesized = spectral_forward(place, owned, weighted, plain, spectral_gain)
    else:
        _, gauss_weights = gauss_grid(lat_count)
        orders = position * owned_orders + jnp.arange(owned_orders, dtype=jnp.int32)
        legendre = legendre_block(orders, order_count, degrees, lat_count)
        plain = legendre.astype(BF16).reshape(owned_orders, degrees, devices, lat_dev)
        weighted = (legendre * jnp.asarray(gauss_weights, F32)[None, None, :]).astype(BF16)
        weighted = weighted.reshape(owned_orders, degrees, devices, lat_dev)

        def opened(array):
            array = array.reshape(devices, group, lat_dev, channels)[:, : 2 * owned_orders]
            return array.reshape(devices, owned_orders, 2, lat_dev, channels)

        def closed(array):
            array = array.reshape(devices, 2 * owned_orders, lat_dev * channels)
            array = jnp.pad(array, ((0, 0), (0, group - 2 * owned_orders), (0, 0)))
            return array.reshape(devices * group, lat_dev * channels).astype(BF16)

        analysed = jnp.einsum(
            "rlsi,srpic->rplc", weighted, opened(owned), preferred_element_type=F32
        )
        scaled = (analysed * spectral_gain).astype(BF16)
        synthesized = closed(
            jnp.einsum("rlsi,rplc->srpic", plain, scaled, preferred_element_type=F32)
        )

    returned = exchange_rows(synthesized)
    output, *blocks = activation(
        place, mixed, weight_rows, returned, grad_output, inverse, inverse_t, devices, terms
    )
    grad_rows, blocks = blocks[:lat_dev], blocks[lat_dev:]
    grad_near, grad_far = paired(grad_rows[0], grad_rows[-1])
    part = filtered(
        order_of(*inner), grad_rows, None, None, back_shifts, back_taps, weight_rows
    )
    if small:
        grad_owned, part = lax.optimization_barrier((exchange(blocks[0]), part))
        gain_part, grad_blocks = spectral_adjoint(
            place, grad_owned, plain, weighted, spectral_gain, analysed, terms
        )
        grad_bands = exchange(grad_blocks)
    else:
        grad_owned = exchange_rows(blocks[0])
        grad_scaled = jnp.einsum(
            "rlsi,srpic->rplc", plain, opened(grad_owned), preferred_element_type=F32
        )
        gain_part = jnp.sum(analysed * grad_scaled, axis=(0, 1))
        grad_analysed = (grad_scaled * spectral_gain).astype(BF16)
        grad_coeff = closed(
            jnp.einsum("rlsi,rplc->srpic", weighted, grad_analysed, preferred_element_type=F32)
        )
        grad_bands = exchange_rows(grad_coeff)

    grad_disco = filtered(
        order_of(near_id, far_id),
        grad_rows,
        grad_near,
        grad_far,
        back_shifts,
        back_taps,
        weight_rows,
        part,
    )
    grad_gain, (grad_features, *grad_weight) = sum_everywhere(
        gain_part, grad_disco, lambda held: final(grad_bands, forward, held, terms)
    )
    if not small:
        grad_weight = [sum_scatter_gather(blocks[1]).astype(F32)]
    return (
        output,
        grad_features,
        grad_weight[0].reshape(kernels, channels, channels),
        grad_gain,
    )


def solution(mesh):
    return jax.shard_map(
        local,
        mesh=mesh,
        in_specs=(
            P(("group", "lat"), None, None),
            P("lat", None),
            P("lat", None),
            P(None, "lat", None),
            P(),
            P(),
            P(("group", "lat"), None, None),
        ),
        out_specs=(
            P(("group", "lat"), None, None),
            P(("group", "lat"), None, None),
            P("group", None, None),
            P("group", None),
        ),
        check_vma=False,
    )
```

```python
import math

import jax
import jax.numpy as jnp
import numpy as np
from jax import lax
from jax.experimental import pallas as pl
from jax.experimental.pallas import tpu as pltpu
from jax.sharding import PartitionSpec as P

HALO = 1
SPAN = 16
STEP = 48
WIN = STEP + 2 * SPAN
GROUP = 8
NONE = -4096
META = 16
PER = 5
CHUNK = 240
ROOT = math.sqrt(2.0 / math.pi)
CUBE = 0.044715
F32 = jnp.float32
BF16 = jnp.bfloat16
MIB = 1 << 20
TABLE_CAP = 1 << 22


def legendre_pair(nodes, lat_count):
    before = nodes * 0.0 + 1.0
    current = nodes * 1.0
    for degree in range(2, lat_count + 1):
        following = ((2.0 * degree - 1.0) * nodes * current - (degree - 1.0) * before) / degree
        before = current
        current = following
    return (before, current)


def gauss_grid(lat_count):
    counter = np.arange(1, lat_count + 1) * 1.0
    nodes = np.cos(np.pi * (counter - 0.25) / (lat_count + 0.5))
    for sweep in range(12):
        before, current = legendre_pair(nodes, lat_count)
        slope = lat_count * (nodes * current - before) / (nodes * nodes - 1.0)
        nodes = nodes - current / slope
    before, current = legendre_pair(nodes, lat_count)
    slope = lat_count * (nodes * current - before) / (nodes * nodes - 1.0)
    weights = 2.0 / ((1.0 - nodes * nodes) * slope * slope)
    return (nodes, weights)


def diagonal_table(order_count, latitude_nodes):
    sine_values = np.sqrt(1.0 - latitude_nodes * latitude_nodes)
    orders = np.arange(order_count)
    positive = np.arange(1, order_count)
    log_steps = np.concatenate(
        [np.zeros(1), 0.5 * np.cumsum(np.log((2.0 * positive + 1.0) / (2.0 * positive)))]
    )
    log_values = (
        0.5 * np.log(0.5) + log_steps[:, None] + orders[:, None] * np.log(sine_values)[None, :]
    )
    return np.exp(log_values)


def legendre_block(orders, order_count, degrees, lat_count):
    latitude_nodes, weights = gauss_grid(lat_count)
    diagonal_start = jnp.asarray(diagonal_table(order_count, latitude_nodes), jnp.float32)[orders]
    node_row = jnp.asarray(latitude_nodes, jnp.float32)[None, :]
    order_column = orders.astype(jnp.float32)[:, None]

    def block_step(carry, block_index):
        previous, earlier = carry
        produced = []
        for offset in range(16):
            degree = (block_index * 16 + offset).astype(jnp.float32)
            squared = degree * degree
            order_squared = order_column * order_column
            forward_factor = jnp.sqrt(
                jnp.maximum(4.0 * squared - 1.0, 1.0) / jnp.maximum(squared - order_squared, 1.0)
            )
            lower = (degree - 1.0) * (degree - 1.0)
            back_factor = jnp.sqrt(
                jnp.maximum(lower - order_squared, 0.0) / jnp.maximum(4.0 * lower - 1.0, 1.0)
            )
            recurred = forward_factor * (node_row * previous - back_factor * earlier)
            fresh = jnp.where(
                degree < order_column,
                0.0,
                jnp.where(degree == order_column, diagonal_start, recurred),
            )
            earlier = previous
            previous = fresh
            produced.append(fresh)
        return ((previous, earlier), jnp.stack(produced))

    zeros = jnp.zeros((orders.shape[0], lat_count), jnp.float32)
    _, blocks = lax.scan(block_step, (zeros, zeros), jnp.arange(degrees // 16, dtype=jnp.int32))
    legendre = blocks.reshape(degrees, orders.shape[0], lat_count)
    return jnp.transpose(legendre, (1, 0, 2))


def legendre_table(order_count, degrees, lat_count):
    nodes, weights = gauss_grid(lat_count)
    start = diagonal_table(order_count, nodes).astype(np.float32)
    node_row = nodes.astype(np.float32)[None, :]
    order = np.arange(order_count, dtype=np.float32)[:, None]
    one = np.float32(1.0)
    four = np.float32(4.0)
    previous = np.zeros((order_count, lat_count), np.float32)
    earlier = previous
    produced = []
    for step in range(degrees):
        degree = np.float32(step)
        squared = degree * degree
        lower = (degree - one) * (degree - one)
        ahead = np.sqrt(
            np.maximum(four * squared - one, one) / np.maximum(squared - order * order, one)
        )
        back = np.sqrt(
            np.maximum(lower - order * order, np.float32(0.0))
            / np.maximum(four * lower - one, one)
        )
        recurred = ahead * (node_row * previous - back * earlier)
        fresh = np.where(degree < order, np.float32(0.0), np.where(degree == order, start, recurred))
        earlier = previous
        previous = fresh.astype(np.float32)
        produced.append(previous)
    legendre = np.stack(produced, axis=1)
    weighted = legendre * weights.astype(np.float32)[None, None, :]
    return (legendre.astype(BF16), weighted.astype(BF16))


def fourier_tables(lon_count, order_count, devices):
    angle = 2.0 * np.pi / lon_count * (np.outer(np.arange(lon_count), np.arange(order_count)) % lon_count)
    cosine = np.cos(angle)
    sine = np.sin(angle)
    doubled = np.where(np.arange(order_count) == 0, 1.0, 2.0)[None, :]
    owned = order_count // devices
    group = -(-2 * owned // GROUP) * GROUP

    def grouped(real, imaginary):
        pairs = np.stack([real, imaginary], axis=2).reshape(lon_count, devices, 2 * owned)
        pairs = np.pad(pairs, ((0, 0), (0, 0), (0, group - 2 * owned)))
        return pairs.reshape(lon_count, devices * group).astype(np.float32).astype(BF16)

    forward = grouped(cosine / lon_count, -sine / lon_count)
    inverse = grouped(doubled * cosine, -doubled * sine)
    return (forward, inverse)


def spectral_table(table, devices, lat_dev, group):
    orders, degrees, lats = table.shape
    owned = orders // devices
    split = np.asarray(table, np.float32).reshape(devices, owned, degrees, devices, lat_dev)
    full = np.zeros((devices, owned, 2, degrees, lat_dev, devices, group), np.float32)
    for r in range(owned):
        for p in range(2):
            full[:, r, p, :, :, :, 2 * r + p] = np.transpose(split[:, r], (0, 1, 3, 2))
    return full.reshape(devices, owned * 2 * degrees, lat_dev * devices * group).astype(BF16)


def params(limit, **kwargs):
    return pltpu.CompilerParams(vmem_limit_bytes=limit * MIB, **kwargs)


def cost(flops, nbytes):
    return pl.CostEstimate(flops=int(flops), bytes_accessed=int(nbytes), transcendentals=0)


def dot(a, b):
    return jnp.dot(a, b, preferred_element_type=F32)


def dot_t(a, b):
    return lax.dot_general(a, b, (((0,), (0,)), ((), ())), preferred_element_type=F32)


def in_hbm(array):
    return pltpu.with_memory_space_constraint(array, pltpu.HBM)


def every(*shape):
    return pl.BlockSpec(shape, lambda *g: (0,) * len(shape))


VMEM = pl.BlockSpec(memory_space=pltpu.VMEM)
SMEM = pl.BlockSpec(memory_space=pltpu.SMEM)
ANYWHERE = pl.BlockSpec(memory_space=pl.ANY)


def transform(position, features, table, rows, cols, basis):
    lat_dev, lon, channels = features.shape
    depth = table.shape[0]
    kernels, _, taps = basis.shape
    edges = (0, lat_dev - 1)

    def body(p_ref, x_ref, t_ref, row_ref, col_ref, basis_ref, o_ref, first_ref, last_ref, *rest):
        edge_refs = (first_ref, last_ref)
        held, table_held, wide, meta, sem, edge_sem, small_sem = rest[:7]
        small_held = rest[7:]
        table_copy = pltpu.make_async_copy(t_ref, table_held, small_sem.at[3])
        copies = [
            pltpu.make_async_copy(x_ref.at[i], held.at[i], sem.at[i]) for i in range(lat_dev)
        ]
        small_copies = [
            pltpu.make_async_copy(ref, to, small_sem.at[n])
            for n, (ref, to) in enumerate(zip((row_ref, col_ref, basis_ref), small_held, strict=True))
        ]
        order = edges + tuple(i for i in range(lat_dev) if i not in edges)
        for copy in [*small_copies, table_copy, *(copies[i] for i in order)]:
            copy.start()
        for copy in small_copies:
            copy.wait()
        rows_held, cols_held, basis_held = small_held
        sent = []
        for n, edge in enumerate(edges):
            wide[...] = jnp.zeros_like(wide)
            own = rows_held[edge : edge + 1, :] - (p_ref[0] * lat_dev + edge)
            wide[0:1, 0:taps] = own.astype(F32)
            wide[1:2, 0:taps] = cols_held[edge : edge + 1, :].astype(F32)
            for k in range(kernels):
                wide[2 + k : 3 + k, 0:taps] = basis_held[k, edge : edge + 1, :].astype(F32)
            meta[n] = wide[...].astype(BF16)
        far = lax.rem(p_ref[0], 2)
        near = 1 - far
        for e, away in enumerate((near, far)):
            sent.append(
                pltpu.make_async_copy(
                    meta.at[away], edge_refs[e].at[pl.ds(lon, META)], edge_sem.at[e, 1]
                )
            )
            sent[-1].start()
        table_copy.wait()
        for n, i in enumerate(order):
            copies[i].wait()
            if n == 1:
                for e, away in enumerate((near, far)):
                    sent.append(
                        pltpu.make_async_copy(
                            held.at[away * (lat_dev - 1)],
                            edge_refs[e].at[pl.ds(0, lon)],
                            edge_sem.at[e, 0],
                        )
                    )
                    sent[-1].start()
            o_ref[:, i * channels : (i + 1) * channels] = dot(table_held[...], held[i]).astype(BF16)
        for copy in sent:
            copy.wait()

    return pl.pallas_call(
        body,
        in_specs=[SMEM] + [ANYWHERE] * 5,
        out_specs=[VMEM, ANYWHERE, ANYWHERE],
        out_shape=[
            pltpu.HBM((depth, lat_dev * channels), BF16),
            pltpu.HBM((lon + META, channels), BF16),
            pltpu.HBM((lon + META, channels), BF16),
        ],
        scratch_shapes=[
            pltpu.VMEM((lat_dev, lon, channels), BF16),
            pltpu.VMEM(table.shape, BF16),
            pltpu.VMEM((META, channels), F32),
            pltpu.VMEM((2, META, channels), BF16),
            pltpu.SemaphoreType.DMA((lat_dev,)),
            pltpu.SemaphoreType.DMA((2, 2)),
            pltpu.SemaphoreType.DMA((4,)),
            pltpu.VMEM(rows.shape, rows.dtype),
            pltpu.VMEM(cols.shape, cols.dtype),
            pltpu.VMEM(basis.shape, basis.dtype),
        ],
        compiler_params=params(16),
        cost_estimate=cost(2 * depth * lon * channels * lat_dev, features.size * 2),
        name="transform",
    )(
        position,
        in_hbm(features),
        in_hbm(table),
        in_hbm(rows),
        in_hbm(cols),
        in_hbm(basis),
    )


def filtered(order, middle, near, far, shifts, taps, weights, before=None):
    total = order.shape[0] - 1
    lat_dev = shifts.shape[0]
    lon, channels = middle[0].shape[-2:]
    kernels = taps.shape[0]
    count = taps.shape[2]
    wide = kernels * channels
    per = PER
    chunk = per * STEP
    keep = weights is None
    beyond = [array for array in (near, far) if array is not None]

    def body(order_ref, shift_ref, tap_ref, *rest):
        rest = list(rest)
        mid_refs = [rest.pop(0) for _ in middle]
        beyond_refs = [rest.pop(0) for _ in beyond]
        w_ref = None if keep else rest.pop(0)
        if before is not None:
            rest.pop(0)
        out_ref, ext, sem, held, out_sem = rest[:5]
        mixed_ref = None if keep else rest[5]
        step_id = pl.program_id(0)
        odd = order_ref[0]
        row = order_ref[1 + step_id]

        sources = []
        if len(middle) == 1:
            sources += [(mid_refs[0].at[i], i + 1) for i in range(1, lat_dev - 1)]
            if far is None:
                i = (1 - odd) * (lat_dev - 1)
                sources.append((mid_refs[0].at[i], i + 1))
            if near is None:
                i = odd * (lat_dev - 1)
                sources.append((mid_refs[0].at[i], i + 1))
        else:
            sources += [(mid_refs[i], i + 1) for i in range(1, lat_dev - 1)]
            sources.append((mid_refs[0], 1 + (1 - odd) * (lat_dev - 1)))
            sources.append((mid_refs[-1], 1 + odd * (lat_dev - 1)))
        if near is not None:
            sources.append((beyond_refs[0], (1 - odd) * (lat_dev + 1)))
        if far is not None:
            sources.append((beyond_refs[-1], odd * (lat_dev + 1)))

        def copies(which):
            return [
                pltpu.make_async_copy(
                    src.at[pl.ds(a, size)], ext.at[to, pl.ds(b, size)], sem.at[s, n]
                )
                for s, (src, to) in list(enumerate(sources))[which]
                for n, (a, b, size) in enumerate(
                    ((0, SPAN, lon), (lon - SPAN, 0, SPAN), (0, lon + SPAN, SPAN))
                )
            ]

        late = -1 if far is not None and total > 1 else len(sources)

        def outgoing(g, place):
            size = lon // 2
            return pltpu.make_async_copy(
                held.at[g, pl.ds(place * size, size)],
                out_ref.at[order_ref[1 + g], pl.ds(place * size, size)],
                out_sem.at[g, place],
            )

        @pl.when(step_id == 0)
        def _():
            for copy in copies(slice(None)):
                copy.start()

        across = lax.broadcasted_iota(jnp.int32, (STEP, 3 * WIN), 1)
        down = lax.broadcasted_iota(jnp.int32, (STEP, 3 * WIN), 0)
        delta = across - down
        band = [jnp.zeros((STEP, 3 * WIN), F32) for _ in range(kernels)]
        for t in range(count):
            hit = delta == shift_ref[row, t]
            for k in range(kernels):
                band[k] = band[k] + jnp.where(hit, tap_ref[k, row, t], 0.0)
        band = jnp.concatenate(band, axis=0).astype(BF16)

        @pl.when(step_id == 0)
        def _():
            for copy in copies(slice(None, late)):
                copy.wait()

        if late == -1:

            @pl.when(step_id == total - 1)
            def _():
                for copy in copies(slice(late, None)):
                    copy.wait()

        for c in range(lon // chunk):
            for b in range(per):
                start = c * chunk + b * STEP
                window = jnp.concatenate(
                    [ext[row + e, start : start + WIN, :] for e in range(3)], axis=0
                )
                sums = dot(band, window).astype(BF16)
                for k in range(kernels):
                    part = sums[k * STEP : (k + 1) * STEP]
                    lanes = slice(k * channels, (k + 1) * channels)
                    if keep:
                        held[step_id, start : start + STEP, lanes] = part
                    else:
                        mixed_ref[c % 2, b * STEP : (b + 1) * STEP, lanes] = part
            if not keep:
                held[step_id, c * chunk : (c + 1) * chunk, :] = sum(
                    lax.dot_general(
                        mixed_ref[c % 2, :, k * channels : (k + 1) * channels],
                        w_ref[k * channels : (k + 1) * channels, :],
                        (((1,), (1,)), ((), ())),
                        preferred_element_type=F32,
                    )
                    for k in range(kernels)
                ).astype(BF16)
            if (c + 1) * chunk * 2 % lon == 0:
                outgoing(step_id, (c + 1) * chunk * 2 // lon - 1).start()

        @pl.when(step_id == total - 1)
        def _():
            for g in range(total):
                for place in range(2):
                    outgoing(g, place).wait()

    depth = wide if keep else channels
    operands = [order, shifts, taps, *(in_hbm(array) for array in middle), *beyond]
    in_specs = [SMEM, SMEM] + [ANYWHERE] * (len(middle) + len(beyond))
    scratch = [
        pltpu.VMEM((lat_dev + 2, lon + 2 * SPAN, channels), BF16),
        pltpu.SemaphoreType.DMA((lat_dev + 2, 3)),
        pltpu.VMEM((total, lon, depth), BF16),
        pltpu.SemaphoreType.DMA((total, 2)),
    ]
    if not keep:
        operands.append(in_hbm(weights))
        in_specs.append(every(wide, channels))
        scratch.append(pltpu.VMEM((2, chunk, wide), BF16))
    aliases = {}
    if before is not None:
        aliases[len(operands)] = 0
        operands.append(before)
        in_specs.append(ANYWHERE)
    return pl.pallas_call(
        body,
        grid=(total,),
        in_specs=[SMEM] + in_specs,
        out_specs=ANYWHERE,
        scratch_shapes=scratch,
        out_shape=pltpu.HBM((lat_dev, lon, depth), BF16),
        input_output_aliases=aliases,
        compiler_params=params(24),
        cost_estimate=cost(
            2 * total * lon * channels * (wide * (0 if keep else 1) + 3 * WIN * kernels),
            total * lon * channels * 8,
        ),
        name="filtered" if keep else "filtered_back",
    )(*operands)


def blocks_of(ref, start, rows, lanes):
    block = ref[:, start : start + rows, lanes].astype(F32)
    return block.reshape(block.shape[0] * rows, block.shape[2]).astype(BF16)


def spectral_forward(position, owned, table_in, table_out, gain):
    group_rows, width = owned.shape
    _, rows, depth = table_in.shape
    degrees, channels = gain.shape
    lat_dev = width // channels

    def body(p_ref, x_ref, a_ref, b_ref, g_ref, analysed_ref, o_ref):
        analysed = jnp.zeros((rows, channels), F32)
        for i in range(lat_dev):
            analysed = analysed + dot(
                a_ref[0, :, i * group_rows : (i + 1) * group_rows],
                x_ref[:, i * channels : (i + 1) * channels],
            )
        analysed_ref[...] = analysed
        gain_rows = jnp.concatenate([g_ref[...]] * (rows // degrees), axis=0)
        scaled = (analysed * gain_rows).astype(BF16)
        for i in range(lat_dev):
            o_ref[:, i * channels : (i + 1) * channels] = dot_t(
                b_ref[0, :, i * group_rows : (i + 1) * group_rows], scaled
            ).astype(BF16)

    table_spec = pl.BlockSpec((1, rows, depth), lambda g, p: (p[0], 0, 0))
    return pl.pallas_call(
        body,
        grid_spec=pltpu.PrefetchScalarGridSpec(
            num_scalar_prefetch=1,
            grid=(1,),
            in_specs=[
                pl.BlockSpec((group_rows, width), lambda g, p: (0, 0)),
                table_spec,
                table_spec,
                pl.BlockSpec((degrees, channels), lambda g, p: (0, 0)),
            ],
            out_specs=[
                pl.BlockSpec((rows, channels), lambda g, p: (0, 0)),
                pl.BlockSpec((group_rows, width), lambda g, p: (0, 0)),
            ],
        ),
        out_shape=[
            pltpu.HBM((rows, channels), F32),
            pltpu.HBM((group_rows, width), BF16),
        ],
        compiler_params=params(16),
        name="spectral_forward",
    )(position, owned, in_hbm(table_in), in_hbm(table_out), in_hbm(gain))


def spectral_adjoint(position, received, table_in, table_out, gain, analysed, terms):
    devices, block_rows, width = received.shape
    group = block_rows - terms
    group_rows = devices * group
    _, rows, depth = table_in.shape
    degrees, channels = gain.shape
    lat_dev = width // channels

    def body(p_ref, x_ref, b_ref, a_ref, g_ref, analysed_ref, gain_ref, o_ref):
        summed = jnp.sum(x_ref[:, 0:terms, :].astype(F32), axis=0).astype(BF16)
        for d in range(devices):
            o_ref[d, 0:terms, :] = summed
        scaled = jnp.zeros((rows, channels), F32)
        for i in range(lat_dev):
            scaled = scaled + dot(
                b_ref[0, :, i * group_rows : (i + 1) * group_rows],
                blocks_of(x_ref, terms, group, slice(i * channels, (i + 1) * channels)),
            )
        products = analysed_ref[...] * scaled
        total = jnp.zeros((degrees, channels), F32)
        for s in range(rows // degrees):
            total = total + products[s * degrees : (s + 1) * degrees]
        gain_ref[...] = total
        gain_rows = jnp.concatenate([g_ref[...]] * (rows // degrees), axis=0)
        grad = (gain_rows * scaled).astype(BF16)
        for i in range(lat_dev):
            part = dot_t(a_ref[0, :, i * group_rows : (i + 1) * group_rows], grad)
            o_ref[:, terms:block_rows, i * channels : (i + 1) * channels] = part.reshape(
                devices, group, channels
            ).astype(BF16)

    table_spec = pl.BlockSpec((1, rows, depth), lambda g, p: (p[0], 0, 0))
    return pl.pallas_call(
        body,
        grid_spec=pltpu.PrefetchScalarGridSpec(
            num_scalar_prefetch=1,
            grid=(1,),
            in_specs=[
                pl.BlockSpec((devices, block_rows, width), lambda g, p: (0, 0, 0)),
                table_spec,
                table_spec,
                pl.BlockSpec((degrees, channels), lambda g, p: (0, 0)),
                pl.BlockSpec((rows, channels), lambda g, p: (0, 0)),
            ],
            out_specs=[
                pl.BlockSpec((degrees, channels), lambda g, p: (0, 0)),
                pl.BlockSpec((devices, block_rows, width), lambda g, p: (0, 0, 0)),
            ],
        ),
        out_shape=[
            jax.ShapeDtypeStruct((degrees, channels), F32),
            pltpu.HBM((devices, block_rows, width), BF16),
        ],
        compiler_params=params(16),
        name="spectral_adjoint",
    )(
        position,
        received,
        in_hbm(table_in),
        in_hbm(table_out),
        in_hbm(gain),
        in_hbm(analysed),
    )


def activation(position, mixed, weights, returned, grad_output, inverse, inverse_t, devices, terms):
    lat_dev, lon, wide = mixed.shape
    channels = grad_output.shape[2]
    group_rows = returned.shape[0]
    group = group_rows // devices
    chunk = CHUNK
    piece = wide // devices // lat_dev

    def body(p_ref, m_ref, w_ref, y_ref, g_ref, inv_ref, invt_ref, *rest):
        o_ref, row_refs = rest[0], rest[1 : 1 + lat_dev]
        rest = rest[1 + lat_dev :]
        acc, held, sem = rest[-3:]
        row = pl.program_id(0)
        gt_ref = held.at[row]
        for c in range(lon // chunk):
            place = slice(c * chunk, (c + 1) * chunk)
            total = dot(m_ref[0, place, :], w_ref[...]) + dot(inv_ref[place, :], y_ref[...])
            square = total * total
            half = 0.5 + 0.5 * jnp.tanh(total * (ROOT + ROOT * CUBE * square))
            value = total * half
            slope = half + value * (1.0 - half) * (2.0 * ROOT + 6.0 * ROOT * CUBE * square)
            o_ref[0, place, :] = value.astype(BF16)
            gt_ref[place, :] = (g_ref[0, place, :].astype(F32) * slope).astype(BF16)
        odd = lax.rem(p_ref[0], 2)
        for i in range(lat_dev):
            for side in range(2):
                to = i if side == 1 else lat_dev - 1 - i

                @pl.when((row == i) & (odd == side))
                def _(i=i, to=to):
                    pltpu.make_async_copy(held.at[i], row_refs[to], sem.at[i]).start()

        spectrum = dot(invt_ref[...], gt_ref[...])
        part = dot(jnp.transpose(gt_ref[...]), m_ref[0])

        @pl.when(row == lat_dev - 1)
        def _():
            for i in range(lat_dev - 1):
                pltpu.make_async_copy(held.at[i], row_refs[i], sem.at[i]).wait()

        @pl.when(row == 0)
        def _():
            acc[...] = part

        @pl.when(row > 0)
        def _():
            acc[...] += part

        if not terms:
            x_ref, weight_ref = rest[0:2]
            x_ref[...] = spectrum.astype(BF16)

            @pl.when(row == lat_dev - 1)
            def _():
                weight_ref[...] = jnp.transpose(acc[...]).astype(BF16)
                pltpu.make_async_copy(held.at[row], row_refs[-1], sem.at[row]).wait()

            return
        x_ref = rest[0]
        spectrum = spectrum.reshape(devices, group, channels).astype(BF16)
        for i in range(lat_dev):

            @pl.when(row == i)
            def _(i=i):
                x_ref[:, terms : terms + group, i * channels : (i + 1) * channels] = spectrum

        @pl.when(row == lat_dev - 1)
        def _():
            weight = jnp.transpose(acc[...]).astype(BF16)
            for d in range(devices):
                for i in range(lat_dev):
                    at = (d * lat_dev + i) * piece
                    x_ref[d, 0:piece, i * channels : (i + 1) * channels] = weight[at : at + piece]
            pltpu.make_async_copy(held.at[row], row_refs[-1], sem.at[row]).wait()

    row_spec = pl.BlockSpec((1, lon, channels), lambda i: (i, 0, 0))
    column_spec = pl.BlockSpec((group_rows, channels), lambda i: (0, i))
    if terms:
        last_specs = [pl.BlockSpec((devices, terms + group, lat_dev * channels), lambda i: (0, 0, 0))]
        last_shapes = [pltpu.HBM((devices, terms + group, lat_dev * channels), BF16)]
    else:
        last_specs = [column_spec, pl.BlockSpec((wide, channels), lambda i: (0, 0))]
        last_shapes = [
            jax.ShapeDtypeStruct((group_rows, lat_dev * channels), BF16),
            jax.ShapeDtypeStruct((wide, channels), BF16),
        ]
    return pl.pallas_call(
        body,
        grid=(lat_dev,),
        in_specs=[
            SMEM,
            pl.BlockSpec((1, lon, wide), lambda i: (i, 0, 0)),
            every(wide, channels),
            column_spec,
            row_spec,
            every(lon, group_rows),
            every(group_rows, lon),
        ],
        out_specs=[row_spec] + [ANYWHERE] * lat_dev + last_specs,
        out_shape=[
            pltpu.HBM((lat_dev, lon, channels), BF16),
        ]
        + [pltpu.HBM((lon, channels), BF16)] * lat_dev
        + last_shapes,
        scratch_shapes=[
            pltpu.VMEM((channels, wide), F32),
            pltpu.VMEM((lat_dev, lon, channels), BF16),
            pltpu.SemaphoreType.DMA((lat_dev,)),
        ],
        compiler_params=params(40),
        cost_estimate=cost(
            4 * grad_output.size * (group_rows + wide), grad_output.size * 14
        ),
        name="activation",
    )(
        position,
        in_hbm(mixed),
        in_hbm(weights),
        returned,
        in_hbm(grad_output),
        in_hbm(inverse),
        in_hbm(inverse_t),
    )


def final(received, forward, grad_disco, terms):
    lat_dev, lon, channels = grad_disco.shape
    depth = forward.shape[1]

    def body(y_ref, f_ref, d_ref, o_ref, *rest):
        w_ref = rest[0] if terms else None
        f_held, d_held, o_held, f_sem, d_sem, o_sem = rest[-7:-1]
        w_held = rest[-1]
        table = pltpu.make_async_copy(f_ref, f_held, f_sem)
        incoming = [
            pltpu.make_async_copy(d_ref.at[i], d_held.at[i], d_sem.at[i]) for i in range(lat_dev)
        ]
        outgoing = [
            pltpu.make_async_copy(o_held.at[i], o_ref.at[i], o_sem.at[i]) for i in range(lat_dev)
        ]
        table.start()
        for copy in incoming:
            copy.start()
        if terms:
            for i in range(lat_dev):
                w_held[:, i] = y_ref[:, 0:terms, i * channels : (i + 1) * channels].astype(F32)
            outgoing.append(pltpu.make_async_copy(w_held, w_ref, o_sem.at[lat_dev]))
            outgoing[-1].start()
        table.wait()
        for i in range(lat_dev):
            lanes = slice(i * channels, (i + 1) * channels)
            if terms:
                bands = blocks_of(y_ref, terms, y_ref.shape[1] - terms, lanes)
            else:
                bands = y_ref[:, lanes]
            incoming[i].wait()
            for c in range(lon // CHUNK):
                place = slice(c * CHUNK, (c + 1) * CHUNK)
                o_held[i, place, :] = (
                    d_held[i, place, :].astype(F32) + dot(f_held[place, :], bands)
                ).astype(BF16)
            outgoing[i].start()
        for copy in outgoing:
            copy.wait()

    out_shape = [pltpu.HBM((lat_dev, lon, channels), BF16)]
    gathered = (16, 128)
    if terms:
        gathered = (received.shape[0], lat_dev, terms, channels)
        out_shape.append(pltpu.HBM(gathered, F32))
    return pl.pallas_call(
        body,
        in_specs=[VMEM, ANYWHERE, ANYWHERE],
        out_specs=[ANYWHERE] * len(out_shape),
        out_shape=out_shape,
        scratch_shapes=[
            pltpu.VMEM((lon, depth), BF16),
            pltpu.VMEM((lat_dev, lon, channels), BF16),
            pltpu.VMEM((lat_dev, lon, channels), BF16),
            pltpu.SemaphoreType.DMA,
            pltpu.SemaphoreType.DMA((lat_dev,)),
            pltpu.SemaphoreType.DMA((lat_dev + 1,)),
            pltpu.VMEM(gathered, F32),
        ],
        compiler_params=params(24),
        cost_estimate=cost(2 * grad_disco.size * depth, grad_disco.size * 6),
        name="final",
    )(received, in_hbm(forward), in_hbm(grad_disco))


def stages(count):
    found = []
    stride = 1
    while stride < count:
        factor = 4 if (count // stride) % 4 == 0 else 2
        found.append((stride, factor))
        stride *= factor
    return found


def partner(array, count, stride, by):
    return lax.ppermute(array, "lat", [(i, i ^ (by * stride)) for i in range(count)])


def sum_scatter_gather(array):
    count = lax.axis_size("lat")
    position = lax.axis_index("lat")
    plan = stages(count)
    for stride, factor in plan:
        digit = (position // stride) % factor
        pieces = array.reshape(factor, array.shape[0] // factor, array.shape[1])
        total = lax.dynamic_index_in_dim(pieces, digit, 0, False).astype(F32)
        for by in range(1, factor):
            piece = lax.dynamic_index_in_dim(pieces, digit ^ by, 0, False)
            total = total + partner(piece, count, stride, by).astype(F32)
        array = total.astype(BF16)
    for stride, factor in reversed(plan):
        digit = (position // stride) % factor
        whole = jnp.zeros((factor,) + array.shape, BF16)
        for by in range(factor):
            part = partner(array, count, stride, by) if by else array
            whole = lax.dynamic_update_index_in_dim(whole, part, digit ^ by, 0)
        array = whole.reshape(-1, array.shape[1])
    return array


def sum_everywhere(array, between, then):
    count = lax.axis_size("lat")
    plan = stages(count)
    for n, (stride, factor) in enumerate(plan):
        last = n == len(plan) - 1
        if last:
            array, between = lax.optimization_barrier((array, between))
        sent = lax.optimization_barrier(array.astype(BF16))
        parts = [sent] + [partner(sent, count, stride, by) for by in range(1, factor)]
        if last:
            parts, result = lax.optimization_barrier((parts, then(between)))
        parts = [part.astype(F32) for part in parts]
        while len(parts) > 1:
            parts = [parts[k] + parts[k + 1] for k in range(0, len(parts), 2)]
        array = parts[0]
    return (array, result)


def paired(near_row, far_row):
    count = lax.axis_size("lat")
    near = lax.ppermute(near_row, "lat", [(i, i ^ 1) for i in range(count)])
    across = [(i, i + 1) for i in range(1, count - 1, 2)]
    far = lax.ppermute(far_row, "lat", across + [(b, a) for a, b in across])
    return (near, far)


def exchange(blocks):
    return lax.all_to_all(blocks, "lat", split_axis=0, concat_axis=0, tiled=True)


def exchange_rows(array):
    count = lax.axis_size("lat")
    rows, width = array.shape
    return exchange(array.reshape(count, rows // count, width)).reshape(rows, width)


def local(features, disco_rows, disco_cols, disco_basis, disco_weight, spectral_gain, grad_output):
    lat_dev, lon, channels = features.shape
    devices = lax.axis_size("lat")
    position = lax.axis_index("lat")
    degrees = spectral_gain.shape[0]
    lat_count = lat_dev * devices
    order_count = lat_count
    owned_orders = order_count // devices
    kernels, _, taps = disco_basis.shape
    wide = kernels * channels
    forward, inverse = fourier_tables(lon, order_count, devices)
    group = forward.shape[1] // devices
    forward_t = jnp.asarray(np.ascontiguousarray(forward.T))
    inverse_t = jnp.asarray(np.ascontiguousarray(inverse.T))
    forward = jnp.asarray(forward)
    inverse = jnp.asarray(inverse)
    place = position.astype(jnp.int32).reshape(1)
    piece = wide // devices // lat_dev
    small = (
        order_count * owned_orders * 2 * degrees * lat_dev * devices * group <= TABLE_CAP * 4
        and piece * devices * lat_dev == wide
        and piece % 16 == 0
    )
    terms = piece if small else 0
    inner = tuple(range(1, lat_dev - 1))

    coefficients, near_row, far_row = transform(
        place, features, forward_t, disco_rows, disco_cols, disco_basis
    )
    near, far = paired(near_row, far_row)
    owned = exchange_rows(coefficients)

    band_rows = position * lat_dev + jnp.arange(lat_dev, dtype=jnp.int32)[:, None]
    basis = disco_basis.astype(F32)
    offsets = disco_rows - band_rows
    shifts = (offsets + 1) * WIN + SPAN + disco_cols
    weight_rows = disco_weight.reshape(wide, channels)
    odd = position % 2
    near_id = (1 - odd) * (lat_dev - 1)
    far_id = odd * (lat_dev - 1)

    def order_of(*rows):
        return jnp.stack([odd, *rows]).astype(jnp.int32)

    mixed = filtered(order_of(*inner), [features], None, None, shifts, basis, None)
    owned, mixed = lax.optimization_barrier((owned, mixed))
    mixed = filtered(order_of(near_id), [features], near, None, shifts, basis, None, mixed)
    mixed = filtered(order_of(far_id), [features], None, far, shifts, basis, None, mixed)

    packed = jnp.concatenate(
        [
            offsets.astype(F32)[:, None, :],
            disco_cols.astype(F32)[:, None, :],
            jnp.transpose(basis, (1, 0, 2)),
        ],
        axis=1,
    )
    near_taps = near[None, lon : lon + 2 + kernels, :taps].astype(F32)
    far_taps = far[None, lon : lon + 2 + kernels, :taps].astype(F32)
    packed_all = jnp.concatenate(
        [jnp.where(odd == 1, near_taps, far_taps), packed, jnp.where(odd == 1, far_taps, near_taps)],
        axis=0,
    )
    back_shifts = []
    back_taps = []
    for e in range(3):
        aimed = packed_all[e : e + lat_dev, 0] == 1.0 - e
        columns = packed_all[e : e + lat_dev, 1].astype(jnp.int32)
        back_shifts.append(jnp.where(aimed, e * WIN + SPAN - columns, NONE))
        back_taps.append(jnp.transpose(packed_all[e : e + lat_dev, 2:], (1, 0, 2)))
    back_shifts = jnp.concatenate(back_shifts, axis=1)
    back_taps = jnp.concatenate(back_taps, axis=2)

    if small:
        plain, weighted = legendre_table(order_count, degrees, lat_count)
        plain = jnp.asarray(spectral_table(plain, devices, lat_dev, group))
        weighted = jnp.asarray(spectral_table(weighted, devices, lat_dev, group))
        analysed, synthesized = spectral_forward(place, owned, weighted, plain, spectral_gain)
    else:
        _, gauss_weights = gauss_grid(lat_count)
        orders = position * owned_orders + jnp.arange(owned_orders, dtype=jnp.int32)
        legendre = legendre_block(orders, order_count, degrees, lat_count)
        plain = legendre.astype(BF16).reshape(owned_orders, degrees, devices, lat_dev)
        weighted = (legendre * jnp.asarray(gauss_weights, F32)[None, None, :]).astype(BF16)
        weighted = weighted.reshape(owned_orders, degrees, devices, lat_dev)

        def opened(array):
            array = array.reshape(devices, group, lat_dev, channels)[:, : 2 * owned_orders]
            return array.reshape(devices, owned_orders, 2, lat_dev, channels)

        def closed(array):
            array = array.reshape(devices, 2 * owned_orders, lat_dev * channels)
            array = jnp.pad(array, ((0, 0), (0, group - 2 * owned_orders), (0, 0)))
            return array.reshape(devices * group, lat_dev * channels).astype(BF16)

        analysed = jnp.einsum(
            "rlsi,srpic->rplc", weighted, opened(owned), preferred_element_type=F32
        )
        scaled = (analysed * spectral_gain).astype(BF16)
        synthesized = closed(
            jnp.einsum("rlsi,rplc->srpic", plain, scaled, preferred_element_type=F32)
        )

    returned = exchange_rows(synthesized)
    output, *blocks = activation(
        place, mixed, weight_rows, returned, grad_output, inverse, inverse_t, devices, terms
    )
    grad_rows, blocks = blocks[:lat_dev], blocks[lat_dev:]
    grad_near, grad_far = paired(grad_rows[0], grad_rows[-1])
    part = filtered(
        order_of(*inner), grad_rows, None, None, back_shifts, back_taps, weight_rows
    )
    if small:
        grad_owned, part = lax.optimization_barrier((exchange(blocks[0]), part))
        gain_part, grad_blocks = spectral_adjoint(
            place, grad_owned, plain, weighted, spectral_gain, analysed, terms
        )
        grad_bands = exchange(grad_blocks)
    else:
        grad_owned = exchange_rows(blocks[0])
        grad_scaled = jnp.einsum(
            "rlsi,srpic->rplc", plain, opened(grad_owned), preferred_element_type=F32
        )
        gain_part = jnp.sum(analysed * grad_scaled, axis=(0, 1))
        grad_analysed = (grad_scaled * spectral_gain).astype(BF16)
        grad_coeff = closed(
            jnp.einsum("rlsi,rplc->srpic", weighted, grad_analysed, preferred_element_type=F32)
        )
        grad_bands = exchange_rows(grad_coeff)

    grad_disco = filtered(
        order_of(near_id, far_id),
        grad_rows,
        grad_near,
        grad_far,
        back_shifts,
        back_taps,
        weight_rows,
        part,
    )
    grad_gain, (grad_features, *grad_weight) = sum_everywhere(
        gain_part, grad_disco, lambda held: final(grad_bands, forward, held, terms)
    )
    if not small:
        grad_weight = [sum_scatter_gather(blocks[1]).astype(F32)]
    return (
        output,
        grad_features,
        grad_weight[0].reshape(kernels, channels, channels),
        grad_gain,
    )


def solution(mesh):
    return jax.shard_map(
        local,
        mesh=mesh,
        in_specs=(
            P(("group", "lat"), None, None),
            P("lat", None),
            P("lat", None),
            P(None, "lat", None),
            P(),
            P(),
            P(("group", "lat"), None, None),
        ),
        out_specs=(
            P(("group", "lat"), None, None),
            P(("group", "lat"), None, None),
            P("group", None, None),
            P("group", None),
        ),
        check_vma=False,
    )
```

```python
import math

import jax
import jax.numpy as jnp
import numpy as np
from jax import lax
from jax.experimental import pallas as pl
from jax.experimental.pallas import tpu as pltpu
from jax.sharding import PartitionSpec as P

HALO = 1
SPAN = 16
STEP = 48
WIN = STEP + 2 * SPAN
GROUP = 8
NONE = -4096
META = 16
PER = 5
CHUNK = 240
ROOT = math.sqrt(2.0 / math.pi)
CUBE = 0.044715
F32 = jnp.float32
BF16 = jnp.bfloat16
MIB = 1 << 20
TABLE_CAP = 1 << 22


def legendre_pair(nodes, lat_count):
    before = nodes * 0.0 + 1.0
    current = nodes * 1.0
    for degree in range(2, lat_count + 1):
        following = ((2.0 * degree - 1.0) * nodes * current - (degree - 1.0) * before) / degree
        before = current
        current = following
    return (before, current)


def gauss_grid(lat_count):
    counter = np.arange(1, lat_count + 1) * 1.0
    nodes = np.cos(np.pi * (counter - 0.25) / (lat_count + 0.5))
    for sweep in range(12):
        before, current = legendre_pair(nodes, lat_count)
        slope = lat_count * (nodes * current - before) / (nodes * nodes - 1.0)
        nodes = nodes - current / slope
    before, current = legendre_pair(nodes, lat_count)
    slope = lat_count * (nodes * current - before) / (nodes * nodes - 1.0)
    weights = 2.0 / ((1.0 - nodes * nodes) * slope * slope)
    return (nodes, weights)


def diagonal_table(order_count, latitude_nodes):
    sine_values = np.sqrt(1.0 - latitude_nodes * latitude_nodes)
    orders = np.arange(order_count)
    positive = np.arange(1, order_count)
    log_steps = np.concatenate(
        [np.zeros(1), 0.5 * np.cumsum(np.log((2.0 * positive + 1.0) / (2.0 * positive)))]
    )
    log_values = (
        0.5 * np.log(0.5) + log_steps[:, None] + orders[:, None] * np.log(sine_values)[None, :]
    )
    return np.exp(log_values)


def legendre_block(orders, order_count, degrees, lat_count):
    latitude_nodes, weights = gauss_grid(lat_count)
    diagonal_start = jnp.asarray(diagonal_table(order_count, latitude_nodes), jnp.float32)[orders]
    node_row = jnp.asarray(latitude_nodes, jnp.float32)[None, :]
    order_column = orders.astype(jnp.float32)[:, None]

    def block_step(carry, block_index):
        previous, earlier = carry
        produced = []
        for offset in range(16):
            degree = (block_index * 16 + offset).astype(jnp.float32)
            squared = degree * degree
            order_squared = order_column * order_column
            forward_factor = jnp.sqrt(
                jnp.maximum(4.0 * squared - 1.0, 1.0) / jnp.maximum(squared - order_squared, 1.0)
            )
            lower = (degree - 1.0) * (degree - 1.0)
            back_factor = jnp.sqrt(
                jnp.maximum(lower - order_squared, 0.0) / jnp.maximum(4.0 * lower - 1.0, 1.0)
            )
            recurred = forward_factor * (node_row * previous - back_factor * earlier)
            fresh = jnp.where(
                degree < order_column,
                0.0,
                jnp.where(degree == order_column, diagonal_start, recurred),
            )
            earlier = previous
            previous = fresh
            produced.append(fresh)
        return ((previous, earlier), jnp.stack(produced))

    zeros = jnp.zeros((orders.shape[0], lat_count), jnp.float32)
    _, blocks = lax.scan(block_step, (zeros, zeros), jnp.arange(degrees // 16, dtype=jnp.int32))
    legendre = blocks.reshape(degrees, orders.shape[0], lat_count)
    return jnp.transpose(legendre, (1, 0, 2))


def legendre_table(order_count, degrees, lat_count):
    nodes, weights = gauss_grid(lat_count)
    start = diagonal_table(order_count, nodes).astype(np.float32)
    node_row = nodes.astype(np.float32)[None, :]
    order = np.arange(order_count, dtype=np.float32)[:, None]
    one = np.float32(1.0)
    four = np.float32(4.0)
    previous = np.zeros((order_count, lat_count), np.float32)
    earlier = previous
    produced = []
    for step in range(degrees):
        degree = np.float32(step)
        squared = degree * degree
        lower = (degree - one) * (degree - one)
        ahead = np.sqrt(
            np.maximum(four * squared - one, one) / np.maximum(squared - order * order, one)
        )
        back = np.sqrt(
            np.maximum(lower - order * order, np.float32(0.0))
            / np.maximum(four * lower - one, one)
        )
        recurred = ahead * (node_row * previous - back * earlier)
        fresh = np.where(degree < order, np.float32(0.0), np.where(degree == order, start, recurred))
        earlier = previous
        previous = fresh.astype(np.float32)
        produced.append(previous)
    legendre = np.stack(produced, axis=1)
    weighted = legendre * weights.astype(np.float32)[None, None, :]
    return (legendre.astype(BF16), weighted.astype(BF16))


def fourier_tables(lon_count, order_count, devices):
    angle = 2.0 * np.pi / lon_count * (np.outer(np.arange(lon_count), np.arange(order_count)) % lon_count)
    cosine = np.cos(angle)
    sine = np.sin(angle)
    doubled = np.where(np.arange(order_count) == 0, 1.0, 2.0)[None, :]
    owned = order_count // devices
    group = -(-2 * owned // GROUP) * GROUP

    def grouped(real, imaginary):
        pairs = np.stack([real, imaginary], axis=2).reshape(lon_count, devices, 2 * owned)
        pairs = np.pad(pairs, ((0, 0), (0, 0), (0, group - 2 * owned)))
        return pairs.reshape(lon_count, devices * group).astype(np.float32).astype(BF16)

    forward = grouped(cosine / lon_count, -sine / lon_count)
    inverse = grouped(doubled * cosine, -doubled * sine)
    return (forward, inverse)


def spectral_table(table, devices, lat_dev, group):
    orders, degrees, lats = table.shape
    owned = orders // devices
    split = np.asarray(table, np.float32).reshape(devices, owned, degrees, devices, lat_dev)
    full = np.zeros((devices, owned, 2, degrees, lat_dev, devices, group), np.float32)
    for r in range(owned):
        for p in range(2):
            full[:, r, p, :, :, :, 2 * r + p] = np.transpose(split[:, r], (0, 1, 3, 2))
    return full.reshape(devices, owned * 2 * degrees, lat_dev * devices * group).astype(BF16)


def params(limit, **kwargs):
    return pltpu.CompilerParams(vmem_limit_bytes=limit * MIB, **kwargs)


def cost(flops, nbytes):
    return pl.CostEstimate(flops=int(flops), bytes_accessed=int(nbytes), transcendentals=0)


def dot(a, b):
    return jnp.dot(a, b, preferred_element_type=F32)


def dot_t(a, b):
    return lax.dot_general(a, b, (((0,), (0,)), ((), ())), preferred_element_type=F32)


def in_hbm(array):
    return pltpu.with_memory_space_constraint(array, pltpu.HBM)


def every(*shape):
    return pl.BlockSpec(shape, lambda *g: (0,) * len(shape))


VMEM = pl.BlockSpec(memory_space=pltpu.VMEM)
SMEM = pl.BlockSpec(memory_space=pltpu.SMEM)
ANYWHERE = pl.BlockSpec(memory_space=pl.ANY)


def transform(position, features, table, rows, cols, basis):
    lat_dev, lon, channels = features.shape
    depth = table.shape[0]
    kernels, _, taps = basis.shape
    edges = (0, lat_dev - 1)

    def body(p_ref, x_ref, t_ref, row_ref, col_ref, basis_ref, o_ref, first_ref, last_ref, *rest):
        edge_refs = (first_ref, last_ref)
        held, table_held, wide, meta, sem, edge_sem, small_sem = rest[:7]
        small_held = rest[7:]
        table_copy = pltpu.make_async_copy(t_ref, table_held, small_sem.at[3])
        copies = [
            pltpu.make_async_copy(x_ref.at[i], held.at[i], sem.at[i]) for i in range(lat_dev)
        ]
        small_copies = [
            pltpu.make_async_copy(ref, to, small_sem.at[n])
            for n, (ref, to) in enumerate(zip((row_ref, col_ref, basis_ref), small_held, strict=True))
        ]
        order = edges + tuple(i for i in range(lat_dev) if i not in edges)
        for copy in [*small_copies, table_copy, *(copies[i] for i in order)]:
            copy.start()
        for copy in small_copies:
            copy.wait()
        rows_held, cols_held, basis_held = small_held
        sent = []
        for n, edge in enumerate(edges):
            wide[...] = jnp.zeros_like(wide)
            own = rows_held[edge : edge + 1, :] - (p_ref[0] * lat_dev + edge)
            wide[0:1, 0:taps] = own.astype(F32)
            wide[1:2, 0:taps] = cols_held[edge : edge + 1, :].astype(F32)
            for k in range(kernels):
                wide[2 + k : 3 + k, 0:taps] = basis_held[k, edge : edge + 1, :].astype(F32)
            meta[n] = wide[...].astype(BF16)
        far = lax.rem(p_ref[0], 2)
        near = 1 - far
        for e, away in enumerate((near, far)):
            sent.append(
                pltpu.make_async_copy(
                    meta.at[away], edge_refs[e].at[pl.ds(lon, META)], edge_sem.at[e, 1]
                )
            )
            sent[-1].start()
        table_copy.wait()
        for n, i in enumerate(order):
            copies[i].wait()
            if n == 1:
                for e, away in enumerate((near, far)):
                    sent.append(
                        pltpu.make_async_copy(
                            held.at[away * (lat_dev - 1)],
                            edge_refs[e].at[pl.ds(0, lon)],
                            edge_sem.at[e, 0],
                        )
                    )
                    sent[-1].start()
            o_ref[:, i * channels : (i + 1) * channels] = dot(table_held[...], held[i]).astype(BF16)
        for copy in sent:
            copy.wait()

    return pl.pallas_call(
        body,
        in_specs=[SMEM] + [ANYWHERE] * 5,
        out_specs=[VMEM, ANYWHERE, ANYWHERE],
        out_shape=[
            pltpu.HBM((depth, lat_dev * channels), BF16),
            pltpu.HBM((lon + META, channels), BF16),
            pltpu.HBM((lon + META, channels), BF16),
        ],
        scratch_shapes=[
            pltpu.VMEM((lat_dev, lon, channels), BF16),
            pltpu.VMEM(table.shape, BF16),
            pltpu.VMEM((META, channels), F32),
            pltpu.VMEM((2, META, channels), BF16),
            pltpu.SemaphoreType.DMA((lat_dev,)),
            pltpu.SemaphoreType.DMA((2, 2)),
            pltpu.SemaphoreType.DMA((4,)),
            pltpu.VMEM(rows.shape, rows.dtype),
            pltpu.VMEM(cols.shape, cols.dtype),
            pltpu.VMEM(basis.shape, basis.dtype),
        ],
        compiler_params=params(16),
        cost_estimate=cost(2 * depth * lon * channels * lat_dev, features.size * 2),
        name="transform",
    )(
        position,
        in_hbm(features),
        in_hbm(table),
        in_hbm(rows),
        in_hbm(cols),
        in_hbm(basis),
    )


def filtered(order, middle, near, far, shifts, taps, weights, before=None):
    total = order.shape[0] - 1
    lat_dev = shifts.shape[0]
    lon, channels = middle[0].shape[-2:]
    kernels = taps.shape[0]
    count = taps.shape[2]
    wide = kernels * channels
    per = PER
    chunk = per * STEP
    keep = weights is None
    beyond = [array for array in (near, far) if array is not None]

    def body(order_ref, shift_ref, tap_ref, *rest):
        rest = list(rest)
        mid_refs = [rest.pop(0) for _ in middle]
        beyond_refs = [rest.pop(0) for _ in beyond]
        w_ref = None if keep else rest.pop(0)
        if before is not None:
            rest.pop(0)
        out_ref, ext, sem, held, out_sem = rest[:5]
        mixed_ref = None if keep else rest[5]
        step_id = pl.program_id(0)
        odd = order_ref[0]
        row = order_ref[1 + step_id]

        sources = []
        if len(middle) == 1:
            sources += [(mid_refs[0].at[i], i + 1) for i in range(1, lat_dev - 1)]
            if far is None:
                i = (1 - odd) * (lat_dev - 1)
                sources.append((mid_refs[0].at[i], i + 1))
            if near is None:
                i = odd * (lat_dev - 1)
                sources.append((mid_refs[0].at[i], i + 1))
        else:
            sources += [(mid_refs[i], i + 1) for i in range(1, lat_dev - 1)]
            sources.append((mid_refs[0], 1 + (1 - odd) * (lat_dev - 1)))
            sources.append((mid_refs[-1], 1 + odd * (lat_dev - 1)))
        if near is not None:
            sources.append((beyond_refs[0], (1 - odd) * (lat_dev + 1)))
        if far is not None:
            sources.append((beyond_refs[-1], odd * (lat_dev + 1)))

        cut = lon // chunk // 2 * chunk + 2 * SPAN + STEP // 3
        pieces = (
            ((lon - SPAN, 0, SPAN), (0, SPAN, cut)),
            ((cut, SPAN + cut, lon - cut), (0, lon + SPAN, SPAN)),
        )

        def copies(which, half):
            return [
                pltpu.make_async_copy(
                    src.at[pl.ds(a, size)], ext.at[to, pl.ds(b, size)], sem.at[s, 2 * half + n]
                )
                for s, (src, to) in list(enumerate(sources))[which]
                for n, (a, b, size) in enumerate(pieces[half])
            ]

        late = -1 if far is not None and total > 1 else len(sources)

        def outgoing(g, place):
            size = lon // 2
            return pltpu.make_async_copy(
                held.at[g, pl.ds(place * size, size)],
                out_ref.at[order_ref[1 + g], pl.ds(place * size, size)],
                out_sem.at[g, place],
            )

        @pl.when(step_id == 0)
        def _():
            for half in range(2):
                for copy in copies(slice(None), half):
                    copy.start()

        across = lax.broadcasted_iota(jnp.int32, (STEP, 3 * WIN), 1)
        down = lax.broadcasted_iota(jnp.int32, (STEP, 3 * WIN), 0)
        delta = across - down
        band = [jnp.zeros((STEP, 3 * WIN), F32) for _ in range(kernels)]
        for t in range(count):
            hit = delta == shift_ref[row, t]
            for k in range(kernels):
                band[k] = band[k] + jnp.where(hit, tap_ref[k, row, t], 0.0)
        band = jnp.concatenate(band, axis=0).astype(BF16)

        @pl.when(step_id == 0)
        def _():
            for half in range(1 if keep else 2):
                for copy in copies(slice(None, late), half):
                    copy.wait()

        if late == -1:

            @pl.when(step_id == total - 1)
            def _():
                for half in range(2):
                    for copy in copies(slice(late, None), half):
                        copy.wait()

        for c in range(lon // chunk):
            if keep and c == lon // chunk // 2:

                @pl.when(step_id == 0)
                def _():
                    for copy in copies(slice(None, late), 1):
                        copy.wait()

            for b in range(per):
                start = c * chunk + b * STEP
                window = jnp.concatenate(
                    [ext[row + e, start : start + WIN, :] for e in range(3)], axis=0
                )
                sums = dot(band, window).astype(BF16)
                for k in range(kernels):
                    part = sums[k * STEP : (k + 1) * STEP]
                    lanes = slice(k * channels, (k + 1) * channels)
                    if keep:
                        held[step_id, start : start + STEP, lanes] = part
                    else:
                        mixed_ref[c % 2, b * STEP : (b + 1) * STEP, lanes] = part
            if not keep:
                held[step_id, c * chunk : (c + 1) * chunk, :] = sum(
                    lax.dot_general(
                        mixed_ref[c % 2, :, k * channels : (k + 1) * channels],
                        w_ref[k * channels : (k + 1) * channels, :],
                        (((1,), (1,)), ((), ())),
                        preferred_element_type=F32,
                    )
                    for k in range(kernels)
                ).astype(BF16)
            if (c + 1) * chunk * 2 % lon == 0:
                outgoing(step_id, (c + 1) * chunk * 2 // lon - 1).start()

        @pl.when(step_id == total - 1)
        def _():
            for g in range(total):
                for place in range(2):
                    outgoing(g, place).wait()

    depth = wide if keep else channels
    operands = [order, shifts, taps, *(in_hbm(array) for array in middle), *beyond]
    in_specs = [SMEM, SMEM] + [ANYWHERE] * (len(middle) + len(beyond))
    scratch = [
        pltpu.VMEM((lat_dev + 2, lon + 2 * SPAN, channels), BF16),
        pltpu.SemaphoreType.DMA((lat_dev + 2, 4)),
        pltpu.VMEM((total, lon, depth), BF16),
        pltpu.SemaphoreType.DMA((total, 2)),
    ]
    if not keep:
        operands.append(in_hbm(weights))
        in_specs.append(every(wide, channels))
        scratch.append(pltpu.VMEM((2, chunk, wide), BF16))
    aliases = {}
    if before is not None:
        aliases[len(operands)] = 0
        operands.append(before)
        in_specs.append(ANYWHERE)
    return pl.pallas_call(
        body,
        grid=(total,),
        in_specs=[SMEM] + in_specs,
        out_specs=ANYWHERE,
        scratch_shapes=scratch,
        out_shape=pltpu.HBM((lat_dev, lon, depth), BF16),
        input_output_aliases=aliases,
        compiler_params=params(24),
        cost_estimate=cost(
            2 * total * lon * channels * (wide * (0 if keep else 1) + 3 * WIN * kernels),
            total * lon * channels * 8,
        ),
        name="filtered" if keep else "filtered_back",
    )(*operands)


def blocks_of(ref, start, rows, lanes):
    block = ref[:, start : start + rows, lanes].astype(F32)
    return block.reshape(block.shape[0] * rows, block.shape[2]).astype(BF16)


def spectral_forward(position, owned, table_in, table_out, gain):
    group_rows, width = owned.shape
    _, rows, depth = table_in.shape
    degrees, channels = gain.shape
    lat_dev = width // channels

    def body(p_ref, x_ref, a_ref, b_ref, g_ref, analysed_ref, o_ref):
        analysed = jnp.zeros((rows, channels), F32)
        for i in range(lat_dev):
            analysed = analysed + dot(
                a_ref[0, :, i * group_rows : (i + 1) * group_rows],
                x_ref[:, i * channels : (i + 1) * channels],
            )
        analysed_ref[...] = analysed
        gain_rows = jnp.concatenate([g_ref[...]] * (rows // degrees), axis=0)
        scaled = (analysed * gain_rows).astype(BF16)
        for i in range(lat_dev):
            o_ref[:, i * channels : (i + 1) * channels] = dot_t(
                b_ref[0, :, i * group_rows : (i + 1) * group_rows], scaled
            ).astype(BF16)

    table_spec = pl.BlockSpec((1, rows, depth), lambda g, p: (p[0], 0, 0))
    return pl.pallas_call(
        body,
        grid_spec=pltpu.PrefetchScalarGridSpec(
            num_scalar_prefetch=1,
            grid=(1,),
            in_specs=[
                pl.BlockSpec((group_rows, width), lambda g, p: (0, 0)),
                table_spec,
                table_spec,
                pl.BlockSpec((degrees, channels), lambda g, p: (0, 0)),
            ],
            out_specs=[
                pl.BlockSpec((rows, channels), lambda g, p: (0, 0)),
                pl.BlockSpec((group_rows, width), lambda g, p: (0, 0)),
            ],
        ),
        out_shape=[
            pltpu.HBM((rows, channels), F32),
            pltpu.HBM((group_rows, width), BF16),
        ],
        compiler_params=params(16),
        name="spectral_forward",
    )(position, owned, in_hbm(table_in), in_hbm(table_out), in_hbm(gain))


def spectral_adjoint(position, received, table_in, table_out, gain, analysed, terms):
    devices, block_rows, width = received.shape
    group = block_rows - terms
    group_rows = devices * group
    _, rows, depth = table_in.shape
    degrees, channels = gain.shape
    lat_dev = width // channels

    def body(p_ref, x_ref, b_ref, a_ref, g_ref, analysed_ref, gain_ref, o_ref):
        summed = jnp.sum(x_ref[:, 0:terms, :].astype(F32), axis=0).astype(BF16)
        for d in range(devices):
            o_ref[d, 0:terms, :] = summed
        scaled = jnp.zeros((rows, channels), F32)
        for i in range(lat_dev):
            scaled = scaled + dot(
                b_ref[0, :, i * group_rows : (i + 1) * group_rows],
                blocks_of(x_ref, terms, group, slice(i * channels, (i + 1) * channels)),
            )
        products = analysed_ref[...] * scaled
        total = jnp.zeros((degrees, channels), F32)
        for s in range(rows // degrees):
            total = total + products[s * degrees : (s + 1) * degrees]
        gain_ref[...] = total
        gain_rows = jnp.concatenate([g_ref[...]] * (rows // degrees), axis=0)
        grad = (gain_rows * scaled).astype(BF16)
        for i in range(lat_dev):
            part = dot_t(a_ref[0, :, i * group_rows : (i + 1) * group_rows], grad)
            o_ref[:, terms:block_rows, i * channels : (i + 1) * channels] = part.reshape(
                devices, group, channels
            ).astype(BF16)

    table_spec = pl.BlockSpec((1, rows, depth), lambda g, p: (p[0], 0, 0))
    return pl.pallas_call(
        body,
        grid_spec=pltpu.PrefetchScalarGridSpec(
            num_scalar_prefetch=1,
            grid=(1,),
            in_specs=[
                pl.BlockSpec((devices, block_rows, width), lambda g, p: (0, 0, 0)),
                table_spec,
                table_spec,
                pl.BlockSpec((degrees, channels), lambda g, p: (0, 0)),
                pl.BlockSpec((rows, channels), lambda g, p: (0, 0)),
            ],
            out_specs=[
                pl.BlockSpec((degrees, channels), lambda g, p: (0, 0)),
                pl.BlockSpec((devices, block_rows, width), lambda g, p: (0, 0, 0)),
            ],
        ),
        out_shape=[
            jax.ShapeDtypeStruct((degrees, channels), F32),
            pltpu.HBM((devices, block_rows, width), BF16),
        ],
        compiler_params=params(16),
        name="spectral_adjoint",
    )(
        position,
        received,
        in_hbm(table_in),
        in_hbm(table_out),
        in_hbm(gain),
        in_hbm(analysed),
    )


def activation(position, mixed, weights, returned, grad_output, inverse, inverse_t, devices, terms):
    lat_dev, lon, wide = mixed.shape
    channels = grad_output.shape[2]
    group_rows = returned.shape[0]
    group = group_rows // devices
    chunk = CHUNK
    piece = wide // devices // lat_dev

    def body(p_ref, m_ref, w_ref, y_ref, g_ref, inv_ref, invt_ref, *rest):
        o_ref, row_refs = rest[0], rest[1 : 1 + lat_dev]
        rest = rest[1 + lat_dev :]
        acc, held, sem = rest[-3:]
        row = pl.program_id(0)
        gt_ref = held.at[row]
        for c in range(lon // chunk):
            place = slice(c * chunk, (c + 1) * chunk)
            total = dot(m_ref[0, place, :], w_ref[...]) + dot(inv_ref[place, :], y_ref[...])
            square = total * total
            half = 0.5 + 0.5 * jnp.tanh(total * (ROOT + ROOT * CUBE * square))
            value = total * half
            slope = half + value * (1.0 - half) * (2.0 * ROOT + 6.0 * ROOT * CUBE * square)
            o_ref[0, place, :] = value.astype(BF16)
            gt_ref[place, :] = (g_ref[0, place, :].astype(F32) * slope).astype(BF16)
        odd = lax.rem(p_ref[0], 2)
        for i in range(lat_dev):
            for side in range(2):
                to = i if side == 1 else lat_dev - 1 - i

                @pl.when((row == i) & (odd == side))
                def _(i=i, to=to):
                    pltpu.make_async_copy(held.at[i], row_refs[to], sem.at[i]).start()

        spectrum = dot(invt_ref[...], gt_ref[...])
        part = dot(jnp.transpose(gt_ref[...]), m_ref[0])

        @pl.when(row == lat_dev - 1)
        def _():
            for i in range(lat_dev - 1):
                pltpu.make_async_copy(held.at[i], row_refs[i], sem.at[i]).wait()

        @pl.when(row == 0)
        def _():
            acc[...] = part

        @pl.when(row > 0)
        def _():
            acc[...] += part

        if not terms:
            x_ref, weight_ref = rest[0:2]
            x_ref[...] = spectrum.astype(BF16)

            @pl.when(row == lat_dev - 1)
            def _():
                weight_ref[...] = jnp.transpose(acc[...]).astype(BF16)
                pltpu.make_async_copy(held.at[row], row_refs[-1], sem.at[row]).wait()

            return
        x_ref = rest[0]
        spectrum = spectrum.reshape(devices, group, channels).astype(BF16)
        for i in range(lat_dev):

            @pl.when(row == i)
            def _(i=i):
                x_ref[:, terms : terms + group, i * channels : (i + 1) * channels] = spectrum

        @pl.when(row == lat_dev - 1)
        def _():
            weight = jnp.transpose(acc[...]).astype(BF16)
            for d in range(devices):
                for i in range(lat_dev):
                    at = (d * lat_dev + i) * piece
                    x_ref[d, 0:piece, i * channels : (i + 1) * channels] = weight[at : at + piece]
            pltpu.make_async_copy(held.at[row], row_refs[-1], sem.at[row]).wait()

    row_spec = pl.BlockSpec((1, lon, channels), lambda i: (i, 0, 0))
    column_spec = pl.BlockSpec((group_rows, channels), lambda i: (0, i))
    if terms:
        last_specs = [pl.BlockSpec((devices, terms + group, lat_dev * channels), lambda i: (0, 0, 0))]
        last_shapes = [pltpu.HBM((devices, terms + group, lat_dev * channels), BF16)]
    else:
        last_specs = [column_spec, pl.BlockSpec((wide, channels), lambda i: (0, 0))]
        last_shapes = [
            jax.ShapeDtypeStruct((group_rows, lat_dev * channels), BF16),
            jax.ShapeDtypeStruct((wide, channels), BF16),
        ]
    return pl.pallas_call(
        body,
        grid=(lat_dev,),
        in_specs=[
            SMEM,
            pl.BlockSpec((1, lon, wide), lambda i: (i, 0, 0)),
            every(wide, channels),
            column_spec,
            row_spec,
            every(lon, group_rows),
            every(group_rows, lon),
        ],
        out_specs=[row_spec] + [ANYWHERE] * lat_dev + last_specs,
        out_shape=[
            pltpu.HBM((lat_dev, lon, channels), BF16),
        ]
        + [pltpu.HBM((lon, channels), BF16)] * lat_dev
        + last_shapes,
        scratch_shapes=[
            pltpu.VMEM((channels, wide), F32),
            pltpu.VMEM((lat_dev, lon, channels), BF16),
            pltpu.SemaphoreType.DMA((lat_dev,)),
        ],
        compiler_params=params(40),
        cost_estimate=cost(
            4 * grad_output.size * (group_rows + wide), grad_output.size * 14
        ),
        name="activation",
    )(
        position,
        in_hbm(mixed),
        in_hbm(weights),
        returned,
        in_hbm(grad_output),
        in_hbm(inverse),
        in_hbm(inverse_t),
    )


def final(received, forward, grad_disco, terms):
    lat_dev, lon, channels = grad_disco.shape
    depth = forward.shape[1]

    def body(y_ref, f_ref, d_ref, o_ref, *rest):
        w_ref = rest[0] if terms else None
        f_held, d_held, o_held, f_sem, d_sem, o_sem = rest[-7:-1]
        w_held = rest[-1]
        table = pltpu.make_async_copy(f_ref, f_held, f_sem)
        incoming = [
            pltpu.make_async_copy(d_ref.at[i], d_held.at[i], d_sem.at[i]) for i in range(lat_dev)
        ]
        outgoing = [
            pltpu.make_async_copy(o_held.at[i], o_ref.at[i], o_sem.at[i]) for i in range(lat_dev)
        ]
        table.start()
        for copy in incoming:
            copy.start()
        if terms:
            for i in range(lat_dev):
                w_held[:, i] = y_ref[:, 0:terms, i * channels : (i + 1) * channels].astype(F32)
            outgoing.append(pltpu.make_async_copy(w_held, w_ref, o_sem.at[lat_dev]))
            outgoing[-1].start()
        table.wait()
        for i in range(lat_dev):
            lanes = slice(i * channels, (i + 1) * channels)
            if terms:
                bands = blocks_of(y_ref, terms, y_ref.shape[1] - terms, lanes)
            else:
                bands = y_ref[:, lanes]
            incoming[i].wait()
            for c in range(lon // CHUNK):
                place = slice(c * CHUNK, (c + 1) * CHUNK)
                o_held[i, place, :] = (
                    d_held[i, place, :].astype(F32) + dot(f_held[place, :], bands)
                ).astype(BF16)
            outgoing[i].start()
        for copy in outgoing:
            copy.wait()

    out_shape = [pltpu.HBM((lat_dev, lon, channels), BF16)]
    gathered = (16, 128)
    if terms:
        gathered = (received.shape[0], lat_dev, terms, channels)
        out_shape.append(pltpu.HBM(gathered, F32))
    return pl.pallas_call(
        body,
        in_specs=[VMEM, ANYWHERE, ANYWHERE],
        out_specs=[ANYWHERE] * len(out_shape),
        out_shape=out_shape,
        scratch_shapes=[
            pltpu.VMEM((lon, depth), BF16),
            pltpu.VMEM((lat_dev, lon, channels), BF16),
            pltpu.VMEM((lat_dev, lon, channels), BF16),
            pltpu.SemaphoreType.DMA,
            pltpu.SemaphoreType.DMA((lat_dev,)),
            pltpu.SemaphoreType.DMA((lat_dev + 1,)),
            pltpu.VMEM(gathered, F32),
        ],
        compiler_params=params(24),
        cost_estimate=cost(2 * grad_disco.size * depth, grad_disco.size * 6),
        name="final",
    )(received, in_hbm(forward), in_hbm(grad_disco))


def stages(count):
    found = []
    stride = 1
    while stride < count:
        factor = 4 if (count // stride) % 4 == 0 else 2
        found.append((stride, factor))
        stride *= factor
    return found


def partner(array, count, stride, by):
    return lax.ppermute(array, "lat", [(i, i ^ (by * stride)) for i in range(count)])


def sum_scatter_gather(array):
    count = lax.axis_size("lat")
    position = lax.axis_index("lat")
    plan = stages(count)
    for stride, factor in plan:
        digit = (position // stride) % factor
        pieces = array.reshape(factor, array.shape[0] // factor, array.shape[1])
        total = lax.dynamic_index_in_dim(pieces, digit, 0, False).astype(F32)
        for by in range(1, factor):
            piece = lax.dynamic_index_in_dim(pieces, digit ^ by, 0, False)
            total = total + partner(piece, count, stride, by).astype(F32)
        array = total.astype(BF16)
    for stride, factor in reversed(plan):
        digit = (position // stride) % factor
        whole = jnp.zeros((factor,) + array.shape, BF16)
        for by in range(factor):
            part = partner(array, count, stride, by) if by else array
            whole = lax.dynamic_update_index_in_dim(whole, part, digit ^ by, 0)
        array = whole.reshape(-1, array.shape[1])
    return array


def sum_everywhere(array, between, then):
    count = lax.axis_size("lat")
    plan = stages(count)
    for n, (stride, factor) in enumerate(plan):
        last = n == len(plan) - 1
        if last:
            array, between = lax.optimization_barrier((array, between))
        sent = lax.optimization_barrier(array.astype(BF16))
        parts = [sent] + [partner(sent, count, stride, by) for by in range(1, factor)]
        if last:
            parts, result = lax.optimization_barrier((parts, then(between)))
        parts = [part.astype(F32) for part in parts]
        while len(parts) > 1:
            parts = [parts[k] + parts[k + 1] for k in range(0, len(parts), 2)]
        array = parts[0]
    return (array, result)


def paired(near_row, far_row):
    count = lax.axis_size("lat")
    near = lax.ppermute(near_row, "lat", [(i, i ^ 1) for i in range(count)])
    across = [(i, i + 1) for i in range(1, count - 1, 2)]
    far = lax.ppermute(far_row, "lat", across + [(b, a) for a, b in across])
    return (near, far)


def exchange(blocks):
    return lax.all_to_all(blocks, "lat", split_axis=0, concat_axis=0, tiled=True)


def exchange_rows(array):
    count = lax.axis_size("lat")
    rows, width = array.shape
    return exchange(array.reshape(count, rows // count, width)).reshape(rows, width)


def local(features, disco_rows, disco_cols, disco_basis, disco_weight, spectral_gain, grad_output):
    lat_dev, lon, channels = features.shape
    devices = lax.axis_size("lat")
    position = lax.axis_index("lat")
    degrees = spectral_gain.shape[0]
    lat_count = lat_dev * devices
    order_count = lat_count
    owned_orders = order_count // devices
    kernels, _, taps = disco_basis.shape
    wide = kernels * channels
    forward, inverse = fourier_tables(lon, order_count, devices)
    group = forward.shape[1] // devices
    forward_t = jnp.asarray(np.ascontiguousarray(forward.T))
    inverse_t = jnp.asarray(np.ascontiguousarray(inverse.T))
    forward = jnp.asarray(forward)
    inverse = jnp.asarray(inverse)
    place = position.astype(jnp.int32).reshape(1)
    piece = wide // devices // lat_dev
    small = (
        order_count * owned_orders * 2 * degrees * lat_dev * devices * group <= TABLE_CAP * 4
        and piece * devices * lat_dev == wide
        and piece % 16 == 0
    )
    terms = piece if small else 0
    inner = tuple(range(1, lat_dev - 1))

    coefficients, near_row, far_row = transform(
        place, features, forward_t, disco_rows, disco_cols, disco_basis
    )
    near, far = paired(near_row, far_row)
    owned = exchange_rows(coefficients)

    band_rows = position * lat_dev + jnp.arange(lat_dev, dtype=jnp.int32)[:, None]
    basis = disco_basis.astype(F32)
    offsets = disco_rows - band_rows
    shifts = (offsets + 1) * WIN + SPAN + disco_cols
    weight_rows = disco_weight.reshape(wide, channels)
    odd = position % 2
    near_id = (1 - odd) * (lat_dev - 1)
    far_id = odd * (lat_dev - 1)

    def order_of(*rows):
        return jnp.stack([odd, *rows]).astype(jnp.int32)

    mixed = filtered(order_of(*inner), [features], None, None, shifts, basis, None)
    owned, mixed = lax.optimization_barrier((owned, mixed))
    mixed = filtered(order_of(near_id), [features], near, None, shifts, basis, None, mixed)
    mixed = filtered(order_of(far_id), [features], None, far, shifts, basis, None, mixed)

    packed = jnp.concatenate(
        [
            offsets.astype(F32)[:, None, :],
            disco_cols.astype(F32)[:, None, :],
            jnp.transpose(basis, (1, 0, 2)),
        ],
        axis=1,
    )
    near_taps = near[None, lon : lon + 2 + kernels, :taps].astype(F32)
    far_taps = far[None, lon : lon + 2 + kernels, :taps].astype(F32)
    packed_all = jnp.concatenate(
        [jnp.where(odd == 1, near_taps, far_taps), packed, jnp.where(odd == 1, far_taps, near_taps)],
        axis=0,
    )
    back_shifts = []
    back_taps = []
    for e in range(3):
        aimed = packed_all[e : e + lat_dev, 0] == 1.0 - e
        columns = packed_all[e : e + lat_dev, 1].astype(jnp.int32)
        back_shifts.append(jnp.where(aimed, e * WIN + SPAN - columns, NONE))
        back_taps.append(jnp.transpose(packed_all[e : e + lat_dev, 2:], (1, 0, 2)))
    back_shifts = jnp.concatenate(back_shifts, axis=1)
    back_taps = jnp.concatenate(back_taps, axis=2)

    if small:
        plain, weighted = legendre_table(order_count, degrees, lat_count)
        plain = jnp.asarray(spectral_table(plain, devices, lat_dev, group))
        weighted = jnp.asarray(spectral_table(weighted, devices, lat_dev, group))
        analysed, synthesized = spectral_forward(place, owned, weighted, plain, spectral_gain)
    else:
        _, gauss_weights = gauss_grid(lat_count)
        orders = position * owned_orders + jnp.arange(owned_orders, dtype=jnp.int32)
        legendre = legendre_block(orders, order_count, degrees, lat_count)
        plain = legendre.astype(BF16).reshape(owned_orders, degrees, devices, lat_dev)
        weighted = (legendre * jnp.asarray(gauss_weights, F32)[None, None, :]).astype(BF16)
        weighted = weighted.reshape(owned_orders, degrees, devices, lat_dev)

        def opened(array):
            array = array.reshape(devices, group, lat_dev, channels)[:, : 2 * owned_orders]
            return array.reshape(devices, owned_orders, 2, lat_dev, channels)

        def closed(array):
            array = array.reshape(devices, 2 * owned_orders, lat_dev * channels)
            array = jnp.pad(array, ((0, 0), (0, group - 2 * owned_orders), (0, 0)))
            return array.reshape(devices * group, lat_dev * channels).astype(BF16)

        analysed = jnp.einsum(
            "rlsi,srpic->rplc", weighted, opened(owned), preferred_element_type=F32
        )
        scaled = (analysed * spectral_gain).astype(BF16)
        synthesized = closed(
            jnp.einsum("rlsi,rplc->srpic", plain, scaled, preferred_element_type=F32)
        )

    returned = exchange_rows(synthesized)
    output, *blocks = activation(
        place, mixed, weight_rows, returned, grad_output, inverse, inverse_t, devices, terms
    )
    grad_rows, blocks = blocks[:lat_dev], blocks[lat_dev:]
    grad_near, grad_far = paired(grad_rows[0], grad_rows[-1])
    part = filtered(
        order_of(*inner), grad_rows, None, None, back_shifts, back_taps, weight_rows
    )
    if small:
        grad_owned, part = lax.optimization_barrier((exchange(blocks[0]), part))
        gain_part, grad_blocks = spectral_adjoint(
            place, grad_owned, plain, weighted, spectral_gain, analysed, terms
        )
        grad_bands = exchange(grad_blocks)
    else:
        grad_owned = exchange_rows(blocks[0])
        grad_scaled = jnp.einsum(
            "rlsi,srpic->rplc", plain, opened(grad_owned), preferred_element_type=F32
        )
        gain_part = jnp.sum(analysed * grad_scaled, axis=(0, 1))
        grad_analysed = (grad_scaled * spectral_gain).astype(BF16)
        grad_coeff = closed(
            jnp.einsum("rlsi,rplc->srpic", weighted, grad_analysed, preferred_element_type=F32)
        )
        grad_bands = exchange_rows(grad_coeff)

    grad_disco = filtered(
        order_of(near_id, far_id),
        grad_rows,
        grad_near,
        grad_far,
        back_shifts,
        back_taps,
        weight_rows,
        part,
    )
    grad_gain, (grad_features, *grad_weight) = sum_everywhere(
        gain_part, grad_disco, lambda held: final(grad_bands, forward, held, terms)
    )
    if not small:
        grad_weight = [sum_scatter_gather(blocks[1]).astype(F32)]
    return (
        output,
        grad_features,
        grad_weight[0].reshape(kernels, channels, channels),
        grad_gain,
    )


def solution(mesh):
    return jax.shard_map(
        local,
        mesh=mesh,
        in_specs=(
            P(("group", "lat"), None, None),
            P("lat", None),
            P("lat", None),
            P(None, "lat", None),
            P(),
            P(),
            P(("group", "lat"), None, None),
        ),
        out_specs=(
            P(("group", "lat"), None, None),
            P(("group", "lat"), None, None),
            P("group", None, None),
            P("group", None),
        ),
        check_vma=False,
    )
```
